32 devices in a mesh: section: 4 (over x, core), dp: 8 (over z, y).
Axes of the slice: x: 2, y: 2, z: 4, core: 2. Of those that a mesh axis runs over, the one named last changes fastest.
Arguments:
- section_input: bfloat16 [3, 16, 6656], P(None, 'dp'), may hold values from -6 to 6
- out_cotangent: bfloat16 [3, 16, 6656], P(None, 'dp'), may hold values from -18 to 18
- up_weight: bfloat16 [4, 6656, 8960], P('section', None, 'dp'), may hold values from -6 to 6
- down_weight: bfloat16 [4, 6656, 8960], P('section', None, 'dp'), may hold values from -6 to 6
- norm_gain: float32 [4, 6656], P('section'), may hold values from 0.25 to 1.75
Outputs:
- grad_up: float32 [4, 6656, 8960], P('section', None, 'dp')
- grad_down: float32 [4, 6656, 8960], P('section', None, 'dp')
- grad_gain: float32 [4, 6656], P('section')
The draws below stay inside these ranges and needn't reach their ends.
All inputs are finite; a program needn't handle non-finite values.
Results may differ from the reference program's by a relative error of at most 0.03.
Values may be sent and summed in bfloat16 or wider, within the bound.
No kernel may reach another device: no remote copies, remote signals or barrier semaphores. Data moves between devices by JAX's collectives and lax.ppermute only.
A program may use at most 384 MiB of HBM per device.

```python
import math
import jax
import jax.numpy as jnp
from jax import lax

D = 6656
HIDDEN_SIZE = 8960
MICRO = 3
SECTIONS = 4
TOKENS = 16
N_SECTION = 4
N_DP = 8


def shard_levels(key, dims, cuts, smallest, top_value):
    def one(axis_at, shards_of):
        heights = jax.random.uniform(jax.random.fold_in(jax.random.fold_in(key, 6), axis_at), (shards_of,), jnp.float32, smallest / len(cuts), top_value / len(cuts))
        return jnp.repeat(jnp.exp(heights), dims[axis_at] // shards_of).reshape((-1,) + (1,) * (len(dims) - axis_at - 1))

    level = one(*cuts[0])
    for cut in cuts[1:]:
        level = level * one(*cut)
    return level


def scatter_about(rng, dims, scale, most, shards=(), dtype=jnp.bfloat16):
    result = scale * jax.random.normal(rng, dims, jnp.float32)
    if shards:
        result = result * shard_levels(rng, dims, shards, -0.22, 0.18)
    return jnp.clip(result, -most, most).astype(dtype)


def setup_inputs(seed: int = 0) -> dict:
    key_list = jax.random.split(jax.random.key(seed), 6)
    section_input = scatter_about(key_list[0], (MICRO, TOKENS, D), 1.0, 6.0, ((1, 8),))
    out_cotangent = scatter_about(key_list[1], (MICRO, TOKENS, D), 3.0, 18.0, ((1, 8),))
    up_weight = scatter_about(key_list[2], (SECTIONS, D, HIDDEN_SIZE), 1.0, 6.0, ((0, 4), (2, 8)))
    down_weight = scatter_about(key_list[3], (SECTIONS, D, HIDDEN_SIZE), 1.0, 6.0, ((0, 4), (2, 8)))
    norm_gain = jnp.clip(1.0 + 0.15 * jax.random.normal(key_list[4], (SECTIONS, D), jnp.float32), 0.25, 1.75)
    return {"section_input": section_input, "out_cotangent": out_cotangent, "up_weight": up_weight, "down_weight": down_weight, "norm_gain": norm_gain}


EPSILON = 1e-05
GELU_SCALE = 0.7978845608028654
GELU_CUBIC = 0.044715

def gelu_value(preact):
    inner = GELU_SCALE * (preact + GELU_CUBIC * preact * preact * preact)
    return 0.5 * preact * (1.0 + jnp.tanh(inner))

def gelu_slope(preact):
    inner = GELU_SCALE * (preact + GELU_CUBIC * preact * preact * preact)
    tangent = jnp.tanh(inner)
    return 0.5 * (1.0 + tangent) + 0.5 * preact * (1.0 - tangent * tangent) * GELU_SCALE * (1.0 + 3.0 * GELU_CUBIC * preact * preact)

def normalize(tok_rows):
    values = tok_rows.astype(jnp.float32)
    norm_scale = lax.rsqrt(lax.optimization_barrier(jnp.mean(values * values, axis=-1, keepdims=True)) + EPSILON)
    return (values, norm_scale, values * norm_scale)

def block_sum(left, right, factor):
    left_blocks = left.reshape(left.shape[0], N_DP, HIDDEN_SIZE // N_DP).astype(jnp.float32)
    right_blocks = right.reshape(right.shape[0], N_DP, HIDDEN_SIZE // N_DP).astype(jnp.float32)
    partial_value = jnp.einsum('tnh,dnh->ntd', left_blocks, right_blocks) * factor
    rounded = lax.optimization_barrier(partial_value.astype(jnp.bfloat16))
    return lax.optimization_barrier(jnp.sum(rounded.astype(jnp.float32), axis=0))

def reference(section_input, out_cotangent, up_weight, down_weight, norm_gain):
    inv_width = 1.0 / math.sqrt(D)
    inv_hidden = 1.0 / math.sqrt(HIDDEN_SIZE)
    grads_up = [jnp.zeros((D, HIDDEN_SIZE), jnp.float32) for section_idx in range(N_SECTION)]
    grads_down = [jnp.zeros((D, HIDDEN_SIZE), jnp.float32) for section_idx in range(N_SECTION)]
    grads_gain = [jnp.zeros((D,), jnp.float32) for section_idx in range(N_SECTION)]
    for batch_idx in range(MICRO):
        tok_rows = section_input[batch_idx]
        saved = []
        for section_idx in range(N_SECTION):
            values, norm_scale, normed = normalize(tok_rows)
            scaled = (normed * norm_gain[section_idx]).astype(jnp.bfloat16)
            preact = jnp.dot(scaled, up_weight[section_idx], preferred_element_type=jnp.float32) * inv_width
            hidden = gelu_value(preact).astype(jnp.bfloat16)
            branch = block_sum(hidden, down_weight[section_idx], inv_hidden)
            saved.append((tok_rows, scaled, preact, hidden))
            tok_rows = (values + branch).astype(jnp.bfloat16)
        grad_rows = out_cotangent[batch_idx]
        for section_idx in reversed(range(N_SECTION)):
            block_in, scaled, preact, hidden = saved[section_idx]
            values, norm_scale, normed = normalize(block_in)
            hidden_grad = jnp.dot(grad_rows, down_weight[section_idx], preferred_element_type=jnp.float32) * inv_hidden
            preact_grad = (hidden_grad * gelu_slope(preact)).astype(jnp.bfloat16)
            scaled_grad = block_sum(preact_grad, up_weight[section_idx], inv_width)
            normed_grad = scaled_grad * norm_gain[section_idx]
            input_grad = grad_rows.astype(jnp.float32) + norm_scale * (normed_grad - normed * lax.optimization_barrier(jnp.mean(normed_grad * normed, axis=-1, keepdims=True)))
            grads_down[section_idx] = grads_down[section_idx] + jnp.dot(grad_rows.T, hidden, preferred_element_type=jnp.float32) * inv_hidden
            grads_up[section_idx] = grads_up[section_idx] + jnp.dot(scaled.T, preact_grad, preferred_element_type=jnp.float32) * inv_width
            grads_gain[section_idx] = grads_gain[section_idx] + lax.optimization_barrier(jnp.sum(scaled_grad * normed, axis=0))
            grad_rows = input_grad.astype(jnp.bfloat16)
    return (jnp.stack(grads_up), jnp.stack(grads_down), jnp.stack(grads_gain))
```

```python
import math

import jax
import jax.numpy as jnp
from jax import lax
from jax.sharding import PartitionSpec as P

D = 6656
HIDDEN_SIZE = 8960


EPSILON = 1e-05
GELU_SCALE = 0.7978845608028654
GELU_CUBIC = 0.044715

AXES = ("section", "dp")


def gelu_value(preact):
    inner = GELU_SCALE * (preact + GELU_CUBIC * preact * preact * preact)
    return 0.5 * preact * (1.0 + jnp.tanh(inner))


def gelu_slope(preact):
    inner = GELU_SCALE * (preact + GELU_CUBIC * preact * preact * preact)
    tangent = jnp.tanh(inner)
    return 0.5 * (1.0 + tangent) + 0.5 * preact * (1.0 - tangent * tangent) * GELU_SCALE * (
        1.0 + 3.0 * GELU_CUBIC * preact * preact
    )


def normalize(tok_rows):
    values = tok_rows.astype(jnp.float32)
    norm_scale = lax.rsqrt(jnp.mean(values * values, axis=-1, keepdims=True) + EPSILON)
    return (values, norm_scale, values * norm_scale)


def outer_rows(left, right):
    return lax.dot_general(
        left, right, (((0,), (0,)), ((), ())), preferred_element_type=jnp.float32
    )


def across_hidden(left, right):
    return lax.dot_general(
        left, right, (((1,), (1,)), ((), ())), preferred_element_type=jnp.float32
    )


def send(value, source, target, step):
    count = lax.axis_size("dp")
    if source == target and step % count == 0:
        return value
    return lax.ppermute(
        value,
        AXES,
        [(source * count + r, target * count + (r + step) % count) for r in range(count)],
    )


def spread(chunk, source, target):
    return jnp.concatenate(
        [send(chunk, source, target, k) for k in range(lax.axis_size("dp"))], axis=0
    )


def collect(parts, section):
    count = lax.axis_size("dp")
    pieces = parts.reshape(count, -1, parts.shape[-1])
    total = pieces[0].astype(jnp.float32)
    for k in range(1, count):
        total = total + send(pieces[k], section, section, -k).astype(jnp.float32)
    return total


def collect_all(parts):
    count = lax.axis_size("dp")
    pieces = parts.reshape(count, -1, parts.shape[-1])
    backward = jnp.concatenate([pieces[:1], pieces[:0:-1]], axis=0)
    doubled = jnp.concatenate([backward, backward], axis=0)
    offset = (count - lax.axis_index("dp")) % count
    placed = lax.dynamic_slice_in_dim(doubled, offset, count, 0)
    arrived = lax.all_to_all(placed, "dp", 0, 0, tiled=True)
    return jnp.sum(arrived.astype(jnp.float32), axis=0)


def sum_over_dp(value):
    count = lax.axis_size("dp")
    if count & (count - 1):
        return lax.psum(value, "dp")
    width = 1
    while width < count:
        value = value + lax.ppermute(value, "dp", [(r, r ^ width) for r in range(count)])
        width *= 2
    return value


def body(section_input, out_cotangent, up_weight, down_weight, norm_gain):
    section_count = lax.axis_size("section")
    section_pos = lax.axis_index("section")
    weight_up = up_weight[0]
    weight_down = down_weight[0]
    gain_row = norm_gain[0]
    model_width = weight_up.shape[0]
    inv_width = 1.0 / math.sqrt(D)
    inv_hidden = 1.0 / math.sqrt(HIDDEN_SIZE)
    first_chunk = section_input.reshape(-1, model_width)
    last_chunk = out_cotangent.reshape(-1, model_width)
    chunk_rows = first_chunk.shape[0]

    def keep(stash, fresh, section):
        return fresh if stash is None else jnp.where(section_pos == section, fresh, stash)

    rows_in = spread(first_chunk, 0, 0)
    grad_rows = spread(last_chunk, section_count - 1, section_count - 1)
    stash_rows = stash_scaled = stash_preact = stash_hidden = None
    for section in range(section_count):
        values, norm_scale, normed = normalize(rows_in)
        scaled = (normed * gain_row).astype(jnp.bfloat16)
        preact = jnp.dot(scaled, weight_up, preferred_element_type=jnp.float32) * inv_width
        hidden = gelu_value(preact).astype(jnp.bfloat16)
        stash_rows = keep(stash_rows, rows_in, section)
        stash_scaled = keep(stash_scaled, scaled, section)
        stash_preact = keep(stash_preact, preact, section)
        stash_hidden = keep(stash_hidden, hidden, section)
        if section < section_count - 1:
            part = (across_hidden(hidden, weight_down) * inv_hidden).astype(jnp.bfloat16)
            result = (values[:chunk_rows] + collect(part, section)).astype(jnp.bfloat16)
            rows_in = spread(result, section, section + 1)
    values, norm_scale, normed = normalize(stash_rows)
    own_scale, own_normed = norm_scale[:chunk_rows], normed[:chunk_rows]
    slope = gelu_slope(stash_preact)
    stash_grad = stash_preact_grad = gain_term = None
    for section in range(section_count - 1, -1, -1):
        hidden_grad = (
            jnp.dot(grad_rows, weight_down, preferred_element_type=jnp.float32) * inv_hidden
        )
        preact_grad = (hidden_grad * slope).astype(jnp.bfloat16)
        part = (across_hidden(preact_grad, weight_up) * inv_width).astype(jnp.bfloat16)
        stash_grad = keep(stash_grad, grad_rows, section)
        stash_preact_grad = keep(stash_preact_grad, preact_grad, section)
        if section > 0:
            scaled_grad = collect_all(part)
            gain_term = keep(gain_term, jnp.sum(scaled_grad * own_normed, axis=0), section)
            normed_grad = scaled_grad * gain_row
            input_grad = grad_rows[:chunk_rows].astype(jnp.float32) + own_scale * (
                normed_grad
                - own_normed * jnp.mean(normed_grad * own_normed, axis=-1, keepdims=True)
            )
            grad_rows = spread(input_grad.astype(jnp.bfloat16), section, section - 1)
        else:
            gain_term = keep(
                gain_term, jnp.sum(part.astype(jnp.float32) * normed, axis=0), section
            )
    grad_gain = sum_over_dp(gain_term)
    grad_down = outer_rows(stash_grad, stash_hidden) * inv_hidden
    grad_up = outer_rows(stash_scaled, stash_preact_grad) * inv_width
    return (grad_up[None], grad_down[None], grad_gain[None])


def solution(mesh):
    placed = (
        P(None, "dp", None),
        P(None, "dp", None),
        P("section", None, "dp"),
        P("section", None, "dp"),
        P("section", None),
    )
    return jax.shard_map(
        body,
        mesh=mesh,
        in_specs=placed,
        out_specs=(P("section", None, "dp"), P("section", None, "dp"), P("section", None)),
        check_vma=False,
    )
```

```python
import functools
import math

import jax
import jax.numpy as jnp
from jax import lax
from jax.experimental import pallas as pl
from jax.experimental.pallas import tpu as pltpu
from jax.sharding import PartitionSpec as P

D = 6656
HIDDEN_SIZE = 8960


EPSILON = 1e-05
GELU_SCALE = 0.7978845608028654
GELU_CUBIC = 0.044715

INV_WIDTH = 1.0 / math.sqrt(D)
INV_HIDDEN = 1.0 / math.sqrt(HIDDEN_SIZE)

AXES = ("section", "dp")
QUARTERS = 4
LANES = 128
BLOCK = 512
VMEM_BYTES = 50 * 1024 * 1024

ANY = pl.BlockSpec(memory_space=pl.ANY)
VMEM = pl.BlockSpec(memory_space=pltpu.VMEM)
SMEM = pl.BlockSpec(memory_space=pltpu.SMEM)


def gelu_value(preact):
    inner = GELU_SCALE * (preact + GELU_CUBIC * preact * preact * preact)
    return 0.5 * preact * (1.0 + jnp.tanh(inner))


def gelu_slope(preact):
    inner = GELU_SCALE * (preact + GELU_CUBIC * preact * preact * preact)
    tangent = jnp.tanh(inner)
    return 0.5 * (1.0 + tangent) + 0.5 * preact * (1.0 - tangent * tangent) * GELU_SCALE * (
        1.0 + 3.0 * GELU_CUBIC * preact * preact
    )


def outer_rows(left, right):
    return lax.dot_general(
        left, right, (((0,), (0,)), ((), ())), preferred_element_type=jnp.float32
    )


def across_hidden(left, right):
    return lax.dot_general(
        left, right, (((1,), (1,)), ((), ())), preferred_element_type=jnp.float32
    )


def block_copies(source, target, sems):
    return [
        pltpu.make_async_copy(
            source.at[pl.ds(i * BLOCK, BLOCK)], target.at[pl.ds(i * BLOCK, BLOCK)], sems.at[i]
        )
        for i in range(source.shape[0] // BLOCK)
    ]


def quarter(place_ref, k, width):
    start = (place_ref[1] ^ k) * width
    return pl.ds(pl.multiple_of(start, LANES), width)


def contract_width(rows_ref, weight_ref, total_ref, copies, then_start):
    for i, copy in enumerate(copies):
        if i < len(then_start):
            then_start[i].start()
        copy.wait()
        part = jnp.dot(
            rows_ref[:, i * BLOCK : (i + 1) * BLOCK],
            weight_ref[i * BLOCK : (i + 1) * BLOCK, :],
            preferred_element_type=jnp.float32,
        )
        total_ref[...] = part if i == 0 else total_ref[...] + part


def forward_kernel(pieces, with_down, with_stash, *refs):
    place_ref, refs = refs[0], refs[1:]
    piece_refs, refs = refs[:pieces], refs[pieces:]
    gain_ref, up_hbm, down_hbm = refs[:3]
    refs = refs[3 + (3 if with_stash else 0) :]
    count = QUARTERS if with_down else 0
    part_refs, refs = refs[:count], refs[count:]
    rows_out, scale_out, preact_out = refs[:3]
    up_ref, down_ref, rows_ref, scaled_ref, scale_ref, preact_ref, part_ref = refs[3:10]
    up_sems, down_sems, out_sems = refs[10:]
    width = rows_ref.shape[1]
    piece_width = width // pieces

    @pl.when(place_ref[0] == 1)
    def _():
        up_copies = block_copies(up_hbm, up_ref, up_sems)
        down_copies = block_copies(down_hbm, down_ref, down_sems) if with_down else []
        for copy in up_copies:
            copy.start()
        squares = 0.0
        for k in range(pieces):
            values = piece_refs[k][...].astype(jnp.float32)
            squares = squares + jnp.sum(values * values, axis=-1, keepdims=True)
        norm_scale = lax.rsqrt(squares * (1.0 / width) + EPSILON)
        scale_ref[...] = jnp.broadcast_to(norm_scale, scale_ref.shape)
        for k in range(pieces):
            columns = quarter(place_ref, k, piece_width) if pieces > 1 else slice(None)
            rows = piece_refs[k][...]
            rows_ref[:, columns] = rows
            normed = rows.astype(jnp.float32) * norm_scale
            scaled_ref[:, columns] = (normed * gain_ref[:, columns]).astype(jnp.bfloat16)
        contract_width(scaled_ref, up_ref, preact_ref, up_copies, down_copies)
        preact = preact_ref[...] * INV_WIDTH
        preact_ref[...] = preact
        stores = [
            pltpu.make_async_copy(source, target, out_sems.at[i])
            for i, (source, target) in enumerate(
                [(rows_ref, rows_out), (scale_ref, scale_out), (preact_ref, preact_out)]
            )
        ]
        for copy in stores:
            copy.start()
        if with_down:
            hidden = gelu_value(preact).astype(jnp.bfloat16)
            for i, copy in enumerate(down_copies):
                copy.wait()
                block = slice(i * BLOCK, (i + 1) * BLOCK)
                part = across_hidden(hidden, down_ref[block, :]) * INV_HIDDEN
                part_ref[:, block] = part.astype(jnp.bfloat16)
            for k in range(QUARTERS):
                part_refs[k][...] = part_ref[:, quarter(place_ref, k, width // QUARTERS)]
        for copy in stores:
            copy.wait()


def backward_kernel(pieces, with_parts, with_stash, *refs):
    place_ref, refs = refs[0], refs[1:]
    piece_refs, refs = refs[:pieces], refs[pieces:]
    rows_ref, scale_ref, preact_ref, up_hbm, down_hbm = refs[:5]
    refs = refs[5 + (3 if with_stash else 0) :]
    count = QUARTERS if with_parts else 0
    part_refs, refs = refs[:count], refs[count:]
    grad_out, preact_grad_out, gain_out = refs[:3]
    up_ref, down_ref, grad_ref, hidden_grad_ref, preact_grad_ref, part_ref, gain_ref = refs[3:10]
    up_sems, down_sems, out_sems = refs[10:]
    width = grad_ref.shape[1]
    piece_width = width // pieces

    @pl.when(place_ref[0] == 1)
    def _():
        up_copies = block_copies(up_hbm, up_ref, up_sems)
        down_copies = block_copies(down_hbm, down_ref, down_sems)
        for copy in down_copies:
            copy.start()
        for k in range(pieces):
            columns = quarter(place_ref, k, piece_width) if pieces > 1 else slice(None)
            grad_ref[:, columns] = piece_refs[k][...]
        contract_width(grad_ref, down_ref, hidden_grad_ref, down_copies, up_copies)
        preact = preact_ref[...]
        hidden_grad = hidden_grad_ref[...] * INV_HIDDEN
        preact_grad = (hidden_grad * gelu_slope(preact)).astype(jnp.bfloat16)
        preact_grad_ref[...] = preact_grad
        norm_scale = scale_ref[:, :1]
        for i, copy in enumerate(up_copies):
            copy.wait()
            block = slice(i * BLOCK, (i + 1) * BLOCK)
            part = across_hidden(preact_grad, up_ref[block, :]) * INV_WIDTH
            normed = rows_ref[:, block].astype(jnp.float32) * norm_scale
            gain_ref[:, block] = jnp.sum(part * normed, axis=0, keepdims=True)
            if with_parts:
                part_ref[:, block] = part.astype(jnp.bfloat16)
        stores = [
            pltpu.make_async_copy(source, target, out_sems.at[i])
            for i, (source, target) in enumerate(
                [
                    (grad_ref, grad_out),
                    (preact_grad_ref, preact_grad_out),
                    (gain_ref, gain_out),
                ]
            )
        ]
        for copy in stores:
            copy.start()
        if with_parts:
            along = jnp.sum(
                preact_grad.astype(jnp.float32) * preact, axis=-1, keepdims=True
            ).astype(jnp.bfloat16)
            quarter_width = width // QUARTERS
            for k in range(QUARTERS):
                part_refs[k][:, :quarter_width] = part_ref[
                    :, quarter(place_ref, k, quarter_width)
                ]
                part_refs[k][:, quarter_width:] = jnp.broadcast_to(along, (along.shape[0], LANES))
        for copy in stores:
            copy.wait()


def call(kernel, inputs, specs, stash, parts, stash_shapes, scratch, passes, shapes):
    rows, width, local = shapes
    aliases = {len(inputs) + i: len(parts) + i for i in range(len(stash))}
    bytes_accessed = passes * width * local * 2
    return pl.pallas_call(
        kernel,
        out_shape=list(parts) + list(stash_shapes),
        in_specs=list(specs) + [ANY] * len(stash),
        out_specs=[VMEM] * len(parts) + [ANY] * len(stash_shapes),
        scratch_shapes=scratch,
        input_output_aliases=aliases,
        cost_estimate=pl.CostEstimate(
            flops=passes * 2 * rows * width * local,
            bytes_accessed=bytes_accessed,
            transcendentals=rows * local,
        ),
        compiler_params=pltpu.CompilerParams(vmem_limit_bytes=VMEM_BYTES),
    )(*inputs, *stash)


def forward_stage(place, pieces, gain, up, down, stash, with_down):
    rows = pieces[0].shape[0]
    width, local = up.shape
    blocks = width // BLOCK
    parts = [jax.ShapeDtypeStruct((rows, width // QUARTERS), jnp.bfloat16)] * QUARTERS
    stash_shapes = [
        jax.ShapeDtypeStruct((rows, width), jnp.bfloat16),
        jax.ShapeDtypeStruct((rows, LANES), jnp.float32),
        jax.ShapeDtypeStruct((rows, local), jnp.float32),
    ]
    scratch = [
        pltpu.VMEM((width, local), jnp.bfloat16),
        pltpu.VMEM((width, local) if with_down else (16, LANES), jnp.bfloat16),
        pltpu.VMEM((rows, width), jnp.bfloat16),
        pltpu.VMEM((rows, width), jnp.bfloat16),
        pltpu.VMEM((rows, LANES), jnp.float32),
        pltpu.VMEM((rows, local), jnp.float32),
        pltpu.VMEM((rows, width), jnp.bfloat16),
        pltpu.SemaphoreType.DMA((blocks,)),
        pltpu.SemaphoreType.DMA((blocks,)),
        pltpu.SemaphoreType.DMA((3,)),
    ]
    result = call(
        functools.partial(forward_kernel, len(pieces), with_down, bool(stash)),
        [place, *pieces, gain, up, down],
        [SMEM] + [VMEM] * len(pieces) + [VMEM, ANY, ANY],
        stash,
        parts if with_down else [],
        stash_shapes,
        scratch,
        2 if with_down else 1,
        (rows, width, local),
    )
    return (result[:-3], result[-3:])


def backward_stage(place, pieces, kept, up, down, stash, with_parts):
    rows = pieces[0].shape[0]
    width, local = up.shape
    blocks = width // BLOCK
    parts = [jax.ShapeDtypeStruct((rows, width // QUARTERS + LANES), jnp.bfloat16)] * QUARTERS
    stash_shapes = [
        jax.ShapeDtypeStruct((rows, width), jnp.bfloat16),
        jax.ShapeDtypeStruct((rows, local), jnp.bfloat16),
        jax.ShapeDtypeStruct((1, width), jnp.float32),
    ]
    scratch = [
        pltpu.VMEM((width, local), jnp.bfloat16),
        pltpu.VMEM((width, local), jnp.bfloat16),
        pltpu.VMEM((rows, width), jnp.bfloat16),
        pltpu.VMEM((rows, local), jnp.float32),
        pltpu.VMEM((rows, local), jnp.bfloat16),
        pltpu.VMEM((rows, width), jnp.bfloat16),
        pltpu.VMEM((1, width), jnp.float32),
        pltpu.SemaphoreType.DMA((blocks,)),
        pltpu.SemaphoreType.DMA((blocks,)),
        pltpu.SemaphoreType.DMA((3,)),
    ]
    result = call(
        functools.partial(backward_kernel, len(pieces), with_parts, bool(stash)),
        [place, *pieces, *kept, up, down],
        [SMEM] + [VMEM] * (len(pieces) + 3) + [ANY, ANY],
        stash,
        parts if with_parts else [],
        stash_shapes,
        scratch,
        2,
        (rows, width, local),
    )
    return (result[:-3], result[-3:])


def within(sections, flip):
    count = lax.axis_size("dp")
    return [(s * count + r, s * count + (r ^ flip)) for s in sections for r in range(count)]


def between(moves, flip):
    count = lax.axis_size("dp")
    return [(s * count + r, t * count + (r ^ flip)) for s, t in moves for r in range(count)]


def sum_quarters(parts, sections):
    inner = lax.axis_size("dp") // QUARTERS
    total = parts[0].astype(jnp.float32)
    arrived = [
        lax.ppermute(parts[k], AXES, within(sections, k * inner)) for k in range(QUARTERS - 1, 0, -1)
    ]
    for value in arrived:
        total = total + value.astype(jnp.float32)
    flip = 1
    while flip < inner:
        rounded = total.astype(jnp.bfloat16)
        other = lax.ppermute(rounded, AXES, within(sections, flip))
        total = rounded.astype(jnp.float32) + other.astype(jnp.float32)
        flip *= 2
    return total


def hand_on(own, moves):
    inner = lax.axis_size("dp") // QUARTERS
    pieces = {
        k: lax.ppermute(own, AXES, between(moves, k * inner)) for k in range(QUARTERS - 1, -1, -1)
    }
    return [pieces[k] for k in range(QUARTERS)]


def gather_rows(chunk, sections):
    count = lax.axis_size("dp")
    position = lax.axis_index("dp")
    held = chunk[None]
    flip = 1
    while flip < count:
        other = lax.ppermute(held, AXES, within(sections, flip))
        low = (position // flip) % 2 == 0
        held = jnp.concatenate([jnp.where(low, held, other), jnp.where(low, other, held)], axis=0)
        flip *= 2
    return held.reshape(-1, chunk.shape[-1])


def sum_over_dp(value):
    flip = 1
    while flip < lax.axis_size("dp"):
        value = value + lax.ppermute(
            value, "dp", [(r, r ^ flip) for r in range(lax.axis_size("dp"))]
        )
        flip *= 2
    return value


def body(section_input, out_cotangent, up_weight, down_weight, norm_gain):
    section_count = lax.axis_size("section")
    section_pos = lax.axis_index("section")
    inner = lax.axis_size("dp") // QUARTERS
    outer_pos = lax.axis_index("dp") // inner
    weight_up = up_weight[0]
    weight_down = down_weight[0]
    width = weight_up.shape[0]
    quarter_width = width // QUARTERS
    last = section_count - 1

    def place(section):
        return jnp.stack([section_pos == section, outer_pos]).astype(jnp.int32)

    def alike(section):
        return [s for s in range(section_count) if s % 2 == section % 2]

    def moves(section, step):
        return [(s, s + step) for s in alike(section) if 0 <= s + step < section_count]

    chunk = jnp.where(section_pos == last, out_cotangent, section_input)
    entered = gather_rows(chunk.reshape(-1, width), [0, last])

    pieces, stash = [entered], ()
    for section in range(section_count):
        parts, stash = forward_stage(
            place(section), pieces, norm_gain, weight_up, weight_down, stash, section < last
        )
        if section < last:
            if section == 0:
                own = lax.dynamic_slice_in_dim(entered, outer_pos * quarter_width, quarter_width, 1)
            else:
                own = pieces[0]
            result = own.astype(jnp.float32) + sum_quarters(parts, alike(section))
            pieces = hand_on(result.astype(jnp.bfloat16), moves(section, 1))

    rows, scale, preact = stash
    own_scale = scale[:, :1]
    own_rows = lax.dynamic_slice_in_dim(rows, outer_pos * quarter_width, quarter_width, 1)
    own_normed = own_rows.astype(jnp.float32) * own_scale
    own_gain = lax.dynamic_slice_in_dim(norm_gain, outer_pos * quarter_width, quarter_width, 1)
    pieces, grads = [entered], ()
    for section in range(last, -1, -1):
        parts, grads = backward_stage(
            place(section), pieces, stash, weight_up, weight_down, grads, section > 0
        )
        if section > 0:
            if section == last:
                own = lax.dynamic_slice_in_dim(entered, outer_pos * quarter_width, quarter_width, 1)
            else:
                own = pieces[0]
            total = sum_quarters(parts, alike(section))
            along = total[:, quarter_width : quarter_width + 1] * (1.0 / width)
            normed_grad = total[:, :quarter_width] * own_gain
            result = own.astype(jnp.float32) + own_scale * (normed_grad - own_normed * along)
            pieces = hand_on(result.astype(jnp.bfloat16), moves(section, -1))

    grad_rows, preact_grad, gain_part = grads
    grad_gain = sum_over_dp(gain_part)
    normed = rows.astype(jnp.float32) * own_scale
    scaled = (normed * norm_gain).astype(jnp.bfloat16)
    hidden = gelu_value(preact).astype(jnp.bfloat16)
    grad_down = outer_rows(grad_rows, hidden) * INV_HIDDEN
    grad_up = outer_rows(scaled, preact_grad) * INV_WIDTH
    return (grad_up[None], grad_down[None], grad_gain)


def solution(mesh):
    placed = (
        P(None, "dp", None),
        P(None, "dp", None),
        P("section", None, "dp"),
        P("section", None, "dp"),
        P("section", None),
    )
    return jax.shard_map(
        body,
        mesh=mesh,
        in_specs=placed,
        out_specs=(P("section", None, "dp"), P("section", None, "dp"), P("section", None)),
        check_vma=False,
    )
```

```python
import functools
import math

import jax
import jax.numpy as jnp
from jax import lax
from jax.experimental import pallas as pl
from jax.experimental.pallas import tpu as pltpu
from jax.sharding import PartitionSpec as P

D = 6656
HIDDEN_SIZE = 8960


EPSILON = 1e-05
GELU_SCALE = 0.7978845608028654
GELU_CUBIC = 0.044715

INV_WIDTH = 1.0 / math.sqrt(D)
INV_HIDDEN = 1.0 / math.sqrt(HIDDEN_SIZE)

AXES = ("section", "dp")
QUARTERS = 4
LANES = 128
BLOCK = 128
SLOTS = 3
STAGE_BYTES = 32 * 1024 * 1024
FINAL_BYTES = 52 * 1024 * 1024

ANY = pl.BlockSpec(memory_space=pl.ANY)
VMEM = pl.BlockSpec(memory_space=pltpu.VMEM)
SMEM = pl.BlockSpec(memory_space=pltpu.SMEM)


def gelu_value(preact):
    inner = GELU_SCALE * (preact + GELU_CUBIC * preact * preact * preact)
    return 0.5 * preact * (1.0 + jnp.tanh(inner))


def gelu_slope(preact):
    inner = GELU_SCALE * (preact + GELU_CUBIC * preact * preact * preact)
    tangent = jnp.tanh(inner)
    return 0.5 * (1.0 + tangent) + 0.5 * preact * (1.0 - tangent * tangent) * GELU_SCALE * (
        1.0 + 3.0 * GELU_CUBIC * preact * preact
    )


def outer_rows(left, right):
    return lax.dot_general(
        left, right, (((0,), (0,)), ((), ())), preferred_element_type=jnp.float32
    )


def across_hidden(left, right):
    return lax.dot_general(
        left, right, (((1,), (1,)), ((), ())), preferred_element_type=jnp.float32
    )


def plain_product(left, right):
    return jnp.dot(left, right, preferred_element_type=jnp.float32)


FAR, NEAR = (3, 2), (1, 0)


def quarter(place_ref, k, width):
    start = (place_ref[1] ^ k) * width
    return pl.ds(pl.multiple_of(start, LANES), width)


def read_quarter(place_ref, piece_refs, k, width):
    if len(piece_refs) == 1:
        return piece_refs[0][:, quarter(place_ref, k, width)]
    return piece_refs[k][...]


def write_out(copies):
    for copy in copies:
        copy.start()
    for copy in copies:
        copy.wait()


def quarter_copies(place_ref, piece_refs, target, sems, width):
    if len(piece_refs) == 1:
        return [pltpu.make_async_copy(piece_refs[0], target, sems.at[0])]
    return [
        pltpu.make_async_copy(ref, target.at[:, quarter(place_ref, k, width)], sems.at[k])
        for k, ref in enumerate(piece_refs)
    ]


def weight_copies(place_ref, source, buffer_ref, sems, quarters):
    width = buffer_ref.shape[2]
    return [
        pltpu.make_async_copy(
            source.at[:, quarter(place_ref, k, width)], buffer_ref.at[at], sems.at[at]
        )
        for at, k in enumerate(quarters)
    ]


def contract_width(buffer_ref, copies, read):
    total = None
    for k in range(QUARTERS):
        copies[k].wait()
        part = across_hidden(read(k), buffer_ref[k])
        total = part if total is None else total + part
    return total


def enter_section(place_ref, piece_refs, gain_ref, up_ref, up_copies, width):
    squares = 0.0
    for k in range(QUARTERS):
        values = read_quarter(place_ref, piece_refs, k, width).astype(jnp.float32)
        squares = squares + jnp.sum(values * values, axis=-1, keepdims=True)
    norm_scale = lax.rsqrt(squares * (1.0 / (QUARTERS * width)) + EPSILON)

    def read(k):
        normed = read_quarter(place_ref, piece_refs, k, width).astype(jnp.float32) * norm_scale
        return (normed * gain_ref[:, quarter(place_ref, k, width)]).astype(jnp.bfloat16)

    return (norm_scale, contract_width(up_ref, up_copies, read) * INV_WIDTH)


def hidden_part(part_refs, hidden, down_ref, copies):
    for at, ref in enumerate(part_refs):
        copies[at].wait()
        ref[...] = (plain_product(hidden, down_ref[at]) * INV_HIDDEN).astype(jnp.bfloat16)


def scaled_part(part_refs, quarters, preact_grad, along, rows_of, up_ref, copies, gain_ref):
    width = up_ref.shape[2]
    for at, k in enumerate(quarters):
        if copies:
            copies[at].wait()
        part = plain_product(preact_grad, up_ref[at if copies else k]) * INV_WIDTH
        gain_ref[at] = jnp.sum(part * rows_of(k), axis=0, keepdims=True)
        part_refs[at][:, :width] = part.astype(jnp.bfloat16)
        part_refs[at][:, width:] = along


def along_rows(preact_grad, preact):
    total = jnp.sum(preact_grad.astype(jnp.float32) * preact, axis=-1, keepdims=True)
    return jnp.broadcast_to(total.astype(jnp.bfloat16), (total.shape[0], LANES))


def gain_copies(place_ref, gain_ref, target, quarters, sems):
    return [
        pltpu.make_async_copy(gain_ref.at[at], target.at[place_ref[1] ^ k], sems.at[at])
        for at, k in enumerate(quarters)
    ]


def forward_far(section, pieces, with_stash, place_ref, *refs):
    piece_refs, refs = refs[:pieces], refs[pieces:]
    gain_ref, up_hbm, down_hbm = refs[:3]
    refs = refs[3 + (4 if with_stash else 0) :]
    part_refs, hidden_ref = refs[:2], refs[2]
    rows_out, scale_out, preact_out, own_out, scale_ref, preact_ref, own_ref, sems = refs[3:11]
    up_ref, down_ref, up_sems, down_sems = refs[11:]
    width = up_ref.shape[2]

    @pl.when(place_ref[0] == section)
    def _():
        up_copies = weight_copies(place_ref, up_hbm, up_ref, up_sems, range(QUARTERS))
        down_copies = weight_copies(place_ref, down_hbm, down_ref, down_sems, FAR)
        copies = quarter_copies(place_ref, piece_refs, rows_out, sems, width)
        for copy in up_copies + down_copies + copies:
            copy.start()
        norm_scale, preact = enter_section(
            place_ref, piece_refs, gain_ref, up_ref, up_copies, width
        )
        scale_ref[...] = jnp.broadcast_to(norm_scale, scale_ref.shape)
        preact_ref[...] = preact
        own_rows = read_quarter(place_ref, piece_refs, 0, width)
        own_ref[...] = own_rows.astype(jnp.float32) * norm_scale
        more = [
            pltpu.make_async_copy(scale_ref, scale_out, sems.at[QUARTERS]),
            pltpu.make_async_copy(preact_ref, preact_out, sems.at[QUARTERS + 1]),
            pltpu.make_async_copy(own_ref, own_out, sems.at[QUARTERS + 2]),
        ]
        for copy in more:
            copy.start()
        hidden = gelu_value(preact).astype(jnp.bfloat16)
        hidden_ref[...] = hidden
        hidden_part(part_refs, hidden, down_ref, down_copies)
        for copy in copies + more:
            copy.wait()


def forward_near(section, place_ref, hidden_ref, down_hbm, first_ref, second_ref, down_ref, sems):
    @pl.when(place_ref[0] == section)
    def _():
        copies = weight_copies(place_ref, down_hbm, down_ref, sems, NEAR)
        for copy in copies:
            copy.start()
        hidden_part([first_ref, second_ref], hidden_ref[...], down_ref, copies)


def early_grad(
    section, place_ref, rows_ref, down_hbm, grad_out, hidden_grad_out,
    total_ref, sems, down_ref, down_sems,
):
    width = down_ref.shape[2]

    @pl.when(place_ref[0] == section)
    def _():
        first = pltpu.make_async_copy(rows_ref, grad_out, sems.at[0])
        down_copies = weight_copies(place_ref, down_hbm, down_ref, down_sems, range(QUARTERS))
        for copy in down_copies + [first]:
            copy.start()
        total_ref[...] = INV_HIDDEN * contract_width(
            down_ref, down_copies, lambda k: read_quarter(place_ref, [rows_ref], k, width)
        )
        second = pltpu.make_async_copy(total_ref, hidden_grad_out, sems.at[1])
        second.start()
        first.wait()
        second.wait()


def last_far(section, place_ref, *refs):
    piece_refs, refs = refs[:QUARTERS], refs[QUARTERS:]
    hidden_grad_ref, gain_row_ref, up_hbm = refs[:3]
    refs = refs[7:]
    part_refs, preact_grad_ref, along_ref = refs[:2], refs[2], refs[3]
    rows_out, scale_out, preact_out, own_out, preact_grad_out, gain_out = refs[4:10]
    scale_ref, preact_ref, own_ref, gain_ref, sems, up_ref, up_sems = refs[10:]
    width = up_ref.shape[2]

    @pl.when(place_ref[0] == section)
    def _():
        up_copies = weight_copies(place_ref, up_hbm, up_ref, up_sems, range(QUARTERS))
        copies = quarter_copies(place_ref, piece_refs, rows_out, sems, width)
        for copy in up_copies + copies:
            copy.start()
        norm_scale, preact = enter_section(
            place_ref, piece_refs, gain_row_ref, up_ref, up_copies, width
        )
        preact_grad = (hidden_grad_ref[...] * gelu_slope(preact)).astype(jnp.bfloat16)
        along = along_rows(preact_grad, preact)
        scale_ref[...] = jnp.broadcast_to(norm_scale, scale_ref.shape)
        preact_ref[...] = preact
        preact_grad_ref[...] = preact_grad
        along_ref[...] = along
        own_ref[...] = piece_refs[0][...].astype(jnp.float32) * norm_scale
        more = [
            pltpu.make_async_copy(scale_ref, scale_out, sems.at[QUARTERS]),
            pltpu.make_async_copy(preact_ref, preact_out, sems.at[QUARTERS + 1]),
            pltpu.make_async_copy(own_ref, own_out, sems.at[QUARTERS + 2]),
            pltpu.make_async_copy(preact_grad_ref, preact_grad_out, sems.at[QUARTERS + 3]),
        ]
        for copy in more:
            copy.start()

        def rows_of(k):
            return piece_refs[k][...].astype(jnp.float32) * norm_scale

        scaled_part(part_refs, FAR, preact_grad, along, rows_of, up_ref, [], gain_ref)
        write_out(gain_copies(place_ref, gain_ref, gain_out, FAR, sems.at[pl.ds(QUARTERS + 4, 2)]))
        for copy in copies + more:
            copy.wait()


def backward_far(section, place_ref, *refs):
    piece_refs, refs = refs[:QUARTERS], refs[QUARTERS:]
    rows_ref, scale_ref, preact_ref, up_hbm, down_hbm = refs[:5]
    refs = refs[8:]
    part_refs, preact_grad_ref, along_ref = refs[:2], refs[2], refs[3]
    grad_out, preact_grad_out, gain_out, gain_ref, sems = refs[4:9]
    up_ref, down_ref, up_sems, down_sems = refs[9:]
    width = up_ref.shape[2]

    @pl.when(place_ref[0] == section)
    def _():
        down_copies = weight_copies(place_ref, down_hbm, down_ref, down_sems, range(QUARTERS))
        up_copies = weight_copies(place_ref, up_hbm, up_ref, up_sems, FAR)
        copies = quarter_copies(place_ref, piece_refs, grad_out, sems, width)
        for copy in down_copies + up_copies + copies:
            copy.start()
        hidden_grad = INV_HIDDEN * contract_width(
            down_ref, down_copies, lambda k: piece_refs[k][...]
        )
        preact = preact_ref[...]
        preact_grad = (hidden_grad * gelu_slope(preact)).astype(jnp.bfloat16)
        along = along_rows(preact_grad, preact)
        preact_grad_ref[...] = preact_grad
        along_ref[...] = along
        more = pltpu.make_async_copy(preact_grad_ref, preact_grad_out, sems.at[QUARTERS])
        more.start()
        norm_scale = scale_ref[:, :1]

        def rows_of(k):
            return rows_ref[:, quarter(place_ref, k, width)].astype(jnp.float32) * norm_scale

        scaled_part(
            part_refs, FAR, preact_grad, along, rows_of, up_ref, up_copies, gain_ref
        )
        write_out(gain_copies(place_ref, gain_ref, gain_out, FAR, sems.at[pl.ds(QUARTERS + 1, 2)]))
        for copy in copies + [more]:
            copy.wait()


def backward_near(
    section, place_ref, preact_grad_ref, along_ref, rows_ref, scale_ref, up_hbm, gain_in,
    first_ref, second_ref, gain_out, gain_ref, sems, up_ref, up_sems,
):
    del gain_in
    width = up_ref.shape[2]

    @pl.when(place_ref[0] == section)
    def _():
        copies = weight_copies(place_ref, up_hbm, up_ref, up_sems, NEAR)
        for copy in copies:
            copy.start()
        norm_scale = scale_ref[:, :1]

        def rows_of(k):
            return rows_ref[:, quarter(place_ref, k, width)].astype(jnp.float32) * norm_scale

        scaled_part(
            [first_ref, second_ref], NEAR, preact_grad_ref[...], along_ref[...],
            rows_of, up_ref, copies, gain_ref,
        )
        write_out(gain_copies(place_ref, gain_ref, gain_out, NEAR, sems))


def hidden_blocks(local):
    return [(start, min(BLOCK, local - start)) for start in range(0, local, BLOCK)]


def outer_blocks(left_ref, right_ref, factor, blocks, target, buffer_ref, sems, beside):
    copies = []
    for i, (start, size) in enumerate(blocks):
        slot = i % SLOTS
        if i >= SLOTS:
            copies[i - SLOTS].wait()
        value = outer_rows(left_ref[:, start : start + size], right_ref[...])
        buffer_ref[slot, :size] = value * factor
        copy = pltpu.make_async_copy(
            buffer_ref.at[slot, pl.ds(0, size)], target.at[pl.ds(start, size)], sems.at[slot]
        )
        copy.start()
        copies.append(copy)
        if i < len(beside):
            beside[i]()
    for run in beside[len(blocks) :]:
        run()
    for copy in copies[-SLOTS:]:
        copy.wait()


def final_down(section, place_ref, *refs):
    piece_refs, refs = refs[:QUARTERS], refs[QUARTERS:]
    grad_in, preact_grad_in, gain_in, rows_ref, scale_ref, preact_ref, gain_row_ref = refs[:7]
    up_hbm, down_hbm = refs[7:9]
    target, preact_grad_ref, gain_ref, scaled_ref = refs[9:13]
    grad_ref, hidden_ref, hidden_grad_ref, buffer_ref, sems = refs[13:18]
    up_ref, down_ref, up_sems, down_sems = refs[18:]
    width = up_ref.shape[2]
    active = place_ref[0] == section
    down_copies = weight_copies(place_ref, down_hbm, down_ref, down_sems, range(QUARTERS))
    up_copies = weight_copies(place_ref, up_hbm, up_ref, up_sems, range(QUARTERS))

    @pl.when(active)
    def _():
        for copy in down_copies + up_copies:
            copy.start()
        for k in range(QUARTERS):
            grad_ref[:, quarter(place_ref, k, width)] = piece_refs[k][...]

    @pl.when(jnp.logical_not(active))
    def _():
        grad_ref[...] = grad_in[...]
        preact_grad_ref[...] = preact_grad_in[...]
        gain_ref[...] = gain_in[...]

    norm_scale = scale_ref[:, :1]
    hidden_ref[...] = gelu_value(preact_ref[...]).astype(jnp.bfloat16)

    def add_grad(k):
        @pl.when(active)
        def _():
            down_copies[k].wait()
            part = across_hidden(piece_refs[k][...], down_ref[k])
            hidden_grad_ref[...] = part if k == 0 else hidden_grad_ref[...] + part

    def finish_grad():
        @pl.when(active)
        def _():
            hidden_grad = hidden_grad_ref[...] * INV_HIDDEN
            preact_grad_ref[...] = (hidden_grad * gelu_slope(preact_ref[...])).astype(jnp.bfloat16)

    def add_gain(k):
        @pl.when(active)
        def _():
            up_copies[k].wait()
            part = plain_product(preact_grad_ref[...], up_ref[k]) * INV_WIDTH
            rows = rows_ref[:, quarter(place_ref, k, width)]
            normed = rows.astype(jnp.float32) * norm_scale
            gain_ref[place_ref[1] ^ k] = jnp.sum(part * normed, axis=0, keepdims=True)

    def scale_rows():
        normed = rows_ref[...].astype(jnp.float32) * norm_scale
        scaled_ref[...] = (normed * gain_row_ref[...]).astype(jnp.bfloat16)

    beside = [functools.partial(add_grad, k) for k in range(QUARTERS)]
    beside += [finish_grad] + [functools.partial(add_gain, k) for k in range(QUARTERS)]
    beside += [scale_rows]
    blocks = hidden_blocks(target.shape[0])
    outer_blocks(hidden_ref, grad_ref, INV_HIDDEN, blocks, target, buffer_ref, sems, beside)


def final_up(blocks, preact_grad_ref, scaled_ref, *refs):
    target, buffer_ref, sems = refs[-3:]
    outer_blocks(preact_grad_ref, scaled_ref, INV_WIDTH, blocks, target, buffer_ref, sems, [])


def struct(*shape, dtype=jnp.bfloat16):
    return jax.ShapeDtypeStruct(shape, dtype)


def call(kernel, inputs, specs, outputs, out_specs, scratch, aliases, limit, products):
    flops = sum(2 * a * b * c for a, b, c in products)
    return pl.pallas_call(
        kernel,
        out_shape=outputs,
        in_specs=specs,
        out_specs=out_specs,
        scratch_shapes=scratch,
        input_output_aliases=aliases,
        cost_estimate=pl.CostEstimate(
            flops=flops,
            bytes_accessed=sum(2 * b * c for _, b, c in products),
            transcendentals=0,
        ),
        compiler_params=pltpu.CompilerParams(vmem_limit_bytes=limit),
    )(*inputs)


def lay_rows(place_ref, held_ref, gain_ref, rows_ref, own_ref, own_gain_ref):
    count, micro, tokens, width = held_ref.shape
    for i in range(count):
        for j in range(micro):
            start = (i * micro + j) * tokens
            rows_ref[start : start + tokens, :] = held_ref[i, j]
    own = quarter(place_ref, 0, width // QUARTERS)
    own_ref[...] = rows_ref[:, own]
    own_gain_ref[...] = gain_ref[:, own]


def run_lay_rows(place, held, gain):
    rows, width = held.size // held.shape[-1], held.shape[-1]
    return call(
        lay_rows,
        [place, held, gain],
        [SMEM, VMEM, VMEM],
        [
            struct(rows, width),
            struct(rows, width // QUARTERS),
            struct(1, width // QUARTERS, dtype=jnp.float32),
        ],
        [VMEM] * 3,
        [],
        {},
        STAGE_BYTES,
        [],
    )


def weight_buffer(up, quarters):
    return pltpu.VMEM((quarters, up.shape[0], up.shape[1] // QUARTERS), up.dtype)


def weight_sems(quarters):
    return pltpu.SemaphoreType.DMA((quarters,))


def run_forward_far(section, place, pieces, gain, up, down, stash):
    rows, (local, width) = pieces[0].shape[0], up.shape
    part = struct(rows, width // QUARTERS)
    first = 4 + len(pieces)
    result = call(
        functools.partial(forward_far, section, len(pieces), bool(stash)),
        [place, *pieces, gain, up, down, *stash],
        [SMEM] + [VMEM] * (len(pieces) + 1) + [ANY] * (2 + len(stash)),
        [
            part,
            part,
            struct(rows, local),
            struct(rows, width),
            struct(rows, LANES, dtype=jnp.float32),
            struct(rows, local, dtype=jnp.float32),
            struct(rows, width // QUARTERS, dtype=jnp.float32),
        ],
        [VMEM] * 3 + [ANY] * 4,
        [
            pltpu.VMEM((rows, LANES), jnp.float32),
            pltpu.VMEM((rows, local), jnp.float32),
            pltpu.VMEM((rows, width // QUARTERS), jnp.float32),
            pltpu.SemaphoreType.DMA((QUARTERS + 3,)),
            weight_buffer(up, QUARTERS),
            weight_buffer(up, 2),
            weight_sems(QUARTERS),
            weight_sems(2),
        ],
        {first + i: 3 + i for i in range(len(stash))},
        STAGE_BYTES,
        [(rows, width, local), (rows, local, width // 2)],
    )
    return (result[:2], result[2], result[3:])


def run_forward_near(section, place, hidden, down):
    rows, (local, width) = hidden.shape[0], down.shape
    part = struct(rows, width // QUARTERS)
    return call(
        functools.partial(forward_near, section),
        [place, hidden, down],
        [SMEM, VMEM, ANY],
        [part, part],
        [VMEM] * 2,
        [weight_buffer(down, 2), weight_sems(2)],
        {},
        STAGE_BYTES,
        [(rows, local, width // 2)],
    )


def run_early_grad(section, place, entered, down):
    rows, (local, width) = entered.shape[0], down.shape
    return call(
        functools.partial(early_grad, section),
        [place, entered, down],
        [SMEM, VMEM, ANY],
        [struct(rows, width), struct(rows, local, dtype=jnp.float32)],
        [ANY] * 2,
        [
            pltpu.VMEM((rows, local), jnp.float32),
            pltpu.SemaphoreType.DMA((2,)),
            weight_buffer(down, QUARTERS),
            weight_sems(QUARTERS),
        ],
        {},
        STAGE_BYTES,
        [(rows, width, local)],
    )


def run_last_far(section, place, pieces, hidden_grad, gain, up, stash):
    rows, (local, width) = pieces[0].shape[0], up.shape
    part = struct(rows, width // QUARTERS + LANES)
    result = call(
        functools.partial(last_far, section),
        [place, *pieces, hidden_grad, gain, up, *stash],
        [SMEM] + [VMEM] * (QUARTERS + 2) + [ANY] * 5,
        [
            part,
            part,
            struct(rows, local),
            struct(rows, LANES),
            struct(rows, width),
            struct(rows, LANES, dtype=jnp.float32),
            struct(rows, local, dtype=jnp.float32),
            struct(rows, width // QUARTERS, dtype=jnp.float32),
            struct(rows, local),
            struct(QUARTERS, 1, width // QUARTERS, dtype=jnp.float32),
        ],
        [VMEM] * 4 + [ANY] * 6,
        [
            pltpu.VMEM((rows, LANES), jnp.float32),
            pltpu.VMEM((rows, local), jnp.float32),
            pltpu.VMEM((rows, width // QUARTERS), jnp.float32),
            pltpu.VMEM((2, 1, width // QUARTERS), jnp.float32),
            pltpu.SemaphoreType.DMA((QUARTERS + 6,)),
            weight_buffer(up, QUARTERS),
            weight_sems(QUARTERS),
        ],
        {QUARTERS + 4 + i: 4 + i for i in range(4)},
        STAGE_BYTES,
        [(rows, width, local), (rows, local, width // 2)],
    )
    return (result[:2], result[2:4], result[4:8], result[8:])


def run_backward_far(section, place, pieces, kept, up, down, grads):
    rows, (local, width) = pieces[0].shape[0], up.shape
    part = struct(rows, width // QUARTERS + LANES)
    result = call(
        functools.partial(backward_far, section),
        [place, *pieces, *kept, up, down, *grads],
        [SMEM] + [VMEM] * (QUARTERS + 3) + [ANY] * 5,
        [
            part,
            part,
            struct(rows, local),
            struct(rows, LANES),
            struct(rows, width),
            struct(rows, local),
            struct(QUARTERS, 1, width // QUARTERS, dtype=jnp.float32),
        ],
        [VMEM] * 4 + [ANY] * 3,
        [
            pltpu.VMEM((2, 1, width // QUARTERS), jnp.float32),
            pltpu.SemaphoreType.DMA((QUARTERS + 3,)),
            weight_buffer(up, 2),
            weight_buffer(up, QUARTERS),
            weight_sems(2),
            weight_sems(QUARTERS),
        ],
        {QUARTERS + 6 + i: 4 + i for i in range(3)},
        STAGE_BYTES,
        [(rows, width, local), (rows, local, width // 2)],
    )
    return (result[:2], result[2:4], result[4:])


def run_backward_near(section, place, passed, kept, up, gain_part):
    rows, (local, width) = kept[0].shape[0], up.shape
    part = struct(rows, width // QUARTERS + LANES)
    result = call(
        functools.partial(backward_near, section),
        [place, *passed, kept[0], kept[1], up, gain_part],
        [SMEM] + [VMEM] * 4 + [ANY] * 2,
        [part, part, struct(*gain_part.shape, dtype=jnp.float32)],
        [VMEM, VMEM, ANY],
        [
            pltpu.VMEM((2, 1, width // QUARTERS), jnp.float32),
            pltpu.SemaphoreType.DMA((2,)),
            weight_buffer(up, 2),
            weight_sems(2),
        ],
        {6: 2},
        STAGE_BYTES,
        [(rows, local, width // 2)],
    )
    return (result[:2], result[2])


def run_final(section, place, pieces, grads, kept, gain, up, down):
    rows, (local, width) = pieces[0].shape[0], up.shape
    buffers = [
        pltpu.VMEM((SLOTS, BLOCK, width), jnp.float32),
        pltpu.SemaphoreType.DMA((SLOTS,)),
    ]
    grad_down, preact_grad, gain_part, scaled = call(
        functools.partial(final_down, section),
        [place, *pieces, *grads, *kept, gain, up, down],
        [SMEM] + [VMEM] * (QUARTERS + 7) + [ANY] * 2,
        [
            struct(local, width, dtype=jnp.float32),
            struct(rows, local),
            struct(*grads[2].shape, dtype=jnp.float32),
            struct(rows, width),
        ],
        [ANY] + [VMEM] * 3,
        [
            pltpu.VMEM((rows, width), jnp.bfloat16),
            pltpu.VMEM((rows, local), jnp.bfloat16),
            pltpu.VMEM((rows, local), jnp.float32),
            *buffers,
            weight_buffer(up, QUARTERS),
            weight_buffer(up, QUARTERS),
            weight_sems(QUARTERS),
            weight_sems(QUARTERS),
        ],
        {},
        FINAL_BYTES,
        [(rows, width, local)] * 2 + [(local, rows, width)],
    )
    blocks = hidden_blocks(local)
    half = (len(blocks) + 1) // 2
    grad_up = ()
    for taken in (blocks[:half], blocks[half:]):
        grad_up = call(
            functools.partial(final_up, taken),
            [preact_grad, scaled, *grad_up],
            [VMEM, VMEM] + [ANY] * len(grad_up),
            [struct(local, width, dtype=jnp.float32)],
            [ANY],
            buffers,
            {2: 0} if grad_up else {},
            FINAL_BYTES,
            [(local // 2, rows, width)],
        )
    return (grad_up[0], grad_down, gain_part)


def within(sections, flip):
    count = lax.axis_size("dp")
    return [(s * count + r, s * count + (r ^ flip)) for s in sections for r in range(count)]


def between(moves, flip):
    count = lax.axis_size("dp")
    return [(s * count + r, t * count + (r ^ flip)) for s, t in moves for r in range(count)]


def send_quarter(part, sections, k):
    return lax.ppermute(part, AXES, within(sections, k * (lax.axis_size("dp") // QUARTERS)))


def sum_quarters(own, arrived, sections):
    inner = lax.axis_size("dp") // QUARTERS
    total = own.astype(jnp.float32)
    for value in arrived:
        total = total + value.astype(jnp.float32)
    flip = 1
    while flip < inner:
        rounded = total.astype(jnp.bfloat16)
        other = lax.ppermute(rounded, AXES, within(sections, flip))
        total = rounded.astype(jnp.float32) + other.astype(jnp.float32)
        flip *= 2
    return total


def hand_on(own, moves):
    inner = lax.axis_size("dp") // QUARTERS
    pieces = {
        k: lax.ppermute(own, AXES, between(moves, k * inner)) for k in range(QUARTERS - 1, -1, -1)
    }
    return [pieces[k] for k in range(QUARTERS)]


def gather_chunks(chunk, sections, lows):
    held = chunk[None]
    for i, low in enumerate(lows):
        other = lax.ppermute(held, AXES, within(sections, 1 << i))
        held = jnp.concatenate([jnp.where(low, held, other), jnp.where(low, other, held)], axis=0)
    return held


def sum_over_dp(value):
    flip = 1
    while flip < lax.axis_size("dp"):
        value = value + lax.ppermute(
            value, "dp", [(r, r ^ flip) for r in range(lax.axis_size("dp"))]
        )
        flip *= 2
    return value


def body(section_input, out_cotangent, up_weight, down_weight, norm_gain):
    section_count = lax.axis_size("section")
    section_pos = lax.axis_index("section")
    count = lax.axis_size("dp")
    position = lax.axis_index("dp")
    outer_pos = position // (count // QUARTERS)
    width = up_weight.shape[1]
    quarter_width = width // QUARTERS
    last = section_count - 1

    def alike(section):
        return [s for s in range(section_count) if s % 2 == section % 2]

    def moves(section, step):
        return [(s, s + step) for s in alike(section) if 0 <= s + step < section_count]

    place = jnp.stack([section_pos, outer_pos]).astype(jnp.int32)
    lows = [(position >> i) % 2 == 0 for i in range(count.bit_length() - 1)]
    chunk = jnp.where(section_pos == last, out_cotangent, section_input)
    chunk, place, lows = lax.optimization_barrier((chunk, place, lows))
    held = gather_chunks(chunk, [0, last], lows)
    up = pltpu.with_memory_space_constraint(up_weight[0].T, pltpu.HBM)
    down = pltpu.with_memory_space_constraint(down_weight[0].T, pltpu.HBM)
    entered, own_entered, own_gain = run_lay_rows(place, held, norm_gain)

    pieces, stash, own = [entered], (), own_entered
    for section in range(last):
        here = alike(section)
        far, hidden, stash = run_forward_far(section, place, pieces, norm_gain, up, down, stash)
        arrived = [send_quarter(part, here, k) for part, k in zip(far, FAR)]
        near = run_forward_near(section, place, hidden, down)
        arrived.append(send_quarter(near[0], here, 1))
        result = own.astype(jnp.float32) + sum_quarters(near[1], arrived, here)
        pieces = hand_on(result.astype(jnp.bfloat16), moves(section, 1))
        own = pieces[0]
        if section == 0:
            grad_rows, early = run_early_grad(last, place, entered, down)

    for section in range(last, 0, -1):
        here = alike(section)
        if section == last:
            far, passed, stash, grads = run_last_far(
                last, place, pieces, early, norm_gain, up, stash
            )
            *stash, own_normed = stash
            own_scale = stash[1][:, :1]
            grads = [grad_rows, *grads]
            own = own_entered
        else:
            far, passed, grads = run_backward_far(section, place, pieces, stash, up, down, grads)
            own = pieces[0]
        arrived = [send_quarter(part, here, k) for part, k in zip(far, FAR)]
        near, gain_part = run_backward_near(section, place, passed, stash, up, grads[2])
        grads = [grads[0], grads[1], gain_part]
        arrived.append(send_quarter(near[0], here, 1))
        total = sum_quarters(near[1], arrived, here)
        along = total[:, quarter_width : quarter_width + 1] * (1.0 / width)
        normed_grad = total[:, :quarter_width] * own_gain
        result = own.astype(jnp.float32) + own_scale * (normed_grad - own_normed * along)
        pieces = hand_on(result.astype(jnp.bfloat16), moves(section, -1))

    grad_up, grad_down, gain_part = run_final(
        0, place, pieces, grads, stash, norm_gain, up, down
    )
    grad_gain = sum_over_dp(gain_part.reshape(1, width))
    return (grad_up.T[None], grad_down.T[None], grad_gain)


def solution(mesh):
    placed = (
        P(None, "dp", None),
        P(None, "dp", None),
        P("section", None, "dp"),
        P("section", None, "dp"),
        P("section", None),
    )
    return jax.shard_map(
        body,
        mesh=mesh,
        in_specs=placed,
        out_specs=(P("section", None, "dp"), P("section", None, "dp"), P("section", None)),
        check_vma=False,
    )
```

```python
import functools
import math

import jax
import jax.numpy as jnp
from jax import lax
from jax.experimental import pallas as pl
from jax.experimental.pallas import tpu as pltpu
from jax.sharding import PartitionSpec as P

D = 6656
HIDDEN_SIZE = 8960


EPSILON = 1e-05
GELU_SCALE = 0.7978845608028654
GELU_CUBIC = 0.044715

INV_WIDTH = 1.0 / math.sqrt(D)
INV_HIDDEN = 1.0 / math.sqrt(HIDDEN_SIZE)

AXES = ("section", "dp")
QUARTERS = 4
LANES = 128
BLOCK = 128
SLOTS = 3
STAGE_BYTES = 32 * 1024 * 1024
FINAL_BYTES = 52 * 1024 * 1024

ANY = pl.BlockSpec(memory_space=pl.ANY)
VMEM = pl.BlockSpec(memory_space=pltpu.VMEM)
SMEM = pl.BlockSpec(memory_space=pltpu.SMEM)


def gelu_value(preact):
    inner = GELU_SCALE * (preact + GELU_CUBIC * preact * preact * preact)
    return 0.5 * preact * (1.0 + jnp.tanh(inner))


def gelu_slope(preact):
    inner = GELU_SCALE * (preact + GELU_CUBIC * preact * preact * preact)
    tangent = jnp.tanh(inner)
    return 0.5 * (1.0 + tangent) + 0.5 * preact * (1.0 - tangent * tangent) * GELU_SCALE * (
        1.0 + 3.0 * GELU_CUBIC * preact * preact
    )


def outer_rows(left, right):
    return lax.dot_general(
        left, right, (((0,), (0,)), ((), ())), preferred_element_type=jnp.float32
    )


def across_hidden(left, right):
    return lax.dot_general(
        left, right, (((1,), (1,)), ((), ())), preferred_element_type=jnp.float32
    )


def plain_product(left, right):
    return jnp.dot(left, right, preferred_element_type=jnp.float32)


FAR, NEAR = (3, 2, 1), (0,)


def quarter(place_ref, k, width):
    start = (place_ref[1] ^ k) * width
    return pl.ds(pl.multiple_of(start, LANES), width)


def read_quarter(place_ref, piece_refs, k, width):
    if len(piece_refs) == 1:
        return piece_refs[0][:, quarter(place_ref, k, width)]
    return piece_refs[k][...]


def write_out(copies):
    for copy in copies:
        copy.start()
    for copy in copies:
        copy.wait()


def quarter_copies(place_ref, piece_refs, target, sems, width):
    if len(piece_refs) == 1:
        return [pltpu.make_async_copy(piece_refs[0], target, sems.at[0])]
    return [
        pltpu.make_async_copy(ref, target.at[:, quarter(place_ref, k, width)], sems.at[k])
        for k, ref in enumerate(piece_refs)
    ]


def weight_copies(place_ref, source, buffer_ref, sems, quarters):
    width = buffer_ref.shape[2]
    return [
        pltpu.make_async_copy(
            source.at[:, quarter(place_ref, k, width)], buffer_ref.at[at], sems.at[at]
        )
        for at, k in enumerate(quarters)
    ]


def contract_width(buffer_ref, copies, read):
    total = None
    for k in range(QUARTERS):
        copies[k].wait()
        part = across_hidden(buffer_ref[k], read(k))
        total = part if total is None else total + part
    return total.T


def enter_section(place_ref, piece_refs, gain_ref, up_ref, up_copies, width):
    squares = 0.0
    for k in range(QUARTERS):
        values = read_quarter(place_ref, piece_refs, k, width).astype(jnp.float32)
        squares = squares + jnp.sum(values * values, axis=-1, keepdims=True)
    norm_scale = lax.rsqrt(squares * (1.0 / (QUARTERS * width)) + EPSILON)

    def read(k):
        normed = read_quarter(place_ref, piece_refs, k, width).astype(jnp.float32) * norm_scale
        return (normed * gain_ref[:, quarter(place_ref, k, width)]).astype(jnp.bfloat16)

    return (norm_scale, contract_width(up_ref, up_copies, read) * INV_WIDTH)


def hidden_part(part_refs, hidden, down_ref, copies):
    for at, ref in enumerate(part_refs):
        copies[at].wait()
        ref[...] = (plain_product(hidden, down_ref[at]) * INV_HIDDEN).astype(jnp.bfloat16)


def scaled_part(part_refs, quarters, preact_grad, along, rows_of, up_ref, copies, gain_ref):
    width = up_ref.shape[2]
    for at, k in enumerate(quarters):
        if copies:
            copies[at].wait()
        part = plain_product(preact_grad, up_ref[at if copies else k]) * INV_WIDTH
        gain_ref[at] = jnp.sum(part * rows_of(k), axis=0, keepdims=True)
        part_refs[at][:, :width] = part.astype(jnp.bfloat16)
        part_refs[at][:, width:] = along


def along_rows(preact_grad, preact):
    total = jnp.sum(preact_grad.astype(jnp.float32) * preact, axis=-1, keepdims=True)
    return jnp.broadcast_to(total.astype(jnp.bfloat16), (total.shape[0], LANES))


def gain_copies(place_ref, gain_ref, target, quarters, sems):
    return [
        pltpu.make_async_copy(gain_ref.at[at], target.at[place_ref[1] ^ k], sems.at[at])
        for at, k in enumerate(quarters)
    ]


def forward_far(section, pieces, with_stash, place_ref, *refs):
    piece_refs, refs = refs[:pieces], refs[pieces:]
    gain_ref, up_hbm, down_hbm = refs[:3]
    refs = refs[3 + (4 if with_stash else 0) :]
    part_refs, hidden_ref, refs = refs[:3], refs[3], refs[4:]
    rows_out, scale_out, preact_out, own_out, scale_ref, preact_ref, own_ref, sems = refs[:8]
    up_ref, down_ref, up_sems, down_sems = refs[8:]
    width = up_ref.shape[2]

    @pl.when(place_ref[0] == section)
    def _():
        up_copies = weight_copies(place_ref, up_hbm, up_ref, up_sems, range(QUARTERS))
        down_copies = weight_copies(place_ref, down_hbm, down_ref, down_sems, FAR)
        copies = quarter_copies(place_ref, piece_refs, rows_out, sems, width)
        for copy in up_copies + down_copies + copies:
            copy.start()
        norm_scale, preact = enter_section(
            place_ref, piece_refs, gain_ref, up_ref, up_copies, width
        )
        scale_ref[...] = jnp.broadcast_to(norm_scale, scale_ref.shape)
        preact_ref[...] = preact
        own_rows = read_quarter(place_ref, piece_refs, 0, width)
        own_ref[...] = own_rows.astype(jnp.float32) * norm_scale
        more = [
            pltpu.make_async_copy(scale_ref, scale_out, sems.at[QUARTERS]),
            pltpu.make_async_copy(preact_ref, preact_out, sems.at[QUARTERS + 1]),
            pltpu.make_async_copy(own_ref, own_out, sems.at[QUARTERS + 2]),
        ]
        for copy in more:
            copy.start()
        hidden = gelu_value(preact).astype(jnp.bfloat16)
        hidden_ref[...] = hidden
        hidden_part(part_refs, hidden, down_ref, down_copies)
        for copy in copies + more:
            copy.wait()


def forward_near(section, place_ref, hidden_ref, down_hbm, part_ref, down_ref, sems):
    @pl.when(place_ref[0] == section)
    def _():
        copies = weight_copies(place_ref, down_hbm, down_ref, sems, NEAR)
        for copy in copies:
            copy.start()
        hidden_part([part_ref], hidden_ref[...], down_ref, copies)


def early_grad(
    section, place_ref, rows_ref, down_hbm, grad_out, hidden_grad_out,
    total_ref, sems, down_ref, down_sems,
):
    width = down_ref.shape[2]

    @pl.when(place_ref[0] == section)
    def _():
        first = pltpu.make_async_copy(rows_ref, grad_out, sems.at[0])
        down_copies = weight_copies(place_ref, down_hbm, down_ref, down_sems, range(QUARTERS))
        for copy in down_copies + [first]:
            copy.start()
        total_ref[...] = INV_HIDDEN * contract_width(
            down_ref, down_copies, lambda k: read_quarter(place_ref, [rows_ref], k, width)
        )
        second = pltpu.make_async_copy(total_ref, hidden_grad_out, sems.at[1])
        second.start()
        first.wait()
        second.wait()


def last_far(section, place_ref, *refs):
    piece_refs, refs = refs[:QUARTERS], refs[QUARTERS:]
    hidden_grad_ref, gain_row_ref, up_hbm = refs[:3]
    refs = refs[7:]
    part_refs, preact_grad_ref, along_ref, refs = refs[:3], refs[3], refs[4], refs[5:]
    rows_out, scale_out, preact_out, own_out, preact_grad_out, gain_out = refs[:6]
    scale_ref, preact_ref, own_ref, gain_ref, sems, up_ref, up_sems = refs[6:]
    width = up_ref.shape[2]

    @pl.when(place_ref[0] == section)
    def _():
        up_copies = weight_copies(place_ref, up_hbm, up_ref, up_sems, range(QUARTERS))
        copies = quarter_copies(place_ref, piece_refs, rows_out, sems, width)
        for copy in up_copies + copies:
            copy.start()
        norm_scale, preact = enter_section(
            place_ref, piece_refs, gain_row_ref, up_ref, up_copies, width
        )
        preact_grad = (hidden_grad_ref[...] * gelu_slope(preact)).astype(jnp.bfloat16)
        along = along_rows(preact_grad, preact)
        scale_ref[...] = jnp.broadcast_to(norm_scale, scale_ref.shape)
        preact_ref[...] = preact
        preact_grad_ref[...] = preact_grad
        along_ref[...] = along
        own_ref[...] = piece_refs[0][...].astype(jnp.float32) * norm_scale
        more = [
            pltpu.make_async_copy(scale_ref, scale_out, sems.at[QUARTERS]),
            pltpu.make_async_copy(preact_ref, preact_out, sems.at[QUARTERS + 1]),
            pltpu.make_async_copy(own_ref, own_out, sems.at[QUARTERS + 2]),
            pltpu.make_async_copy(preact_grad_ref, preact_grad_out, sems.at[QUARTERS + 3]),
        ]
        for copy in more:
            copy.start()

        def rows_of(k):
            return piece_refs[k][...].astype(jnp.float32) * norm_scale

        scaled_part(part_refs, FAR, preact_grad, along, rows_of, up_ref, [], gain_ref)
        write_out(gain_copies(place_ref, gain_ref, gain_out, FAR, sems.at[pl.ds(QUARTERS + 4, len(FAR))]))
        for copy in copies + more:
            copy.wait()


def backward_far(section, place_ref, *refs):
    piece_refs, refs = refs[:QUARTERS], refs[QUARTERS:]
    rows_ref, scale_ref, preact_ref, up_hbm, down_hbm = refs[:5]
    refs = refs[8:]
    part_refs, preact_grad_ref, along_ref, refs = refs[:3], refs[3], refs[4], refs[5:]
    grad_out, preact_grad_out, gain_out, gain_ref, sems = refs[:5]
    up_ref, down_ref, up_sems, down_sems = refs[5:]
    width = up_ref.shape[2]

    @pl.when(place_ref[0] == section)
    def _():
        down_copies = weight_copies(place_ref, down_hbm, down_ref, down_sems, range(QUARTERS))
        up_copies = weight_copies(place_ref, up_hbm, up_ref, up_sems, FAR)
        copies = quarter_copies(place_ref, piece_refs, grad_out, sems, width)
        for copy in down_copies + up_copies + copies:
            copy.start()
        hidden_grad = INV_HIDDEN * contract_width(
            down_ref, down_copies, lambda k: piece_refs[k][...]
        )
        preact = preact_ref[...]
        preact_grad = (hidden_grad * gelu_slope(preact)).astype(jnp.bfloat16)
        along = along_rows(preact_grad, preact)
        preact_grad_ref[...] = preact_grad
        along_ref[...] = along
        more = pltpu.make_async_copy(preact_grad_ref, preact_grad_out, sems.at[QUARTERS])
        more.start()
        norm_scale = scale_ref[:, :1]

        def rows_of(k):
            return rows_ref[:, quarter(place_ref, k, width)].astype(jnp.float32) * norm_scale

        scaled_part(
            part_refs, FAR, preact_grad, along, rows_of, up_ref, up_copies, gain_ref
        )
        write_out(gain_copies(place_ref, gain_ref, gain_out, FAR, sems.at[pl.ds(QUARTERS + 1, len(FAR))]))
        for copy in copies + [more]:
            copy.wait()


def backward_near(
    section, place_ref, preact_grad_ref, along_ref, rows_ref, scale_ref, up_hbm, gain_in,
    part_ref, gain_out, gain_ref, sems, up_ref, up_sems,
):
    del gain_in
    width = up_ref.shape[2]

    @pl.when(place_ref[0] == section)
    def _():
        copies = weight_copies(place_ref, up_hbm, up_ref, up_sems, NEAR)
        for copy in copies:
            copy.start()
        norm_scale = scale_ref[:, :1]

        def rows_of(k):
            return rows_ref[:, quarter(place_ref, k, width)].astype(jnp.float32) * norm_scale

        scaled_part(
            [part_ref], NEAR, preact_grad_ref[...], along_ref[...],
            rows_of, up_ref, copies, gain_ref,
        )
        write_out(gain_copies(place_ref, gain_ref, gain_out, NEAR, sems))


def hidden_blocks(local):
    return [(start, min(BLOCK, local - start)) for start in range(0, local, BLOCK)]


def outer_blocks(left_ref, right_ref, factor, blocks, target, buffer_ref, sems, beside):
    copies = []
    for i, (start, size) in enumerate(blocks):
        slot = i % SLOTS
        if i >= SLOTS:
            copies[i - SLOTS].wait()
        value = outer_rows(left_ref[:, start : start + size], right_ref[...])
        buffer_ref[slot, :size] = value * factor
        copy = pltpu.make_async_copy(
            buffer_ref.at[slot, pl.ds(0, size)], target.at[pl.ds(start, size)], sems.at[slot]
        )
        copy.start()
        copies.append(copy)
        if i < len(beside):
            beside[i]()
    for run in beside[len(blocks) :]:
        run()
    for copy in copies[-SLOTS:]:
        copy.wait()


def final_down(section, place_ref, *refs):
    piece_refs, refs = refs[:QUARTERS], refs[QUARTERS:]
    grad_in, preact_grad_in, gain_in, rows_ref, scale_ref, preact_ref, gain_row_ref = refs[:7]
    up_hbm, down_hbm = refs[7:9]
    target, preact_grad_ref, gain_ref, scaled_ref = refs[9:13]
    grad_ref, hidden_ref, hidden_grad_ref, buffer_ref, sems = refs[13:18]
    up_ref, down_ref, up_sems, down_sems = refs[18:]
    width = up_ref.shape[2]
    active = place_ref[0] == section
    down_copies = weight_copies(place_ref, down_hbm, down_ref, down_sems, range(QUARTERS))
    up_copies = weight_copies(place_ref, up_hbm, up_ref, up_sems, range(QUARTERS))

    @pl.when(active)
    def _():
        for copy in down_copies + up_copies:
            copy.start()
        for k in range(QUARTERS):
            grad_ref[:, quarter(place_ref, k, width)] = piece_refs[k][...]

    @pl.when(jnp.logical_not(active))
    def _():
        grad_ref[...] = grad_in[...]
        preact_grad_ref[...] = preact_grad_in[...]
        gain_ref[...] = gain_in[...]

    norm_scale = scale_ref[:, :1]
    hidden_ref[...] = gelu_value(preact_ref[...]).astype(jnp.bfloat16)

    def add_grad(k):
        @pl.when(active)
        def _():
            down_copies[k].wait()
            part = across_hidden(down_ref[k], piece_refs[k][...])
            hidden_grad_ref[...] = part if k == 0 else hidden_grad_ref[...] + part

    def finish_grad():
        @pl.when(active)
        def _():
            hidden_grad = hidden_grad_ref[...].T * INV_HIDDEN
            preact_grad_ref[...] = (hidden_grad * gelu_slope(preact_ref[...])).astype(jnp.bfloat16)

    def add_gain(k):
        @pl.when(active)
        def _():
            up_copies[k].wait()
            part = plain_product(preact_grad_ref[...], up_ref[k]) * INV_WIDTH
            rows = rows_ref[:, quarter(place_ref, k, width)]
            normed = rows.astype(jnp.float32) * norm_scale
            gain_ref[place_ref[1] ^ k] = jnp.sum(part * normed, axis=0, keepdims=True)

    def scale_rows():
        normed = rows_ref[...].astype(jnp.float32) * norm_scale
        scaled_ref[...] = (normed * gain_row_ref[...]).astype(jnp.bfloat16)

    beside = [functools.partial(add_grad, k) for k in range(QUARTERS)]
    beside += [finish_grad] + [functools.partial(add_gain, k) for k in range(QUARTERS)]
    beside += [scale_rows]
    blocks = hidden_blocks(target.shape[0])
    outer_blocks(hidden_ref, grad_ref, INV_HIDDEN, blocks, target, buffer_ref, sems, beside)


def final_up(blocks, preact_grad_ref, scaled_ref, *refs):
    target, buffer_ref, sems = refs[-3:]
    outer_blocks(preact_grad_ref, scaled_ref, INV_WIDTH, blocks, target, buffer_ref, sems, [])


def struct(*shape, dtype=jnp.bfloat16):
    return jax.ShapeDtypeStruct(shape, dtype)


def call(kernel, inputs, specs, outputs, out_specs, scratch, aliases, limit, products):
    flops = sum(2 * a * b * c for a, b, c in products)
    return pl.pallas_call(
        kernel,
        out_shape=outputs,
        in_specs=specs,
        out_specs=out_specs,
        scratch_shapes=scratch,
        input_output_aliases=aliases,
        cost_estimate=pl.CostEstimate(
            flops=flops,
            bytes_accessed=sum(2 * b * c for _, b, c in products),
            transcendentals=0,
        ),
        compiler_params=pltpu.CompilerParams(vmem_limit_bytes=limit),
    )(*inputs)


def lay_rows(place_ref, *refs):
    piece_refs, gain_ref = refs[:QUARTERS], refs[QUARTERS]
    rows_ref, own_ref, own_gain_ref = refs[QUARTERS + 1 :]
    inner, micro, tokens, width = piece_refs[0].shape
    for outer in range(QUARTERS):
        for k, ref in enumerate(piece_refs):

            @pl.when((place_ref[1] ^ k) == outer)
            def _(outer=outer, ref=ref):
                for i in range(inner):
                    for j in range(micro):
                        start = ((outer * inner + i) * micro + j) * tokens
                        rows_ref[start : start + tokens, :] = ref[place_ref[2] ^ i, j]

    own = quarter(place_ref, 0, width // QUARTERS)
    own_ref[...] = rows_ref[:, own]
    own_gain_ref[...] = gain_ref[:, own]


def run_lay_rows(place, pieces, gain):
    rows, width = QUARTERS * pieces[0].size // gain.size, gain.shape[1]
    return call(
        lay_rows,
        [place, *pieces, gain],
        [SMEM] + [VMEM] * (QUARTERS + 1),
        [
            struct(rows, width),
            struct(rows, width // QUARTERS),
            struct(1, width // QUARTERS, dtype=jnp.float32),
        ],
        [VMEM] * 3,
        [],
        {},
        STAGE_BYTES,
        [],
    )


def weight_buffer(up, quarters):
    return pltpu.VMEM((quarters, up.shape[0], up.shape[1] // QUARTERS), up.dtype)


def weight_sems(quarters):
    return pltpu.SemaphoreType.DMA((quarters,))


def run_forward_far(section, place, pieces, gain, up, down, stash):
    rows, (local, width) = pieces[0].shape[0], up.shape
    part = struct(rows, width // QUARTERS)
    first = 4 + len(pieces)
    result = call(
        functools.partial(forward_far, section, len(pieces), bool(stash)),
        [place, *pieces, gain, up, down, *stash],
        [SMEM] + [VMEM] * (len(pieces) + 1) + [ANY] * (2 + len(stash)),
        [
            *[part] * len(FAR),
            struct(rows, local),
            struct(rows, width),
            struct(rows, LANES, dtype=jnp.float32),
            struct(rows, local, dtype=jnp.float32),
            struct(rows, width // QUARTERS, dtype=jnp.float32),
        ],
        [VMEM] * 4 + [ANY] * 4,
        [
            pltpu.VMEM((rows, LANES), jnp.float32),
            pltpu.VMEM((rows, local), jnp.float32),
            pltpu.VMEM((rows, width // QUARTERS), jnp.float32),
            pltpu.SemaphoreType.DMA((QUARTERS + 3,)),
            weight_buffer(up, QUARTERS),
            weight_buffer(up, len(FAR)),
            weight_sems(QUARTERS),
            weight_sems(len(FAR)),
        ],
        {first + i: 4 + i for i in range(len(stash))},
        STAGE_BYTES,
        [(rows, width, local), (rows, local, 3 * width // 4)],
    )
    return (result[:3], result[3], result[4:])


def run_forward_near(section, place, hidden, down):
    rows, (local, width) = hidden.shape[0], down.shape
    part = struct(rows, width // QUARTERS)
    return call(
        functools.partial(forward_near, section),
        [place, hidden, down],
        [SMEM, VMEM, ANY],
        [part],
        [VMEM],
        [weight_buffer(down, len(NEAR)), weight_sems(len(NEAR))],
        {},
        STAGE_BYTES,
        [(rows, local, width // 4)],
    )


def run_early_grad(section, place, entered, down):
    rows, (local, width) = entered.shape[0], down.shape
    return call(
        functools.partial(early_grad, section),
        [place, entered, down],
        [SMEM, VMEM, ANY],
        [struct(rows, width), struct(rows, local, dtype=jnp.float32)],
        [ANY] * 2,
        [
            pltpu.VMEM((rows, local), jnp.float32),
            pltpu.SemaphoreType.DMA((2,)),
            weight_buffer(down, QUARTERS),
            weight_sems(QUARTERS),
        ],
        {},
        STAGE_BYTES,
        [(rows, width, local)],
    )


def run_last_far(section, place, pieces, hidden_grad, gain, up, stash):
    rows, (local, width) = pieces[0].shape[0], up.shape
    part = struct(rows, width // QUARTERS + LANES)
    result = call(
        functools.partial(last_far, section),
        [place, *pieces, hidden_grad, gain, up, *stash],
        [SMEM] + [VMEM] * (QUARTERS + 2) + [ANY] * 5,
        [
            *[part] * len(FAR),
            struct(rows, local),
            struct(rows, LANES),
            struct(rows, width),
            struct(rows, LANES, dtype=jnp.float32),
            struct(rows, local, dtype=jnp.float32),
            struct(rows, width // QUARTERS, dtype=jnp.float32),
            struct(rows, local),
            struct(QUARTERS, 1, width // QUARTERS, dtype=jnp.float32),
        ],
        [VMEM] * 5 + [ANY] * 6,
        [
            pltpu.VMEM((rows, LANES), jnp.float32),
            pltpu.VMEM((rows, local), jnp.float32),
            pltpu.VMEM((rows, width // QUARTERS), jnp.float32),
            pltpu.VMEM((len(FAR), 1, width // QUARTERS), jnp.float32),
            pltpu.SemaphoreType.DMA((QUARTERS + 7,)),
            weight_buffer(up, QUARTERS),
            weight_sems(QUARTERS),
        ],
        {QUARTERS + 4 + i: 5 + i for i in range(4)},
        STAGE_BYTES,
        [(rows, width, local), (rows, local, 3 * width // 4)],
    )
    return (result[:3], result[3:5], result[5:9], result[9:])


def run_backward_far(section, place, pieces, kept, up, down, grads):
    rows, (local, width) = pieces[0].shape[0], up.shape
    part = struct(rows, width // QUARTERS + LANES)
    result = call(
        functools.partial(backward_far, section),
        [place, *pieces, *kept, up, down, *grads],
        [SMEM] + [VMEM] * (QUARTERS + 3) + [ANY] * 5,
        [
            *[part] * len(FAR),
            struct(rows, local),
            struct(rows, LANES),
            struct(rows, width),
            struct(rows, local),
            struct(QUARTERS, 1, width // QUARTERS, dtype=jnp.float32),
        ],
        [VMEM] * 5 + [ANY] * 3,
        [
            pltpu.VMEM((len(FAR), 1, width // QUARTERS), jnp.float32),
            pltpu.SemaphoreType.DMA((QUARTERS + 4,)),
            weight_buffer(up, len(FAR)),
            weight_buffer(up, QUARTERS),
            weight_sems(len(FAR)),
            weight_sems(QUARTERS),
        ],
        {QUARTERS + 6 + i: 5 + i for i in range(3)},
        STAGE_BYTES,
        [(rows, width, local), (rows, local, 3 * width // 4)],
    )
    return (result[:3], result[3:5], result[5:])


def run_backward_near(section, place, passed, kept, up, gain_part):
    rows, (local, width) = kept[0].shape[0], up.shape
    part = struct(rows, width // QUARTERS + LANES)
    result = call(
        functools.partial(backward_near, section),
        [place, *passed, kept[0], kept[1], up, gain_part],
        [SMEM] + [VMEM] * 4 + [ANY] * 2,
        [part, struct(*gain_part.shape, dtype=jnp.float32)],
        [VMEM, ANY],
        [
            pltpu.VMEM((len(NEAR), 1, width // QUARTERS), jnp.float32),
            pltpu.SemaphoreType.DMA((len(NEAR),)),
            weight_buffer(up, len(NEAR)),
            weight_sems(len(NEAR)),
        ],
        {6: 1},
        STAGE_BYTES,
        [(rows, local, width // 4)],
    )
    return result


def run_final(section, place, pieces, grads, kept, gain, up, down):
    rows, (local, width) = pieces[0].shape[0], up.shape
    buffers = [
        pltpu.VMEM((SLOTS, BLOCK, width), jnp.float32),
        pltpu.SemaphoreType.DMA((SLOTS,)),
    ]
    grad_down, preact_grad, gain_part, scaled = call(
        functools.partial(final_down, section),
        [place, *pieces, *grads, *kept, gain, up, down],
        [SMEM] + [VMEM] * (QUARTERS + 7) + [ANY] * 2,
        [
            struct(local, width, dtype=jnp.float32),
            struct(rows, local),
            struct(*grads[2].shape, dtype=jnp.float32),
            struct(rows, width),
        ],
        [ANY] + [VMEM] * 3,
        [
            pltpu.VMEM((rows, width), jnp.bfloat16),
            pltpu.VMEM((rows, local), jnp.bfloat16),
            pltpu.VMEM((local, rows), jnp.float32),
            *buffers,
            weight_buffer(up, QUARTERS),
            weight_buffer(up, QUARTERS),
            weight_sems(QUARTERS),
            weight_sems(QUARTERS),
        ],
        {},
        FINAL_BYTES,
        [(rows, width, local)] * 2 + [(local, rows, width)],
    )
    blocks = hidden_blocks(local)
    half = (len(blocks) + 1) // 2
    grad_up = ()
    for taken in (blocks[:half], blocks[half:]):
        grad_up = call(
            functools.partial(final_up, taken),
            [preact_grad, scaled, *grad_up],
            [VMEM, VMEM] + [ANY] * len(grad_up),
            [struct(local, width, dtype=jnp.float32)],
            [ANY],
            buffers,
            {2: 0} if grad_up else {},
            FINAL_BYTES,
            [(local // 2, rows, width)],
        )
    return (grad_up[0], grad_down, gain_part)


def within(sections, flip):
    count = lax.axis_size("dp")
    return [(s * count + r, s * count + (r ^ flip)) for s in sections for r in range(count)]


def between(moves, flip):
    count = lax.axis_size("dp")
    return [(s * count + r, t * count + (r ^ flip)) for s, t in moves for r in range(count)]


def send_quarter(part, sections, k):
    return lax.ppermute(part, AXES, within(sections, k * (lax.axis_size("dp") // QUARTERS)))


def sum_quarters(own, arrived, sections):
    inner = lax.axis_size("dp") // QUARTERS
    total = own.astype(jnp.float32)
    for value in arrived:
        total = total + value.astype(jnp.float32)
    flip = 1
    while flip < inner:
        rounded = total.astype(jnp.bfloat16)
        other = lax.ppermute(rounded, AXES, within(sections, flip))
        total = rounded.astype(jnp.float32) + other.astype(jnp.float32)
        flip *= 2
    return total


def hand_on(own, moves):
    inner = lax.axis_size("dp") // QUARTERS
    pieces = {
        k: lax.ppermute(own, AXES, between(moves, k * inner)) for k in range(QUARTERS - 1, -1, -1)
    }
    return [pieces[k] for k in range(QUARTERS)]


def gather_chunks(chunk, sections):
    inner = lax.axis_size("dp") // QUARTERS
    held = chunk[None]
    flip = 1
    while flip < inner:
        other = lax.ppermute(held, AXES, within(sections, flip))
        held = jnp.concatenate([held, other], axis=0)
        flip *= 2
    pieces = {k: send_quarter(held, sections, k) for k in range(QUARTERS - 1, 0, -1)}
    return [held] + [pieces[k] for k in range(1, QUARTERS)]


def sum_over_dp(value):
    flip = 1
    while flip < lax.axis_size("dp"):
        value = value + lax.ppermute(
            value, "dp", [(r, r ^ flip) for r in range(lax.axis_size("dp"))]
        )
        flip *= 2
    return value


def body(section_input, out_cotangent, up_weight, down_weight, norm_gain):
    section_count = lax.axis_size("section")
    section_pos = lax.axis_index("section")
    count = lax.axis_size("dp")
    position = lax.axis_index("dp")
    width = up_weight.shape[1]
    quarter_width = width // QUARTERS
    last = section_count - 1

    def alike(section):
        return [s for s in range(section_count) if s % 2 == section % 2]

    def moves(section, step):
        return [(s, s + step) for s in alike(section) if 0 <= s + step < section_count]

    inner = count // QUARTERS
    place = jnp.stack([section_pos, position // inner, position % inner]).astype(jnp.int32)
    chunk = jnp.where(section_pos == last, out_cotangent, section_input)
    chunk, place = lax.optimization_barrier((chunk, place))
    held = gather_chunks(chunk, [0, last])
    up = pltpu.with_memory_space_constraint(up_weight[0].T, pltpu.HBM)
    down = pltpu.with_memory_space_constraint(down_weight[0].T, pltpu.HBM)
    entered, own_entered, own_gain = run_lay_rows(place, held, norm_gain)

    pieces, stash, own = [entered], (), own_entered
    for section in range(last):
        here = alike(section)
        far, hidden, stash = run_forward_far(section, place, pieces, norm_gain, up, down, stash)
        arrived = [send_quarter(part, here, k) for part, k in zip(far, FAR)]
        (near,) = run_forward_near(section, place, hidden, down)
        result = own.astype(jnp.float32) + sum_quarters(near, arrived, here)
        pieces = hand_on(result.astype(jnp.bfloat16), moves(section, 1))
        own = pieces[0]
        if section == 0:
            grad_rows, early = run_early_grad(last, place, entered, down)

    for section in range(last, 0, -1):
        here = alike(section)
        if section == last:
            far, passed, stash, grads = run_last_far(
                last, place, pieces, early, norm_gain, up, stash
            )
            *stash, own_normed = stash
            own_scale = stash[1][:, :1]
            grads = [grad_rows, *grads]
            own = own_entered
        else:
            far, passed, grads = run_backward_far(section, place, pieces, stash, up, down, grads)
            own = pieces[0]
        arrived = [send_quarter(part, here, k) for part, k in zip(far, FAR)]
        near, gain_part = run_backward_near(section, place, passed, stash, up, grads[2])
        grads = [grads[0], grads[1], gain_part]
        total = sum_quarters(near, arrived, here)
        along = total[:, quarter_width : quarter_width + 1] * (1.0 / width)
        normed_grad = total[:, :quarter_width] * own_gain
        result = own.astype(jnp.float32) + own_scale * (normed_grad - own_normed * along)
        pieces = hand_on(result.astype(jnp.bfloat16), moves(section, -1))

    grad_up, grad_down, gain_part = run_final(
        0, place, pieces, grads, stash, norm_gain, up, down
    )
    grad_gain = sum_over_dp(gain_part.reshape(1, width))
    return (grad_up.T[None], grad_down.T[None], grad_gain)


def solution(mesh):
    placed = (
        P(None, "dp", None),
        P(None, "dp", None),
        P("section", None, "dp"),
        P("section", None, "dp"),
        P("section", None),
    )
    return jax.shard_map(
        body,
        mesh=mesh,
        in_specs=placed,
        out_specs=(P("section", None, "dp"), P("section", None, "dp"), P("section", None)),
        check_vma=False,
    )
```

```python
import functools
import math

import jax
import jax.numpy as jnp
from jax import lax
from jax.experimental import pallas as pl
from jax.experimental.pallas import tpu as pltpu
from jax.sharding import PartitionSpec as P

D = 6656
HIDDEN_SIZE = 8960


EPSILON = 1e-05
GELU_SCALE = 0.7978845608028654
GELU_CUBIC = 0.044715

INV_WIDTH = 1.0 / math.sqrt(D)
INV_HIDDEN = 1.0 / math.sqrt(HIDDEN_SIZE)

AXES = ("section", "dp")
QUARTERS = 4
LANES = 128
BLOCK = 128
SLOTS = 3
STAGE_BYTES = 20 * 1024 * 1024
FINAL_BYTES = 34 * 1024 * 1024

ANY = pl.BlockSpec(memory_space=pl.ANY)
VMEM = pl.BlockSpec(memory_space=pltpu.VMEM)
SMEM = pl.BlockSpec(memory_space=pltpu.SMEM)


def gelu_value(preact):
    inner = GELU_SCALE * (preact + GELU_CUBIC * preact * preact * preact)
    return 0.5 * preact * (1.0 + jnp.tanh(inner))


def gelu_slope(preact):
    inner = GELU_SCALE * (preact + GELU_CUBIC * preact * preact * preact)
    tangent = jnp.tanh(inner)
    return 0.5 * (1.0 + tangent) + 0.5 * preact * (1.0 - tangent * tangent) * GELU_SCALE * (
        1.0 + 3.0 * GELU_CUBIC * preact * preact
    )


def outer_rows(left, right):
    return lax.dot_general(
        left, right, (((0,), (0,)), ((), ())), preferred_element_type=jnp.float32
    )


def across_hidden(left, right):
    return lax.dot_general(
        left, right, (((1,), (1,)), ((), ())), preferred_element_type=jnp.float32
    )


def plain_product(left, right):
    return jnp.dot(left, right, preferred_element_type=jnp.float32)


FAR, NEAR = (3, 2, 1), (0,)


def quarter(place_ref, k, width):
    start = (place_ref[1] ^ k) * width
    return pl.ds(pl.multiple_of(start, LANES), width)


def read_quarter(place_ref, piece_refs, k, width):
    if len(piece_refs) == 1:
        return piece_refs[0][:, quarter(place_ref, k, width)]
    return piece_refs[k][...]


def write_out(copies):
    for copy in copies:
        copy.start()
    for copy in copies:
        copy.wait()


def quarter_copies(place_ref, piece_refs, target, sems, width):
    if len(piece_refs) == 1:
        return [pltpu.make_async_copy(piece_refs[0], target, sems.at[0])]
    return [
        pltpu.make_async_copy(ref, target.at[:, quarter(place_ref, k, width)], sems.at[k])
        for k, ref in enumerate(piece_refs)
    ]


def weight_copies(place_ref, source, buffer_ref, sems, quarters):
    width = buffer_ref.shape[2]
    return [
        pltpu.make_async_copy(
            source.at[:, quarter(place_ref, k, width)], buffer_ref.at[at], sems.at[at]
        )
        for at, k in enumerate(quarters)
    ]


def streamed(buffer_ref, copies):
    def read(at, k):
        del k
        copies[at].wait()
        return buffer_ref[at]

    return read


def lying(place_ref, weight_ref):
    width = weight_ref.shape[1] // QUARTERS
    return lambda at, k: weight_ref[:, quarter(place_ref, k, width)]


def contract_width(weight, rows):
    total = None
    for k in range(QUARTERS):
        part = across_hidden(weight(k, k), rows(k))
        total = part if total is None else total + part
    return total.T


def enter_section(place_ref, piece_refs, gain_ref, up, width):
    squares = 0.0
    for k in range(QUARTERS):
        values = read_quarter(place_ref, piece_refs, k, width).astype(jnp.float32)
        squares = squares + jnp.sum(values * values, axis=-1, keepdims=True)
    norm_scale = lax.rsqrt(squares * (1.0 / (QUARTERS * width)) + EPSILON)

    def read(k):
        normed = read_quarter(place_ref, piece_refs, k, width).astype(jnp.float32) * norm_scale
        return (normed * gain_ref[:, quarter(place_ref, k, width)]).astype(jnp.bfloat16)

    return (norm_scale, contract_width(up, read) * INV_WIDTH)


def hidden_part(part_refs, quarters, hidden, down):
    for at, k in enumerate(quarters):
        part_refs[at][...] = (plain_product(hidden, down(at, k)) * INV_HIDDEN).astype(jnp.bfloat16)


def scaled_part(part_refs, quarters, preact_grad, along, rows_of, up, gain_ref):
    width = gain_ref.shape[2]
    for at, k in enumerate(quarters):
        part = plain_product(preact_grad, up(at, k)) * INV_WIDTH
        gain_ref[at] = jnp.sum(part * rows_of(k), axis=0, keepdims=True)
        part_refs[at][:, :width] = part.astype(jnp.bfloat16)
        part_refs[at][:, width:] = along


def along_rows(preact_grad, preact):
    total = jnp.sum(preact_grad.astype(jnp.float32) * preact, axis=-1, keepdims=True)
    return jnp.broadcast_to(total.astype(jnp.bfloat16), (total.shape[0], LANES))


def gain_copies(place_ref, gain_ref, target, quarters, sems):
    return [
        pltpu.make_async_copy(gain_ref.at[at], target.at[place_ref[1] ^ k], sems.at[at])
        for at, k in enumerate(quarters)
    ]


def forward_far(section, pieces, with_stash, place_ref, *refs):
    piece_refs, refs = refs[:pieces], refs[pieces:]
    gain_ref, up_ref, down_hbm = refs[:3]
    refs = refs[3 + (4 if with_stash else 0) :]
    part_refs, hidden_ref, refs = refs[:3], refs[3], refs[4:]
    rows_out, scale_out, preact_out, own_out, scale_ref, preact_ref, own_ref, sems = refs[:8]
    down_ref, down_sems = refs[8:]
    width = down_ref.shape[2]

    @pl.when(place_ref[0] == section)
    def _():
        down_copies = weight_copies(place_ref, down_hbm, down_ref, down_sems, FAR)
        copies = quarter_copies(place_ref, piece_refs, rows_out, sems, width)
        for copy in down_copies + copies:
            copy.start()
        norm_scale, preact = enter_section(
            place_ref, piece_refs, gain_ref, lying(place_ref, up_ref), width
        )
        scale_ref[...] = jnp.broadcast_to(norm_scale, scale_ref.shape)
        preact_ref[...] = preact
        own_rows = read_quarter(place_ref, piece_refs, 0, width)
        own_ref[...] = own_rows.astype(jnp.float32) * norm_scale
        more = [
            pltpu.make_async_copy(scale_ref, scale_out, sems.at[QUARTERS]),
            pltpu.make_async_copy(preact_ref, preact_out, sems.at[QUARTERS + 1]),
            pltpu.make_async_copy(own_ref, own_out, sems.at[QUARTERS + 2]),
        ]
        for copy in more:
            copy.start()
        hidden = gelu_value(preact).astype(jnp.bfloat16)
        hidden_ref[...] = hidden
        hidden_part(part_refs, FAR, hidden, streamed(down_ref, down_copies))
        for copy in copies + more:
            copy.wait()


def forward_near(section, place_ref, hidden_ref, down_hbm, part_ref, down_ref, sems):
    @pl.when(place_ref[0] == section)
    def _():
        copies = weight_copies(place_ref, down_hbm, down_ref, sems, NEAR)
        for copy in copies:
            copy.start()
        hidden_part([part_ref], NEAR, hidden_ref[...], streamed(down_ref, copies))


def early_grad(
    section, place_ref, rows_ref, down_hbm, grad_out, hidden_grad_out,
    total_ref, sems, down_ref, down_sems,
):
    width = down_ref.shape[2]

    @pl.when(place_ref[0] == section)
    def _():
        first = pltpu.make_async_copy(rows_ref, grad_out, sems.at[0])
        down_copies = weight_copies(place_ref, down_hbm, down_ref, down_sems, range(QUARTERS))
        for copy in down_copies + [first]:
            copy.start()
        total_ref[...] = INV_HIDDEN * contract_width(
            streamed(down_ref, down_copies),
            lambda k: read_quarter(place_ref, [rows_ref], k, width),
        )
        second = pltpu.make_async_copy(total_ref, hidden_grad_out, sems.at[1])
        second.start()
        first.wait()
        second.wait()


def last_far(section, place_ref, *refs):
    piece_refs, refs = refs[:QUARTERS], refs[QUARTERS:]
    hidden_grad_ref, gain_row_ref, up_ref = refs[:3]
    refs = refs[7:]
    part_refs, preact_grad_ref, along_ref, refs = refs[:3], refs[3], refs[4], refs[5:]
    rows_out, scale_out, preact_out, own_out, preact_grad_out, gain_out = refs[:6]
    scale_ref, preact_ref, own_ref, gain_ref, sems = refs[6:]
    width = gain_ref.shape[2]
    up = lying(place_ref, up_ref)

    @pl.when(place_ref[0] == section)
    def _():
        copies = quarter_copies(place_ref, piece_refs, rows_out, sems, width)
        for copy in copies:
            copy.start()
        norm_scale, preact = enter_section(place_ref, piece_refs, gain_row_ref, up, width)
        preact_grad = (hidden_grad_ref[...] * gelu_slope(preact)).astype(jnp.bfloat16)
        along = along_rows(preact_grad, preact)
        scale_ref[...] = jnp.broadcast_to(norm_scale, scale_ref.shape)
        preact_ref[...] = preact
        preact_grad_ref[...] = preact_grad
        along_ref[...] = along
        own_ref[...] = piece_refs[0][...].astype(jnp.float32) * norm_scale
        more = [
            pltpu.make_async_copy(scale_ref, scale_out, sems.at[QUARTERS]),
            pltpu.make_async_copy(preact_ref, preact_out, sems.at[QUARTERS + 1]),
            pltpu.make_async_copy(own_ref, own_out, sems.at[QUARTERS + 2]),
            pltpu.make_async_copy(preact_grad_ref, preact_grad_out, sems.at[QUARTERS + 3]),
        ]
        for copy in more:
            copy.start()

        def rows_of(k):
            return piece_refs[k][...].astype(jnp.float32) * norm_scale

        scaled_part(part_refs, FAR, preact_grad, along, rows_of, up, gain_ref)
        write_out(gain_copies(place_ref, gain_ref, gain_out, FAR, sems.at[pl.ds(QUARTERS + 4, len(FAR))]))
        for copy in copies + more:
            copy.wait()


def backward_far(section, place_ref, *refs):
    piece_refs, refs = refs[:QUARTERS], refs[QUARTERS:]
    rows_ref, scale_ref, preact_ref, up_ref, down_hbm = refs[:5]
    refs = refs[8:]
    part_refs, preact_grad_ref, along_ref, refs = refs[:3], refs[3], refs[4], refs[5:]
    grad_out, preact_grad_out, gain_out, gain_ref, sems = refs[:5]
    down_ref, down_sems = refs[5:]
    width = down_ref.shape[2]

    @pl.when(place_ref[0] == section)
    def _():
        down_copies = weight_copies(place_ref, down_hbm, down_ref, down_sems, range(QUARTERS))
        copies = quarter_copies(place_ref, piece_refs, grad_out, sems, width)
        for copy in down_copies + copies:
            copy.start()
        hidden_grad = INV_HIDDEN * contract_width(
            streamed(down_ref, down_copies), lambda k: piece_refs[k][...]
        )
        preact = preact_ref[...]
        preact_grad = (hidden_grad * gelu_slope(preact)).astype(jnp.bfloat16)
        along = along_rows(preact_grad, preact)
        preact_grad_ref[...] = preact_grad
        along_ref[...] = along
        more = pltpu.make_async_copy(preact_grad_ref, preact_grad_out, sems.at[QUARTERS])
        more.start()
        norm_scale = scale_ref[:, :1]

        def rows_of(k):
            return rows_ref[:, quarter(place_ref, k, width)].astype(jnp.float32) * norm_scale

        up = lying(place_ref, up_ref)
        scaled_part(part_refs, FAR, preact_grad, along, rows_of, up, gain_ref)
        write_out(gain_copies(place_ref, gain_ref, gain_out, FAR, sems.at[pl.ds(QUARTERS + 1, len(FAR))]))
        for copy in copies + [more]:
            copy.wait()


def backward_near(
    section, place_ref, preact_grad_ref, along_ref, rows_ref, scale_ref, up_ref, gain_in,
    part_ref, gain_out, gain_ref, sems,
):
    del gain_in
    width = gain_ref.shape[2]

    @pl.when(place_ref[0] == section)
    def _():
        norm_scale = scale_ref[:, :1]

        def rows_of(k):
            return rows_ref[:, quarter(place_ref, k, width)].astype(jnp.float32) * norm_scale

        scaled_part(
            [part_ref], NEAR, preact_grad_ref[...], along_ref[...],
            rows_of, lying(place_ref, up_ref), gain_ref,
        )
        write_out(gain_copies(place_ref, gain_ref, gain_out, NEAR, sems))


def hidden_blocks(local):
    return [(start, min(BLOCK, local - start)) for start in range(0, local, BLOCK)]


def outer_blocks(left_ref, right_ref, factor, blocks, target, buffer_ref, sems, beside):
    copies = []
    for i, (start, size) in enumerate(blocks):
        slot = i % SLOTS
        if i >= SLOTS:
            copies[i - SLOTS].wait()
        value = outer_rows(left_ref[:, start : start + size], right_ref[...])
        buffer_ref[slot, :size] = value * factor
        copy = pltpu.make_async_copy(
            buffer_ref.at[slot, pl.ds(0, size)], target.at[pl.ds(start, size)], sems.at[slot]
        )
        copy.start()
        copies.append(copy)
        if i < len(beside):
            beside[i]()
    for run in beside[len(blocks) :]:
        run()
    for copy in copies[-SLOTS:]:
        copy.wait()


def final_down(section, place_ref, *refs):
    piece_refs, refs = refs[:QUARTERS], refs[QUARTERS:]
    grad_in, preact_grad_in, gain_in, rows_ref, scale_ref, preact_ref, gain_row_ref = refs[:7]
    up_ref, down_hbm = refs[7:9]
    target, preact_grad_ref, gain_ref, scaled_ref = refs[9:13]
    grad_ref, hidden_ref, hidden_grad_ref, buffer_ref, sems = refs[13:18]
    down_ref, down_sems = refs[18:]
    width = down_ref.shape[2]
    up = lying(place_ref, up_ref)
    active = place_ref[0] == section
    down_copies = weight_copies(place_ref, down_hbm, down_ref, down_sems, range(QUARTERS))

    @pl.when(active)
    def _():
        for copy in down_copies:
            copy.start()
        for k in range(QUARTERS):
            grad_ref[:, quarter(place_ref, k, width)] = piece_refs[k][...]

    @pl.when(jnp.logical_not(active))
    def _():
        grad_ref[...] = grad_in[...]
        preact_grad_ref[...] = preact_grad_in[...]
        gain_ref[...] = gain_in[...]

    norm_scale = scale_ref[:, :1]
    hidden_ref[...] = gelu_value(preact_ref[...]).astype(jnp.bfloat16)

    def add_grad(k):
        @pl.when(active)
        def _():
            down_copies[k].wait()
            part = across_hidden(down_ref[k], piece_refs[k][...])
            hidden_grad_ref[...] = part if k == 0 else hidden_grad_ref[...] + part

    def finish_grad():
        @pl.when(active)
        def _():
            hidden_grad = hidden_grad_ref[...].T * INV_HIDDEN
            preact_grad_ref[...] = (hidden_grad * gelu_slope(preact_ref[...])).astype(jnp.bfloat16)

    def add_gain(k):
        @pl.when(active)
        def _():
            part = plain_product(preact_grad_ref[...], up(k, k)) * INV_WIDTH
            rows = rows_ref[:, quarter(place_ref, k, width)]
            normed = rows.astype(jnp.float32) * norm_scale
            gain_ref[place_ref[1] ^ k] = jnp.sum(part * normed, axis=0, keepdims=True)

    def scale_rows():
        normed = rows_ref[...].astype(jnp.float32) * norm_scale
        scaled_ref[...] = (normed * gain_row_ref[...]).astype(jnp.bfloat16)

    beside = [functools.partial(add_grad, k) for k in range(QUARTERS)]
    beside += [finish_grad] + [functools.partial(add_gain, k) for k in range(QUARTERS)]
    beside += [scale_rows]
    blocks = hidden_blocks(target.shape[0])
    outer_blocks(hidden_ref, grad_ref, INV_HIDDEN, blocks, target, buffer_ref, sems, beside)


def final_up(blocks, preact_grad_ref, scaled_ref, *refs):
    target, buffer_ref, sems = refs[-3:]
    outer_blocks(preact_grad_ref, scaled_ref, INV_WIDTH, blocks, target, buffer_ref, sems, [])


def struct(*shape, dtype=jnp.bfloat16):
    return jax.ShapeDtypeStruct(shape, dtype)


def call(kernel, inputs, specs, outputs, out_specs, scratch, aliases, limit, products):
    flops = sum(2 * a * b * c for a, b, c in products)
    return pl.pallas_call(
        kernel,
        out_shape=outputs,
        in_specs=specs,
        out_specs=out_specs,
        scratch_shapes=scratch,
        input_output_aliases=aliases,
        cost_estimate=pl.CostEstimate(
            flops=flops,
            bytes_accessed=sum(2 * b * c for _, b, c in products),
            transcendentals=0,
        ),
        compiler_params=pltpu.CompilerParams(vmem_limit_bytes=limit),
    )(*inputs)


def lay_rows(place_ref, *refs):
    piece_refs, gain_ref = refs[:QUARTERS], refs[QUARTERS]
    rows_ref, own_ref, own_gain_ref = refs[QUARTERS + 1 :]
    inner, micro, tokens, width = piece_refs[0].shape
    for outer in range(QUARTERS):
        for k, ref in enumerate(piece_refs):

            @pl.when((place_ref[1] ^ k) == outer)
            def _(outer=outer, ref=ref):
                for i in range(inner):
                    for j in range(micro):
                        start = ((outer * inner + i) * micro + j) * tokens
                        rows_ref[start : start + tokens, :] = ref[place_ref[2] ^ i, j]

    own = quarter(place_ref, 0, width // QUARTERS)
    own_ref[...] = rows_ref[:, own]
    own_gain_ref[...] = gain_ref[:, own]


def run_lay_rows(place, pieces, gain):
    rows, width = QUARTERS * pieces[0].size // gain.size, gain.shape[1]
    return call(
        lay_rows,
        [place, *pieces, gain],
        [SMEM] + [VMEM] * (QUARTERS + 1),
        [
            struct(rows, width),
            struct(rows, width // QUARTERS),
            struct(1, width // QUARTERS, dtype=jnp.float32),
        ],
        [VMEM] * 3,
        [],
        {},
        STAGE_BYTES,
        [],
    )


def weight_buffer(up, quarters):
    return pltpu.VMEM((quarters, up.shape[0], up.shape[1] // QUARTERS), up.dtype)


def weight_sems(quarters):
    return pltpu.SemaphoreType.DMA((quarters,))


def run_forward_far(section, place, pieces, gain, up, down, stash):
    rows, (local, width) = pieces[0].shape[0], up.shape
    part = struct(rows, width // QUARTERS)
    first = 4 + len(pieces)
    result = call(
        functools.partial(forward_far, section, len(pieces), bool(stash)),
        [place, *pieces, gain, up, down, *stash],
        [SMEM] + [VMEM] * (len(pieces) + 2) + [ANY] * (1 + len(stash)),
        [
            *[part] * len(FAR),
            struct(rows, local),
            struct(rows, width),
            struct(rows, LANES, dtype=jnp.float32),
            struct(rows, local, dtype=jnp.float32),
            struct(rows, width // QUARTERS, dtype=jnp.float32),
        ],
        [VMEM] * 4 + [ANY] * 4,
        [
            pltpu.VMEM((rows, LANES), jnp.float32),
            pltpu.VMEM((rows, local), jnp.float32),
            pltpu.VMEM((rows, width // QUARTERS), jnp.float32),
            pltpu.SemaphoreType.DMA((QUARTERS + 3,)),
            weight_buffer(down, len(FAR)),
            weight_sems(len(FAR)),
        ],
        {first + i: 4 + i for i in range(len(stash))},
        STAGE_BYTES,
        [(rows, width, local), (rows, local, 3 * width // 4)],
    )
    return (result[:3], result[3], result[4:])


def run_forward_near(section, place, hidden, down):
    rows, (local, width) = hidden.shape[0], down.shape
    part = struct(rows, width // QUARTERS)
    return call(
        functools.partial(forward_near, section),
        [place, hidden, down],
        [SMEM, VMEM, ANY],
        [part],
        [VMEM],
        [weight_buffer(down, len(NEAR)), weight_sems(len(NEAR))],
        {},
        STAGE_BYTES,
        [(rows, local, width // 4)],
    )


def run_early_grad(section, place, entered, down):
    rows, (local, width) = entered.shape[0], down.shape
    return call(
        functools.partial(early_grad, section),
        [place, entered, down],
        [SMEM, VMEM, ANY],
        [struct(rows, width), struct(rows, local, dtype=jnp.float32)],
        [ANY] * 2,
        [
            pltpu.VMEM((rows, local), jnp.float32),
            pltpu.SemaphoreType.DMA((2,)),
            weight_buffer(down, QUARTERS),
            weight_sems(QUARTERS),
        ],
        {},
        STAGE_BYTES,
        [(rows, width, local)],
    )


def run_last_far(section, place, pieces, hidden_grad, gain, up, stash):
    rows, (local, width) = pieces[0].shape[0], up.shape
    part = struct(rows, width // QUARTERS + LANES)
    result = call(
        functools.partial(last_far, section),
        [place, *pieces, hidden_grad, gain, up, *stash],
        [SMEM] + [VMEM] * (QUARTERS + 3) + [ANY] * 4,
        [
            *[part] * len(FAR),
            struct(rows, local),
            struct(rows, LANES),
            struct(rows, width),
            struct(rows, LANES, dtype=jnp.float32),
            struct(rows, local, dtype=jnp.float32),
            struct(rows, width // QUARTERS, dtype=jnp.float32),
            struct(rows, local),
            struct(QUARTERS, 1, width // QUARTERS, dtype=jnp.float32),
        ],
        [VMEM] * 5 + [ANY] * 6,
        [
            pltpu.VMEM((rows, LANES), jnp.float32),
            pltpu.VMEM((rows, local), jnp.float32),
            pltpu.VMEM((rows, width // QUARTERS), jnp.float32),
            pltpu.VMEM((len(FAR), 1, width // QUARTERS), jnp.float32),
            pltpu.SemaphoreType.DMA((QUARTERS + 7,)),
        ],
        {QUARTERS + 4 + i: 5 + i for i in range(4)},
        STAGE_BYTES,
        [(rows, width, local), (rows, local, 3 * width // 4)],
    )
    return (result[:3], result[3:5], result[5:9], result[9:])


def run_backward_far(section, place, pieces, kept, up, down, grads):
    rows, (local, width) = pieces[0].shape[0], up.shape
    part = struct(rows, width // QUARTERS + LANES)
    result = call(
        functools.partial(backward_far, section),
        [place, *pieces, *kept, up, down, *grads],
        [SMEM] + [VMEM] * (QUARTERS + 4) + [ANY] * 4,
        [
            *[part] * len(FAR),
            struct(rows, local),
            struct(rows, LANES),
            struct(rows, width),
            struct(rows, local),
            struct(QUARTERS, 1, width // QUARTERS, dtype=jnp.float32),
        ],
        [VMEM] * 5 + [ANY] * 3,
        [
            pltpu.VMEM((len(FAR), 1, width // QUARTERS), jnp.float32),
            pltpu.SemaphoreType.DMA((QUARTERS + 4,)),
            weight_buffer(down, QUARTERS),
            weight_sems(QUARTERS),
        ],
        {QUARTERS + 6 + i: 5 + i for i in range(3)},
        STAGE_BYTES,
        [(rows, width, local), (rows, local, 3 * width // 4)],
    )
    return (result[:3], result[3:5], result[5:])


def run_backward_near(section, place, passed, kept, up, gain_part):
    rows, (local, width) = kept[0].shape[0], up.shape
    part = struct(rows, width // QUARTERS + LANES)
    result = call(
        functools.partial(backward_near, section),
        [place, *passed, kept[0], kept[1], up, gain_part],
        [SMEM] + [VMEM] * 5 + [ANY],
        [part, struct(*gain_part.shape, dtype=jnp.float32)],
        [VMEM, ANY],
        [
            pltpu.VMEM((len(NEAR), 1, width // QUARTERS), jnp.float32),
            pltpu.SemaphoreType.DMA((len(NEAR),)),
        ],
        {6: 1},
        STAGE_BYTES,
        [(rows, local, width // 4)],
    )
    return result


def run_final(section, place, pieces, grads, kept, gain, up, down):
    rows, (local, width) = pieces[0].shape[0], up.shape
    buffers = [
        pltpu.VMEM((SLOTS, BLOCK, width), jnp.float32),
        pltpu.SemaphoreType.DMA((SLOTS,)),
    ]
    grad_down, preact_grad, gain_part, scaled = call(
        functools.partial(final_down, section),
        [place, *pieces, *grads, *kept, gain, up, down],
        [SMEM] + [VMEM] * (QUARTERS + 8) + [ANY],
        [
            struct(local, width, dtype=jnp.float32),
            struct(rows, local),
            struct(*grads[2].shape, dtype=jnp.float32),
            struct(rows, width),
        ],
        [ANY] + [VMEM] * 3,
        [
            pltpu.VMEM((rows, width), jnp.bfloat16),
            pltpu.VMEM((rows, local), jnp.bfloat16),
            pltpu.VMEM((local, rows), jnp.float32),
            *buffers,
            weight_buffer(down, QUARTERS),
            weight_sems(QUARTERS),
        ],
        {},
        FINAL_BYTES,
        [(rows, width, local)] * 2 + [(local, rows, width)],
    )
    blocks = hidden_blocks(local)
    half = (len(blocks) + 1) // 2
    grad_up = ()
    for taken in (blocks[:half], blocks[half:]):
        grad_up = call(
            functools.partial(final_up, taken),
            [preact_grad, scaled, *grad_up],
            [VMEM, VMEM] + [ANY] * len(grad_up),
            [struct(local, width, dtype=jnp.float32)],
            [ANY],
            buffers,
            {2: 0} if grad_up else {},
            FINAL_BYTES,
            [(local // 2, rows, width)],
        )
    return (grad_up[0], grad_down, gain_part)


def within(sections, flip):
    count = lax.axis_size("dp")
    return [(s * count + r, s * count + (r ^ flip)) for s in sections for r in range(count)]


def between(moves, flip):
    count = lax.axis_size("dp")
    return [(s * count + r, t * count + (r ^ flip)) for s, t in moves for r in range(count)]


def send_quarter(part, sections, k):
    return lax.ppermute(part, AXES, within(sections, k * (lax.axis_size("dp") // QUARTERS)))


def sum_quarters(own, arrived, sections):
    inner = lax.axis_size("dp") // QUARTERS
    total = own.astype(jnp.float32)
    for value in arrived:
        total = total + value.astype(jnp.float32)
    flip = 1
    while flip < inner:
        rounded = total.astype(jnp.bfloat16)
        other = lax.ppermute(rounded, AXES, within(sections, flip))
        total = rounded.astype(jnp.float32) + other.astype(jnp.float32)
        flip *= 2
    return total


def hand_on(own, moves):
    inner = lax.axis_size("dp") // QUARTERS
    pieces = {
        k: lax.ppermute(own, AXES, between(moves, k * inner)) for k in range(QUARTERS - 1, -1, -1)
    }
    return [pieces[k] for k in range(QUARTERS)]


def gather_chunks(chunk, sections):
    inner = lax.axis_size("dp") // QUARTERS
    held = chunk[None]
    flip = 1
    while flip < inner:
        other = lax.ppermute(held, AXES, within(sections, flip))
        held = jnp.concatenate([held, other], axis=0)
        flip *= 2
    pieces = {k: send_quarter(held, sections, k) for k in range(QUARTERS - 1, 0, -1)}
    return [held] + [pieces[k] for k in range(1, QUARTERS)]


def sum_over_dp(value):
    flip = 1
    while flip < lax.axis_size("dp"):
        value = value + lax.ppermute(
            value, "dp", [(r, r ^ flip) for r in range(lax.axis_size("dp"))]
        )
        flip *= 2
    return value


def body(section_input, out_cotangent, up_weight, down_weight, norm_gain):
    section_count = lax.axis_size("section")
    section_pos = lax.axis_index("section")
    count = lax.axis_size("dp")
    position = lax.axis_index("dp")
    width = up_weight.shape[1]
    quarter_width = width // QUARTERS
    last = section_count - 1

    def alike(section):
        return [s for s in range(section_count) if s % 2 == section % 2]

    def moves(section, step):
        return [(s, s + step) for s in alike(section) if 0 <= s + step < section_count]

    inner = count // QUARTERS
    place = jnp.stack([section_pos, position // inner, position % inner]).astype(jnp.int32)
    chunk = jnp.where(section_pos == last, out_cotangent, section_input)
    chunk, place = lax.optimization_barrier((chunk, place))
    held = gather_chunks(chunk, [0, last])
    up = pltpu.with_memory_space_constraint(up_weight[0].T, pltpu.VMEM)
    down = pltpu.with_memory_space_constraint(down_weight[0].T, pltpu.HBM)
    entered, own_entered, own_gain = run_lay_rows(place, held, norm_gain)

    pieces, stash, own = [entered], (), own_entered
    for section in range(last):
        here = alike(section)
        far, hidden, stash = run_forward_far(section, place, pieces, norm_gain, up, down, stash)
        arrived = [send_quarter(part, here, k) for part, k in zip(far, FAR)]
        (near,) = run_forward_near(section, place, hidden, down)
        result = own.astype(jnp.float32) + sum_quarters(near, arrived, here)
        pieces = hand_on(result.astype(jnp.bfloat16), moves(section, 1))
        own = pieces[0]
        if section == 0:
            grad_rows, early = run_early_grad(last, place, entered, down)

    for section in range(last, 0, -1):
        here = alike(section)
        if section == last:
            far, passed, stash, grads = run_last_far(
                last, place, pieces, early, norm_gain, up, stash
            )
            *stash, own_normed = stash
            own_scale = stash[1][:, :1]
            grads = [grad_rows, *grads]
            own = own_entered
        else:
            far, passed, grads = run_backward_far(section, place, pieces, stash, up, down, grads)
            own = pieces[0]
        arrived = [send_quarter(part, here, k) for part, k in zip(far, FAR)]
        near, gain_part = run_backward_near(section, place, passed, stash, up, grads[2])
        grads = [grads[0], grads[1], gain_part]
        total = sum_quarters(near, arrived, here)
        along = total[:, quarter_width : quarter_width + 1] * (1.0 / width)
        normed_grad = total[:, :quarter_width] * own_gain
        result = own.astype(jnp.float32) + own_scale * (normed_grad - own_normed * along)
        pieces = hand_on(result.astype(jnp.bfloat16), moves(section, -1))

    grad_up, grad_down, gain_part = run_final(
        0, place, pieces, grads, stash, norm_gain, up, down
    )
    grad_gain = sum_over_dp(gain_part.reshape(1, width))
    return (grad_up.T[None], grad_down.T[None], grad_gain)


def solution(mesh):
    placed = (
        P(None, "dp", None),
        P(None, "dp", None),
        P("section", None, "dp"),
        P("section", None, "dp"),
        P("section", None),
    )
    return jax.shard_map(
        body,
        mesh=mesh,
        in_specs=placed,
        out_specs=(P("section", None, "dp"), P("section", None, "dp"), P("section", None)),
        check_vma=False,
    )
```

```python
import functools
import math

import jax
import jax.numpy as jnp
from jax import lax
from jax.experimental import pallas as pl
from jax.experimental.pallas import tpu as pltpu
from jax.sharding import PartitionSpec as P

D = 6656
HIDDEN_SIZE = 8960


EPSILON = 1e-05
GELU_SCALE = 0.7978845608028654
GELU_CUBIC = 0.044715

INV_WIDTH = 1.0 / math.sqrt(D)
INV_HIDDEN = 1.0 / math.sqrt(HIDDEN_SIZE)

AXES = ("section", "dp")
QUARTERS = 4
LANES = 128
BLOCK = 128
SLOTS = 3
TOUCHES = 1
KERNEL_BYTES = 18 * 1024 * 1024
STREAM_BYTES = 32 * 1024 * 1024

ANY = pl.BlockSpec(memory_space=pl.ANY)
VMEM = pl.BlockSpec(memory_space=pltpu.VMEM)
SMEM = pl.BlockSpec(memory_space=pltpu.SMEM)


def gelu_value(preact):
    inner = GELU_SCALE * (preact + GELU_CUBIC * preact * preact * preact)
    return 0.5 * preact * (1.0 + jnp.tanh(inner))


def gelu_slope(preact):
    inner = GELU_SCALE * (preact + GELU_CUBIC * preact * preact * preact)
    tangent = jnp.tanh(inner)
    return 0.5 * (1.0 + tangent) + 0.5 * preact * (1.0 - tangent * tangent) * GELU_SCALE * (
        1.0 + 3.0 * GELU_CUBIC * preact * preact
    )


def outer_rows(left, right):
    return lax.dot_general(
        left, right, (((0,), (0,)), ((), ())), preferred_element_type=jnp.float32
    )


def across_hidden(left, right):
    return lax.dot_general(
        left, right, (((1,), (1,)), ((), ())), preferred_element_type=jnp.float32
    )


def plain_product(left, right):
    return jnp.dot(left, right, preferred_element_type=jnp.float32)


FAR, NEAR = (3, 2, 1), (0,)


def quarter(place_ref, k, width):
    start = (place_ref[1] ^ k) * width
    return pl.ds(pl.multiple_of(start, LANES), width)


def read_quarter(place_ref, piece_refs, k, width):
    if len(piece_refs) == 1:
        return piece_refs[0][:, quarter(place_ref, k, width)]
    return piece_refs[k][...]


def write_out(copies):
    for copy in copies:
        copy.start()
    for copy in copies:
        copy.wait()


def quarter_copies(place_ref, piece_refs, target, sems, width):
    if len(piece_refs) == 1:
        return [pltpu.make_async_copy(piece_refs[0], target, sems.at[0])]
    return [
        pltpu.make_async_copy(ref, target.at[:, quarter(place_ref, k, width)], sems.at[k])
        for k, ref in enumerate(piece_refs)
    ]


def stream(place_ref, source, buffer_ref, sems, quarters):
    width = buffer_ref.shape[2]
    copies = {
        k: pltpu.make_async_copy(
            source.at[:, quarter(place_ref, k, width)], buffer_ref.at[at], sems.at[at]
        )
        for at, k in enumerate(quarters)
    }
    for copy in copies.values():
        copy.start()

    def read(k):
        copies[k].wait()
        return buffer_ref[list(quarters).index(k)]

    return read


def lying(place_ref, weight_ref):
    width = weight_ref.shape[1] // QUARTERS
    return lambda k: weight_ref[:, quarter(place_ref, k, width)]


def contract_width(weight, rows):
    total = None
    for k in range(QUARTERS):
        part = across_hidden(weight(k), rows(k))
        total = part if total is None else total + part
    return total.T


def enter_section(place_ref, piece_refs, gain_ref, up, width):
    squares = 0.0
    for k in range(QUARTERS):
        values = read_quarter(place_ref, piece_refs, k, width).astype(jnp.float32)
        squares = squares + jnp.sum(values * values, axis=-1, keepdims=True)
    norm_scale = lax.rsqrt(squares * (1.0 / (QUARTERS * width)) + EPSILON)

    def read(k):
        normed = read_quarter(place_ref, piece_refs, k, width).astype(jnp.float32) * norm_scale
        return (normed * gain_ref[:, quarter(place_ref, k, width)]).astype(jnp.bfloat16)

    return (norm_scale, contract_width(up, read) * INV_WIDTH)


def hidden_part(part_refs, quarters, hidden, down):
    for at, k in enumerate(quarters):
        part_refs[at][...] = (plain_product(hidden, down(k)) * INV_HIDDEN).astype(jnp.bfloat16)


def scaled_part(part_refs, quarters, preact_grad, along, rows_of, up, gain_ref):
    width = gain_ref.shape[2]
    for at, k in enumerate(quarters):
        part = plain_product(preact_grad, up(k)) * INV_WIDTH
        gain_ref[at] = jnp.sum(part * rows_of(k), axis=0, keepdims=True)
        part_refs[at][:, :width] = part.astype(jnp.bfloat16)
        part_refs[at][:, width:] = along


def along_rows(preact_grad, preact):
    total = jnp.sum(preact_grad.astype(jnp.float32) * preact, axis=-1, keepdims=True)
    return jnp.broadcast_to(total.astype(jnp.bfloat16), (total.shape[0], LANES))


def gain_copies(place_ref, gain_ref, target, quarters, sems):
    return [
        pltpu.make_async_copy(gain_ref.at[at], target.at[place_ref[1] ^ k], sems.at[at])
        for at, k in enumerate(quarters)
    ]


def forward_far(section, pieces, with_stash, streams, place_ref, *refs):
    piece_refs, refs = refs[:pieces], refs[pieces:]
    gain_ref, up_ref, down_ref = refs[:3]
    refs = refs[3 + (4 if with_stash else 0) :]
    part_refs, hidden_ref, refs = refs[:3], refs[3], refs[4:]
    rows_out, scale_out, preact_out, own_out, scale_ref, preact_ref, own_ref, sems = refs[:8]
    width = own_ref.shape[1]

    @pl.when(place_ref[0] == section)
    def _():
        if streams:
            up_buffer, down_buffer, up_sems, down_sems = refs[8:]
            up = stream(place_ref, up_ref, up_buffer, up_sems, range(QUARTERS))
            down = stream(place_ref, down_ref, down_buffer, down_sems, FAR)
        else:
            up, down = lying(place_ref, up_ref), lying(place_ref, down_ref)
        copies = quarter_copies(place_ref, piece_refs, rows_out, sems, width)
        for copy in copies:
            copy.start()
        norm_scale, preact = enter_section(
            place_ref, piece_refs, gain_ref, up, width
        )
        scale_ref[...] = jnp.broadcast_to(norm_scale, scale_ref.shape)
        preact_ref[...] = preact
        own_rows = read_quarter(place_ref, piece_refs, 0, width)
        own_ref[...] = own_rows.astype(jnp.float32) * norm_scale
        more = [
            pltpu.make_async_copy(scale_ref, scale_out, sems.at[QUARTERS]),
            pltpu.make_async_copy(preact_ref, preact_out, sems.at[QUARTERS + 1]),
            pltpu.make_async_copy(own_ref, own_out, sems.at[QUARTERS + 2]),
        ]
        for copy in more:
            copy.start()
        hidden = gelu_value(preact).astype(jnp.bfloat16)
        hidden_ref[...] = hidden
        hidden_part(part_refs, FAR, hidden, down)
        for copy in copies + more:
            copy.wait()


def forward_near(section, streams, place_ref, hidden_ref, down_ref, part_ref, *refs):
    @pl.when(place_ref[0] == section)
    def _():
        if streams:
            down = stream(place_ref, down_ref, *refs, NEAR)
        else:
            down = lying(place_ref, down_ref)
        hidden_part([part_ref], NEAR, hidden_ref[...], down)


def early_grad(
    section, place_ref, rows_ref, down_ref, grad_out, hidden_grad_out, total_ref, sems
):
    width = rows_ref.shape[1] // QUARTERS

    @pl.when(place_ref[0] == section)
    def _():
        first = pltpu.make_async_copy(rows_ref, grad_out, sems.at[0])
        first.start()
        total_ref[...] = INV_HIDDEN * contract_width(
            lying(place_ref, down_ref),
            lambda k: read_quarter(place_ref, [rows_ref], k, width),
        )
        second = pltpu.make_async_copy(total_ref, hidden_grad_out, sems.at[1])
        second.start()
        first.wait()
        second.wait()


def last_far(section, place_ref, *refs):
    piece_refs, refs = refs[:QUARTERS], refs[QUARTERS:]
    hidden_grad_ref, gain_row_ref, up_ref = refs[:3]
    refs = refs[7:]
    part_refs, preact_grad_ref, along_ref, refs = refs[:3], refs[3], refs[4], refs[5:]
    rows_out, scale_out, preact_out, own_out, preact_grad_out, gain_out = refs[:6]
    scale_ref, preact_ref, own_ref, gain_ref, sems = refs[6:]
    width = gain_ref.shape[2]
    up = lying(place_ref, up_ref)

    @pl.when(place_ref[0] == section)
    def _():
        copies = quarter_copies(place_ref, piece_refs, rows_out, sems, width)
        for copy in copies:
            copy.start()
        norm_scale, preact = enter_section(place_ref, piece_refs, gain_row_ref, up, width)
        preact_grad = (hidden_grad_ref[...] * gelu_slope(preact)).astype(jnp.bfloat16)
        along = along_rows(preact_grad, preact)
        scale_ref[...] = jnp.broadcast_to(norm_scale, scale_ref.shape)
        preact_ref[...] = preact
        preact_grad_ref[...] = preact_grad
        along_ref[...] = along
        own_ref[...] = piece_refs[0][...].astype(jnp.float32) * norm_scale
        more = [
            pltpu.make_async_copy(scale_ref, scale_out, sems.at[QUARTERS]),
            pltpu.make_async_copy(preact_ref, preact_out, sems.at[QUARTERS + 1]),
            pltpu.make_async_copy(own_ref, own_out, sems.at[QUARTERS + 2]),
            pltpu.make_async_copy(preact_grad_ref, preact_grad_out, sems.at[QUARTERS + 3]),
        ]
        for copy in more:
            copy.start()

        def rows_of(k):
            return piece_refs[k][...].astype(jnp.float32) * norm_scale

        scaled_part(part_refs, FAR, preact_grad, along, rows_of, up, gain_ref)
        write_out(gain_copies(place_ref, gain_ref, gain_out, FAR, sems.at[pl.ds(QUARTERS + 4, len(FAR))]))
        for copy in copies + more:
            copy.wait()


def backward_far(section, place_ref, *refs):
    piece_refs, refs = refs[:QUARTERS], refs[QUARTERS:]
    rows_ref, scale_ref, preact_ref, up_ref, down_ref = refs[:5]
    refs = refs[8:]
    part_refs, preact_grad_ref, along_ref, refs = refs[:3], refs[3], refs[4], refs[5:]
    grad_out, preact_grad_out, gain_out, gain_ref, sems = refs
    width = gain_ref.shape[2]

    @pl.when(place_ref[0] == section)
    def _():
        copies = quarter_copies(place_ref, piece_refs, grad_out, sems, width)
        for copy in copies:
            copy.start()
        hidden_grad = INV_HIDDEN * contract_width(
            lying(place_ref, down_ref), lambda k: piece_refs[k][...]
        )
        preact = preact_ref[...]
        preact_grad = (hidden_grad * gelu_slope(preact)).astype(jnp.bfloat16)
        along = along_rows(preact_grad, preact)
        preact_grad_ref[...] = preact_grad
        along_ref[...] = along
        more = pltpu.make_async_copy(preact_grad_ref, preact_grad_out, sems.at[QUARTERS])
        more.start()
        norm_scale = scale_ref[:, :1]

        def rows_of(k):
            return rows_ref[:, quarter(place_ref, k, width)].astype(jnp.float32) * norm_scale

        up = lying(place_ref, up_ref)
        scaled_part(part_refs, FAR, preact_grad, along, rows_of, up, gain_ref)
        write_out(gain_copies(place_ref, gain_ref, gain_out, FAR, sems.at[pl.ds(QUARTERS + 1, len(FAR))]))
        for copy in copies + [more]:
            copy.wait()


def backward_near(
    section, place_ref, preact_grad_ref, along_ref, rows_ref, scale_ref, up_ref, gain_in,
    part_ref, gain_out, gain_ref, sems,
):
    del gain_in
    width = gain_ref.shape[2]

    @pl.when(place_ref[0] == section)
    def _():
        norm_scale = scale_ref[:, :1]

        def rows_of(k):
            return rows_ref[:, quarter(place_ref, k, width)].astype(jnp.float32) * norm_scale

        scaled_part(
            [part_ref], NEAR, preact_grad_ref[...], along_ref[...],
            rows_of, lying(place_ref, up_ref), gain_ref,
        )
        write_out(gain_copies(place_ref, gain_ref, gain_out, NEAR, sems))


def hidden_blocks(local):
    return [(start, min(BLOCK, local - start)) for start in range(0, local, BLOCK)]


def outer_blocks(left_ref, right_ref, factor, blocks, target, buffer_ref, sems, beside):
    copies = []
    for i, (start, size) in enumerate(blocks):
        slot = i % SLOTS
        if i >= SLOTS:
            copies[i - SLOTS].wait()
        value = outer_rows(left_ref[:, start : start + size], right_ref[...])
        buffer_ref[slot, :size] = value * factor
        copy = pltpu.make_async_copy(
            buffer_ref.at[slot, pl.ds(0, size)], target.at[pl.ds(start, size)], sems.at[slot]
        )
        copy.start()
        copies.append(copy)
        if i < len(beside):
            beside[i]()
    for run in beside[len(blocks) :]:
        run()
    for copy in copies[-SLOTS:]:
        copy.wait()


def final_down(section, place_ref, *refs):
    piece_refs, refs = refs[:QUARTERS], refs[QUARTERS:]
    grad_in, preact_grad_in, gain_in, rows_ref, scale_ref, preact_ref, gain_row_ref = refs[:7]
    up_ref, down_ref = refs[7:9]
    target, preact_grad_ref, gain_ref, scaled_ref = refs[9:13]
    grad_ref, hidden_ref, hidden_grad_ref, buffer_ref, sems = refs[13:]
    width = gain_ref.shape[2]
    up, down = lying(place_ref, up_ref), lying(place_ref, down_ref)
    active = place_ref[0] == section

    @pl.when(active)
    def _():
        for k in range(QUARTERS):
            grad_ref[:, quarter(place_ref, k, width)] = piece_refs[k][...]

    @pl.when(jnp.logical_not(active))
    def _():
        grad_ref[...] = grad_in[...]
        preact_grad_ref[...] = preact_grad_in[...]
        gain_ref[...] = gain_in[...]

    norm_scale = scale_ref[:, :1]
    hidden_ref[...] = gelu_value(preact_ref[...]).astype(jnp.bfloat16)

    def add_grad(k):
        @pl.when(active)
        def _():
            part = across_hidden(down(k), piece_refs[k][...])
            hidden_grad_ref[...] = part if k == 0 else hidden_grad_ref[...] + part

    def finish_grad():
        @pl.when(active)
        def _():
            hidden_grad = hidden_grad_ref[...].T * INV_HIDDEN
            preact_grad_ref[...] = (hidden_grad * gelu_slope(preact_ref[...])).astype(jnp.bfloat16)

    def add_gain(k):
        @pl.when(active)
        def _():
            part = plain_product(preact_grad_ref[...], up(k)) * INV_WIDTH
            rows = rows_ref[:, quarter(place_ref, k, width)]
            normed = rows.astype(jnp.float32) * norm_scale
            gain_ref[place_ref[1] ^ k] = jnp.sum(part * normed, axis=0, keepdims=True)

    def scale_rows():
        normed = rows_ref[...].astype(jnp.float32) * norm_scale
        scaled_ref[...] = (normed * gain_row_ref[...]).astype(jnp.bfloat16)

    beside = [functools.partial(add_grad, k) for k in range(QUARTERS)]
    beside += [finish_grad] + [functools.partial(add_gain, k) for k in range(QUARTERS)]
    beside += [scale_rows]
    blocks = hidden_blocks(target.shape[0])
    outer_blocks(hidden_ref, grad_ref, INV_HIDDEN, blocks, target, buffer_ref, sems, beside)


def final_up(blocks, preact_grad_ref, scaled_ref, *refs):
    target, buffer_ref, sems = refs[-3:]
    outer_blocks(preact_grad_ref, scaled_ref, INV_WIDTH, blocks, target, buffer_ref, sems, [])


def struct(*shape, dtype=jnp.bfloat16):
    return jax.ShapeDtypeStruct(shape, dtype)


def call(kernel, inputs, specs, outputs, out_specs, scratch, aliases, limit, products):
    flops = sum(2 * a * b * c for a, b, c in products)
    return pl.pallas_call(
        kernel,
        out_shape=outputs,
        in_specs=specs,
        out_specs=out_specs,
        scratch_shapes=scratch,
        input_output_aliases=aliases,
        cost_estimate=pl.CostEstimate(
            flops=flops,
            bytes_accessed=sum(2 * b * c for _, b, c in products),
            transcendentals=0,
        ),
        compiler_params=pltpu.CompilerParams(vmem_limit_bytes=limit),
    )(*inputs)


def touch(place_ref, after_ref, up_ref, down_ref, place_out):
    del after_ref, up_ref, down_ref
    for i in range(place_ref.shape[0]):
        place_out[i] = place_ref[i]


def run_touch(place, after, up, down):
    return pl.pallas_call(
        touch,
        out_shape=jax.ShapeDtypeStruct(place.shape, place.dtype),
        in_specs=[SMEM, ANY, VMEM, VMEM],
        out_specs=SMEM,
        compiler_params=pltpu.CompilerParams(vmem_limit_bytes=KERNEL_BYTES),
    )(place, after, up, down)


def lay_rows(place_ref, *refs):
    piece_refs, gain_ref = refs[:QUARTERS], refs[QUARTERS]
    rows_ref, own_ref, own_gain_ref = refs[QUARTERS + 1 :]
    inner, micro, tokens, width = piece_refs[0].shape
    for outer in range(QUARTERS):
        for k, ref in enumerate(piece_refs):

            @pl.when((place_ref[1] ^ k) == outer)
            def _(outer=outer, ref=ref):
                for i in range(inner):
                    for j in range(micro):
                        start = ((outer * inner + i) * micro + j) * tokens
                        rows_ref[start : start + tokens, :] = ref[place_ref[2] ^ i, j]

    own = quarter(place_ref, 0, width // QUARTERS)
    own_ref[...] = rows_ref[:, own]
    own_gain_ref[...] = jnp.broadcast_to(gain_ref[:, own], own_gain_ref.shape)


def run_lay_rows(place, pieces, gain):
    rows, width = QUARTERS * pieces[0].size // gain.size, gain.shape[1]
    return call(
        lay_rows,
        [place, *pieces, gain],
        [SMEM] + [VMEM] * (QUARTERS + 1),
        [
            struct(rows, width),
            struct(rows, width // QUARTERS),
            struct(rows, width // QUARTERS, dtype=jnp.float32),
        ],
        [VMEM] * 3,
        [],
        {},
        KERNEL_BYTES,
        [],
    )


def weight_specs(streams):
    return [ANY if streams else VMEM]


def weight_buffers(weight, quarters):
    shape = (weight.shape[0], weight.shape[1] // QUARTERS)
    return [pltpu.VMEM((count, *shape), weight.dtype) for count in quarters] + [
        pltpu.SemaphoreType.DMA((count,)) for count in quarters
    ]


def run_forward_far(section, place, pieces, gain, up, down, stash, streams):
    rows, (local, width) = pieces[0].shape[0], up.shape
    part = struct(rows, width // QUARTERS)
    first = 4 + len(pieces)
    result = call(
        functools.partial(forward_far, section, len(pieces), bool(stash), streams),
        [place, *pieces, gain, up, down, *stash],
        [SMEM] + [VMEM] * (len(pieces) + 1) + weight_specs(streams) * 2 + [ANY] * len(stash),
        [
            *[part] * len(FAR),
            struct(rows, local),
            struct(rows, width),
            struct(rows, LANES, dtype=jnp.float32),
            struct(rows, local, dtype=jnp.float32),
            struct(rows, width // QUARTERS, dtype=jnp.float32),
        ],
        [VMEM] * 4 + [ANY] * 4,
        [
            pltpu.VMEM((rows, LANES), jnp.float32),
            pltpu.VMEM((rows, local), jnp.float32),
            pltpu.VMEM((rows, width // QUARTERS), jnp.float32),
            pltpu.SemaphoreType.DMA((QUARTERS + 3,)),
            *(weight_buffers(up, [QUARTERS, len(FAR)]) if streams else []),
        ],
        {first + i: 4 + i for i in range(len(stash))},
        STREAM_BYTES if streams else KERNEL_BYTES,
        [(rows, width, local), (rows, local, 3 * width // 4)],
    )
    return (result[:3], result[3], result[4:])


def run_forward_near(section, place, hidden, down, streams):
    rows, (local, width) = hidden.shape[0], down.shape
    part = struct(rows, width // QUARTERS)
    return call(
        functools.partial(forward_near, section, streams),
        [place, hidden, down],
        [SMEM, VMEM, *weight_specs(streams)],
        [part],
        [VMEM],
        weight_buffers(down, [len(NEAR)]) if streams else [],
        {},
        KERNEL_BYTES,
        [(rows, local, width // 4)],
    )


def run_early_grad(section, place, entered, down):
    rows, (local, width) = entered.shape[0], down.shape
    return call(
        functools.partial(early_grad, section),
        [place, entered, down],
        [SMEM, VMEM, VMEM],
        [struct(rows, width), struct(rows, local, dtype=jnp.float32)],
        [ANY] * 2,
        [pltpu.VMEM((rows, local), jnp.float32), pltpu.SemaphoreType.DMA((2,))],
        {},
        KERNEL_BYTES,
        [(rows, width, local)],
    )


def run_last_far(section, place, pieces, hidden_grad, gain, up, stash):
    rows, (local, width) = pieces[0].shape[0], up.shape
    part = struct(rows, width // QUARTERS + LANES)
    result = call(
        functools.partial(last_far, section),
        [place, *pieces, hidden_grad, gain, up, *stash],
        [SMEM] + [VMEM] * (QUARTERS + 3) + [ANY] * 4,
        [
            *[part] * len(FAR),
            struct(rows, local),
            struct(rows, LANES),
            struct(rows, width),
            struct(rows, LANES, dtype=jnp.float32),
            struct(rows, local, dtype=jnp.float32),
            struct(rows, width // QUARTERS, dtype=jnp.float32),
            struct(rows, local),
            struct(QUARTERS, 1, width // QUARTERS, dtype=jnp.float32),
        ],
        [VMEM] * 5 + [ANY] * 6,
        [
            pltpu.VMEM((rows, LANES), jnp.float32),
            pltpu.VMEM((rows, local), jnp.float32),
            pltpu.VMEM((rows, width // QUARTERS), jnp.float32),
            pltpu.VMEM((len(FAR), 1, width // QUARTERS), jnp.float32),
            pltpu.SemaphoreType.DMA((QUARTERS + 7,)),
        ],
        {QUARTERS + 4 + i: 5 + i for i in range(4)},
        KERNEL_BYTES,
        [(rows, width, local), (rows, local, 3 * width // 4)],
    )
    return (result[:3], result[3:5], result[5:9], result[9:])


def run_backward_far(section, place, pieces, kept, up, down, grads):
    rows, (local, width) = pieces[0].shape[0], up.shape
    part = struct(rows, width // QUARTERS + LANES)
    result = call(
        functools.partial(backward_far, section),
        [place, *pieces, *kept, up, down, *grads],
        [SMEM] + [VMEM] * (QUARTERS + 5) + [ANY] * 3,
        [
            *[part] * len(FAR),
            struct(rows, local),
            struct(rows, LANES),
            struct(rows, width),
            struct(rows, local),
            struct(QUARTERS, 1, width // QUARTERS, dtype=jnp.float32),
        ],
        [VMEM] * 5 + [ANY] * 3,
        [
            pltpu.VMEM((len(FAR), 1, width // QUARTERS), jnp.float32),
            pltpu.SemaphoreType.DMA((QUARTERS + 4,)),
        ],
        {QUARTERS + 6 + i: 5 + i for i in range(3)},
        KERNEL_BYTES,
        [(rows, width, local), (rows, local, 3 * width // 4)],
    )
    return (result[:3], result[3:5], result[5:])


def run_backward_near(section, place, passed, kept, up, gain_part):
    rows, (local, width) = kept[0].shape[0], up.shape
    part = struct(rows, width // QUARTERS + LANES)
    result = call(
        functools.partial(backward_near, section),
        [place, *passed, kept[0], kept[1], up, gain_part],
        [SMEM] + [VMEM] * 5 + [ANY],
        [part, struct(*gain_part.shape, dtype=jnp.float32)],
        [VMEM, ANY],
        [
            pltpu.VMEM((len(NEAR), 1, width // QUARTERS), jnp.float32),
            pltpu.SemaphoreType.DMA((len(NEAR),)),
        ],
        {6: 1},
        KERNEL_BYTES,
        [(rows, local, width // 4)],
    )
    return result


def run_final(section, place, pieces, grads, kept, gain, up, down):
    rows, (local, width) = pieces[0].shape[0], up.shape
    buffers = [
        pltpu.VMEM((SLOTS, BLOCK, width), jnp.float32),
        pltpu.SemaphoreType.DMA((SLOTS,)),
    ]
    grad_down, preact_grad, gain_part, scaled = call(
        functools.partial(final_down, section),
        [place, *pieces, *grads, *kept, gain, up, down],
        [SMEM] + [VMEM] * (QUARTERS + 9),
        [
            struct(local, width, dtype=jnp.float32),
            struct(rows, local),
            struct(*grads[2].shape, dtype=jnp.float32),
            struct(rows, width),
        ],
        [ANY] + [VMEM] * 3,
        [
            pltpu.VMEM((rows, width), jnp.bfloat16),
            pltpu.VMEM((rows, local), jnp.bfloat16),
            pltpu.VMEM((local, rows), jnp.float32),
            *buffers,
        ],
        {},
        KERNEL_BYTES,
        [(rows, width, local)] * 2 + [(local, rows, width)],
    )
    blocks = hidden_blocks(local)
    half = (len(blocks) + 1) // 2
    grad_up = ()
    for taken in (blocks[:half], blocks[half:]):
        grad_up = call(
            functools.partial(final_up, taken),
            [preact_grad, scaled, *grad_up],
            [VMEM, VMEM] + [ANY] * len(grad_up),
            [struct(local, width, dtype=jnp.float32)],
            [ANY],
            buffers,
            {2: 0} if grad_up else {},
            KERNEL_BYTES,
            [(local // 2, rows, width)],
        )
    return (grad_up[0], grad_down, gain_part)


def within(sections, flip):
    count = lax.axis_size("dp")
    return [(s * count + r, s * count + (r ^ flip)) for s in sections for r in range(count)]


def between(moves, flip):
    count = lax.axis_size("dp")
    return [(s * count + r, t * count + (r ^ flip)) for s, t in moves for r in range(count)]


def send_quarter(part, sections, k):
    return lax.ppermute(part, AXES, within(sections, k * (lax.axis_size("dp") // QUARTERS)))


def sum_quarters(own, arrived, sections):
    inner = lax.axis_size("dp") // QUARTERS
    total = own.astype(jnp.float32)
    for value in arrived:
        total = total + value.astype(jnp.float32)
    flip = 1
    while flip < inner:
        rounded = total.astype(jnp.bfloat16)
        other = lax.ppermute(rounded, AXES, within(sections, flip))
        total = rounded.astype(jnp.float32) + other.astype(jnp.float32)
        flip *= 2
    return total


def hand_on(own, moves):
    inner = lax.axis_size("dp") // QUARTERS
    pieces = {
        k: lax.ppermute(own, AXES, between(moves, k * inner)) for k in range(QUARTERS - 1, -1, -1)
    }
    return [pieces[k] for k in range(QUARTERS)]


def gather_chunks(chunk, sections):
    inner = lax.axis_size("dp") // QUARTERS
    held = chunk
    flip = 1
    while flip < inner:
        other = lax.ppermute(held, AXES, within(sections, flip))
        held = jnp.concatenate([held, other], axis=0)
        flip *= 2
    pieces = {k: send_quarter(held, sections, k) for k in range(QUARTERS - 1, 0, -1)}
    return [held] + [pieces[k] for k in range(1, QUARTERS)]


def sum_over_dp(value):
    flip = 1
    while flip < lax.axis_size("dp"):
        value = value + lax.ppermute(
            value, "dp", [(r, r ^ flip) for r in range(lax.axis_size("dp"))]
        )
        flip *= 2
    return value


def body(section_input, out_cotangent, up_weight, down_weight, norm_gain):
    section_count = lax.axis_size("section")
    section_pos = lax.axis_index("section")
    count = lax.axis_size("dp")
    position = lax.axis_index("dp")
    width = up_weight.shape[1]
    quarter_width = width // QUARTERS
    last = section_count - 1

    def alike(section):
        return [s for s in range(section_count) if s % 2 == section % 2]

    def moves(section, step):
        return [(s, s + step) for s in alike(section) if 0 <= s + step < section_count]

    inner = count // QUARTERS
    place = jnp.stack([section_pos, position // inner, position % inner]).astype(jnp.int32)
    chunk = jnp.where(section_pos == last, out_cotangent, section_input)
    chunk, place = lax.optimization_barrier((chunk[None], place))
    held = gather_chunks(chunk, [0, last])
    streamed_up, streamed_down = (
        pltpu.with_memory_space_constraint(weight[0].T, pltpu.HBM)
        for weight in (up_weight, down_weight)
    )
    up, down = (
        pltpu.with_memory_space_constraint(weight[0].T, pltpu.VMEM)
        for weight in (up_weight, down_weight)
    )
    place = run_touch(place, held[0], up, down)
    entered, own_entered, own_gain = run_lay_rows(place, held, norm_gain)

    pieces, stash, own = [entered], (), own_entered
    for section in range(last):
        here = alike(section)
        streams = section == 0
        weights = (streamed_up, streamed_down) if streams else (up, down)
        far, hidden, stash = run_forward_far(
            section, place, pieces, norm_gain, *weights, stash, streams
        )
        arrived = [send_quarter(part, here, k) for part, k in zip(far, FAR)]
        (near,) = run_forward_near(section, place, hidden, weights[1], streams)
        result = own.astype(jnp.float32) + sum_quarters(near, arrived, here)
        result = result.astype(jnp.bfloat16)
        pieces = hand_on(result, moves(section, 1))
        own = pieces[0]
        if section == 0:
            for _ in range(TOUCHES):
                place = run_touch(place, result, up, down)
            grad_rows, early = run_early_grad(last, place, entered, down)

    for section in range(last, 0, -1):
        here = alike(section)
        if section == last:
            far, passed, stash, grads = run_last_far(
                last, place, pieces, early, norm_gain, up, stash
            )
            *stash, own_normed = stash
            own_scale = stash[1][:, :1]
            grads = [grad_rows, *grads]
            own = own_entered
        else:
            far, passed, grads = run_backward_far(section, place, pieces, stash, up, down, grads)
            own = pieces[0]
        arrived = [send_quarter(part, here, k) for part, k in zip(far, FAR)]
        near, gain_part = run_backward_near(section, place, passed, stash, up, grads[2])
        grads = [grads[0], grads[1], gain_part]
        total = sum_quarters(near, arrived, here)
        along = total[:, quarter_width : quarter_width + 1] * (1.0 / width)
        normed_grad = total[:, :quarter_width] * own_gain
        result = own.astype(jnp.float32) + own_scale * (normed_grad - own_normed * along)
        pieces = hand_on(result.astype(jnp.bfloat16), moves(section, -1))

    grad_up, grad_down, gain_part = run_final(
        0, place, pieces, grads, stash, norm_gain, up, down
    )
    grad_gain = sum_over_dp(gain_part.reshape(1, width))
    return (grad_up.T[None], grad_down.T[None], grad_gain)


def solution(mesh):
    placed = (
        P(None, "dp", None),
        P(None, "dp", None),
        P("section", None, "dp"),
        P("section", None, "dp"),
        P("section", None),
    )
    return jax.shard_map(
        body,
        mesh=mesh,
        in_specs=placed,
        out_specs=(P("section", None, "dp"), P("section", None, "dp"), P("section", None)),
        check_vma=False,
    )
```

```python
import functools
import math

import jax
import jax.numpy as jnp
from jax import lax
from jax.experimental import pallas as pl
from jax.experimental.pallas import tpu as pltpu
from jax.sharding import PartitionSpec as P

D = 6656
HIDDEN_SIZE = 8960


EPSILON = 1e-05
GELU_SCALE = 0.7978845608028654
GELU_CUBIC = 0.044715

INV_WIDTH = 1.0 / math.sqrt(D)
INV_HIDDEN = 1.0 / math.sqrt(HIDDEN_SIZE)

AXES = ("section", "dp")
QUARTERS = 4
LANES = 128
BLOCK = 128
SLOTS = 3
TOUCHES = 1
KERNEL_BYTES = 18 * 1024 * 1024
STREAM_BYTES = 32 * 1024 * 1024

ANY = pl.BlockSpec(memory_space=pl.ANY)
VMEM = pl.BlockSpec(memory_space=pltpu.VMEM)
SMEM = pl.BlockSpec(memory_space=pltpu.SMEM)


def gelu_value(preact):
    inner = GELU_SCALE * (preact + GELU_CUBIC * preact * preact * preact)
    return 0.5 * preact * (1.0 + jnp.tanh(inner))


def gelu_slope(preact):
    inner = GELU_SCALE * (preact + GELU_CUBIC * preact * preact * preact)
    tangent = jnp.tanh(inner)
    return 0.5 * (1.0 + tangent) + 0.5 * preact * (1.0 - tangent * tangent) * GELU_SCALE * (
        1.0 + 3.0 * GELU_CUBIC * preact * preact
    )


def outer_rows(left, right):
    return lax.dot_general(
        left, right, (((0,), (0,)), ((), ())), preferred_element_type=jnp.float32
    )


def across_hidden(left, right):
    return lax.dot_general(
        left, right, (((1,), (1,)), ((), ())), preferred_element_type=jnp.float32
    )


def plain_product(left, right):
    return jnp.dot(left, right, preferred_element_type=jnp.float32)


FAR, NEAR = (1, 3), (2, 0)


def quarter(place_ref, k, width):
    start = (place_ref[1] ^ k) * width
    return pl.ds(pl.multiple_of(start, LANES), width)


def read_quarter(place_ref, piece_refs, k, width):
    if len(piece_refs) == 1:
        return piece_refs[0][:, quarter(place_ref, k, width)]
    return piece_refs[k][...]


def write_out(copies):
    for copy in copies:
        copy.start()
    for copy in copies:
        copy.wait()


def quarter_copies(place_ref, piece_refs, target, sems, width):
    if len(piece_refs) == 1:
        return [pltpu.make_async_copy(piece_refs[0], target, sems.at[0])]
    return [
        pltpu.make_async_copy(ref, target.at[:, quarter(place_ref, k, width)], sems.at[k])
        for k, ref in enumerate(piece_refs)
    ]


def stream(place_ref, source, buffer_ref, sems, quarters):
    width = buffer_ref.shape[2]
    copies = {
        k: pltpu.make_async_copy(
            source.at[:, quarter(place_ref, k, width)], buffer_ref.at[at], sems.at[at]
        )
        for at, k in enumerate(quarters)
    }
    for copy in copies.values():
        copy.start()

    def read(k):
        copies[k].wait()
        return buffer_ref[list(quarters).index(k)]

    return read


def lying(place_ref, weight_ref):
    width = weight_ref.shape[1] // QUARTERS
    return lambda k: weight_ref[:, quarter(place_ref, k, width)]


def contract_width(weight, rows):
    total = None
    for k in range(QUARTERS):
        part = across_hidden(weight(k), rows(k))
        total = part if total is None else total + part
    return total.T


def enter_section(place_ref, piece_refs, gain_ref, up, width):
    squares = 0.0
    for k in range(QUARTERS):
        values = read_quarter(place_ref, piece_refs, k, width).astype(jnp.float32)
        squares = squares + jnp.sum(values * values, axis=-1, keepdims=True)
    norm_scale = lax.rsqrt(squares * (1.0 / (QUARTERS * width)) + EPSILON)

    def read(k):
        normed = read_quarter(place_ref, piece_refs, k, width).astype(jnp.float32) * norm_scale
        return (normed * gain_ref[:, quarter(place_ref, k, width)]).astype(jnp.bfloat16)

    return (norm_scale, contract_width(up, read) * INV_WIDTH)


def hidden_part(part_refs, quarters, hidden, down):
    for at, k in enumerate(quarters):
        part_refs[at][...] = (plain_product(hidden, down(k)) * INV_HIDDEN).astype(jnp.bfloat16)


def scaled_part(part_refs, quarters, preact_grad, along, rows_of, up, gain_ref):
    width = gain_ref.shape[2]
    for at, k in enumerate(quarters):
        part = plain_product(preact_grad, up(k)) * INV_WIDTH
        gain_ref[at] = jnp.sum(part * rows_of(k), axis=0, keepdims=True)
        part_refs[at][:, :width] = part.astype(jnp.bfloat16)
        part_refs[at][:, width:] = along


def segments(ref, count):
    width = ref.shape[1] // count
    return [ref.at[:, pl.ds(i * width, width)] for i in range(count)]


def along_rows(preact_grad, preact):
    total = jnp.sum(preact_grad.astype(jnp.float32) * preact, axis=-1, keepdims=True)
    return jnp.broadcast_to(total.astype(jnp.bfloat16), (total.shape[0], LANES))


def gain_copies(place_ref, gain_ref, target, quarters, sems):
    return [
        pltpu.make_async_copy(gain_ref.at[at], target.at[place_ref[1] ^ k], sems.at[at])
        for at, k in enumerate(quarters)
    ]


def forward_far(section, pieces, with_stash, streams, place_ref, *refs):
    piece_refs, refs = refs[:pieces], refs[pieces:]
    gain_ref, up_ref, down_ref = refs[:3]
    refs = refs[3 + (4 if with_stash else 0) :]
    part_refs, hidden_ref, refs = segments(refs[0], len(FAR)), refs[1], refs[2:]
    rows_out, scale_out, preact_out, own_out, scale_ref, preact_ref, own_ref, sems = refs[:8]
    width = own_ref.shape[1]

    @pl.when(place_ref[0] == section)
    def _():
        if streams:
            up_buffer, down_buffer, up_sems, down_sems = refs[8:]
            up = stream(place_ref, up_ref, up_buffer, up_sems, range(QUARTERS))
            down = stream(place_ref, down_ref, down_buffer, down_sems, FAR)
        else:
            up, down = lying(place_ref, up_ref), lying(place_ref, down_ref)
        copies = quarter_copies(place_ref, piece_refs, rows_out, sems, width)
        for copy in copies:
            copy.start()
        norm_scale, preact = enter_section(
            place_ref, piece_refs, gain_ref, up, width
        )
        scale_ref[...] = jnp.broadcast_to(norm_scale, scale_ref.shape)
        preact_ref[...] = preact
        own_rows = read_quarter(place_ref, piece_refs, 0, width)
        own_ref[...] = own_rows.astype(jnp.float32) * norm_scale
        more = [
            pltpu.make_async_copy(scale_ref, scale_out, sems.at[QUARTERS]),
            pltpu.make_async_copy(preact_ref, preact_out, sems.at[QUARTERS + 1]),
            pltpu.make_async_copy(own_ref, own_out, sems.at[QUARTERS + 2]),
        ]
        for copy in more:
            copy.start()
        hidden = gelu_value(preact).astype(jnp.bfloat16)
        hidden_ref[...] = hidden
        hidden_part(part_refs, FAR, hidden, down)
        for copy in copies + more:
            copy.wait()


def forward_near(section, streams, place_ref, hidden_ref, down_ref, cross_ref, own_ref, *refs):
    @pl.when(place_ref[0] == section)
    def _():
        if streams:
            down = stream(place_ref, down_ref, *refs, NEAR)
        else:
            down = lying(place_ref, down_ref)
        hidden_part([cross_ref, own_ref], NEAR, hidden_ref[...], down)


def early_grad(
    section, place_ref, rows_ref, down_ref, grad_out, hidden_grad_out, total_ref, sems
):
    width = rows_ref.shape[1] // QUARTERS

    @pl.when(place_ref[0] == section)
    def _():
        first = pltpu.make_async_copy(rows_ref, grad_out, sems.at[0])
        first.start()
        total_ref[...] = INV_HIDDEN * contract_width(
            lying(place_ref, down_ref),
            lambda k: read_quarter(place_ref, [rows_ref], k, width),
        )
        second = pltpu.make_async_copy(total_ref, hidden_grad_out, sems.at[1])
        second.start()
        first.wait()
        second.wait()


def last_far(section, place_ref, *refs):
    piece_refs, refs = refs[:QUARTERS], refs[QUARTERS:]
    hidden_grad_ref, gain_row_ref, up_ref = refs[:3]
    refs = refs[7:]
    part_refs, preact_grad_ref, along_ref = segments(refs[0], len(FAR)), refs[1], refs[2]
    refs = refs[3:]
    rows_out, scale_out, preact_out, own_out, preact_grad_out, gain_out = refs[:6]
    scale_ref, preact_ref, own_ref, gain_ref, sems = refs[6:]
    width = gain_ref.shape[2]
    up = lying(place_ref, up_ref)

    @pl.when(place_ref[0] == section)
    def _():
        copies = quarter_copies(place_ref, piece_refs, rows_out, sems, width)
        for copy in copies:
            copy.start()
        norm_scale, preact = enter_section(place_ref, piece_refs, gain_row_ref, up, width)
        preact_grad = (hidden_grad_ref[...] * gelu_slope(preact)).astype(jnp.bfloat16)
        along = along_rows(preact_grad, preact)
        scale_ref[...] = jnp.broadcast_to(norm_scale, scale_ref.shape)
        preact_ref[...] = preact
        preact_grad_ref[...] = preact_grad
        along_ref[...] = along
        own_ref[...] = piece_refs[0][...].astype(jnp.float32) * norm_scale
        more = [
            pltpu.make_async_copy(scale_ref, scale_out, sems.at[QUARTERS]),
            pltpu.make_async_copy(preact_ref, preact_out, sems.at[QUARTERS + 1]),
            pltpu.make_async_copy(own_ref, own_out, sems.at[QUARTERS + 2]),
            pltpu.make_async_copy(preact_grad_ref, preact_grad_out, sems.at[QUARTERS + 3]),
        ]
        for copy in more:
            copy.start()

        def rows_of(k):
            return piece_refs[k][...].astype(jnp.float32) * norm_scale

        scaled_part(part_refs, FAR, preact_grad, along, rows_of, up, gain_ref)
        write_out(gain_copies(place_ref, gain_ref, gain_out, FAR, sems.at[pl.ds(QUARTERS + 4, len(FAR))]))
        for copy in copies + more:
            copy.wait()


def backward_far(section, place_ref, *refs):
    piece_refs, refs = refs[:QUARTERS], refs[QUARTERS:]
    rows_ref, scale_ref, preact_ref, up_ref, down_ref = refs[:5]
    refs = refs[8:]
    part_refs, preact_grad_ref, along_ref = segments(refs[0], len(FAR)), refs[1], refs[2]
    refs = refs[3:]
    grad_out, preact_grad_out, gain_out, gain_ref, sems = refs
    width = gain_ref.shape[2]

    @pl.when(place_ref[0] == section)
    def _():
        copies = quarter_copies(place_ref, piece_refs, grad_out, sems, width)
        for copy in copies:
            copy.start()
        hidden_grad = INV_HIDDEN * contract_width(
            lying(place_ref, down_ref), lambda k: piece_refs[k][...]
        )
        preact = preact_ref[...]
        preact_grad = (hidden_grad * gelu_slope(preact)).astype(jnp.bfloat16)
        along = along_rows(preact_grad, preact)
        preact_grad_ref[...] = preact_grad
        along_ref[...] = along
        more = pltpu.make_async_copy(preact_grad_ref, preact_grad_out, sems.at[QUARTERS])
        more.start()
        norm_scale = scale_ref[:, :1]

        def rows_of(k):
            return rows_ref[:, quarter(place_ref, k, width)].astype(jnp.float32) * norm_scale

        up = lying(place_ref, up_ref)
        scaled_part(part_refs, FAR, preact_grad, along, rows_of, up, gain_ref)
        write_out(gain_copies(place_ref, gain_ref, gain_out, FAR, sems.at[pl.ds(QUARTERS + 1, len(FAR))]))
        for copy in copies + [more]:
            copy.wait()


def backward_near(
    section, place_ref, preact_grad_ref, along_ref, rows_ref, scale_ref, up_ref, gain_in,
    cross_ref, own_ref, gain_out, gain_ref, sems,
):
    del gain_in
    width = gain_ref.shape[2]

    @pl.when(place_ref[0] == section)
    def _():
        norm_scale = scale_ref[:, :1]

        def rows_of(k):
            return rows_ref[:, quarter(place_ref, k, width)].astype(jnp.float32) * norm_scale

        scaled_part(
            [cross_ref, own_ref], NEAR, preact_grad_ref[...], along_ref[...],
            rows_of, lying(place_ref, up_ref), gain_ref,
        )
        write_out(gain_copies(place_ref, gain_ref, gain_out, NEAR, sems))


def hidden_blocks(local):
    return [(start, min(BLOCK, local - start)) for start in range(0, local, BLOCK)]


def outer_blocks(left_ref, right_ref, factor, blocks, target, buffer_ref, sems, beside):
    copies = []
    for i, (start, size) in enumerate(blocks):
        slot = i % SLOTS
        if i >= SLOTS:
            copies[i - SLOTS].wait()
        value = outer_rows(left_ref[:, start : start + size], right_ref[...])
        buffer_ref[slot, :size] = value * factor
        copy = pltpu.make_async_copy(
            buffer_ref.at[slot, pl.ds(0, size)], target.at[pl.ds(start, size)], sems.at[slot]
        )
        copy.start()
        copies.append(copy)
        if i < len(beside):
            beside[i]()
    for run in beside[len(blocks) :]:
        run()
    for copy in copies[-SLOTS:]:
        copy.wait()


def final_down(section, place_ref, *refs):
    piece_refs, refs = refs[:QUARTERS], refs[QUARTERS:]
    grad_in, preact_grad_in, gain_in, rows_ref, scale_ref, preact_ref, gain_row_ref = refs[:7]
    up_ref, down_ref = refs[7:9]
    target, preact_grad_ref, gain_ref, scaled_ref = refs[9:13]
    grad_ref, hidden_ref, hidden_grad_ref, buffer_ref, sems = refs[13:]
    width = gain_ref.shape[2]
    up, down = lying(place_ref, up_ref), lying(place_ref, down_ref)
    active = place_ref[0] == section

    @pl.when(active)
    def _():
        for k in range(QUARTERS):
            grad_ref[:, quarter(place_ref, k, width)] = piece_refs[k][...]

    @pl.when(jnp.logical_not(active))
    def _():
        grad_ref[...] = grad_in[...]
        preact_grad_ref[...] = preact_grad_in[...]
        gain_ref[...] = gain_in[...]

    norm_scale = scale_ref[:, :1]
    hidden_ref[...] = gelu_value(preact_ref[...]).astype(jnp.bfloat16)

    def add_grad(k):
        @pl.when(active)
        def _():
            part = across_hidden(down(k), piece_refs[k][...])
            hidden_grad_ref[...] = part if k == 0 else hidden_grad_ref[...] + part

    def finish_grad():
        @pl.when(active)
        def _():
            hidden_grad = hidden_grad_ref[...].T * INV_HIDDEN
            preact_grad_ref[...] = (hidden_grad * gelu_slope(preact_ref[...])).astype(jnp.bfloat16)

    def add_gain(k):
        @pl.when(active)
        def _():
            part = plain_product(preact_grad_ref[...], up(k)) * INV_WIDTH
            rows = rows_ref[:, quarter(place_ref, k, width)]
            normed = rows.astype(jnp.float32) * norm_scale
            gain_ref[place_ref[1] ^ k] = jnp.sum(part * normed, axis=0, keepdims=True)

    def scale_rows():
        normed = rows_ref[...].astype(jnp.float32) * norm_scale
        scaled_ref[...] = (normed * gain_row_ref[...]).astype(jnp.bfloat16)

    beside = [functools.partial(add_grad, k) for k in range(QUARTERS)]
    beside += [finish_grad] + [functools.partial(add_gain, k) for k in range(QUARTERS)]
    beside += [scale_rows]
    blocks = hidden_blocks(target.shape[0])
    outer_blocks(hidden_ref, grad_ref, INV_HIDDEN, blocks, target, buffer_ref, sems, beside)


def final_up(blocks, preact_grad_ref, scaled_ref, *refs):
    target, buffer_ref, sems = refs[-3:]
    outer_blocks(preact_grad_ref, scaled_ref, INV_WIDTH, blocks, target, buffer_ref, sems, [])


def struct(*shape, dtype=jnp.bfloat16):
    return jax.ShapeDtypeStruct(shape, dtype)


def call(kernel, inputs, specs, outputs, out_specs, scratch, aliases, limit, products):
    flops = sum(2 * a * b * c for a, b, c in products)
    return pl.pallas_call(
        kernel,
        out_shape=outputs,
        in_specs=specs,
        out_specs=out_specs,
        scratch_shapes=scratch,
        input_output_aliases=aliases,
        cost_estimate=pl.CostEstimate(
            flops=flops,
            bytes_accessed=sum(2 * b * c for _, b, c in products),
            transcendentals=0,
        ),
        compiler_params=pltpu.CompilerParams(vmem_limit_bytes=limit),
    )(*inputs)


def touch(place_ref, after_ref, up_ref, down_ref, place_out):
    del after_ref, up_ref, down_ref
    for i in range(place_ref.shape[0]):
        place_out[i] = place_ref[i]


def run_touch(place, after, up, down):
    return pl.pallas_call(
        touch,
        out_shape=jax.ShapeDtypeStruct(place.shape, place.dtype),
        in_specs=[SMEM, ANY, VMEM, VMEM],
        out_specs=SMEM,
        compiler_params=pltpu.CompilerParams(vmem_limit_bytes=KERNEL_BYTES),
    )(place, after, up, down)


def lay_rows(place_ref, *refs):
    piece_refs, gain_ref = refs[:QUARTERS], refs[QUARTERS]
    rows_ref, own_ref, own_gain_ref = refs[QUARTERS + 1 :]
    inner, micro, tokens, width = piece_refs[0].shape
    for outer in range(QUARTERS):
        for k, ref in enumerate(piece_refs):

            @pl.when((place_ref[1] ^ k) == outer)
            def _(outer=outer, ref=ref):
                for i in range(inner):
                    for j in range(micro):
                        start = ((outer * inner + i) * micro + j) * tokens
                        rows_ref[start : start + tokens, :] = ref[place_ref[2] ^ i, j]

    own = quarter(place_ref, 0, width // QUARTERS)
    own_ref[...] = rows_ref[:, own]
    own_gain_ref[...] = jnp.broadcast_to(gain_ref[:, own], own_gain_ref.shape)


def run_lay_rows(place, pieces, gain):
    rows, width = QUARTERS * pieces[0].size // gain.size, gain.shape[1]
    return call(
        lay_rows,
        [place, *pieces, gain],
        [SMEM] + [VMEM] * (QUARTERS + 1),
        [
            struct(rows, width),
            struct(rows, width // QUARTERS),
            struct(rows, width // QUARTERS, dtype=jnp.float32),
        ],
        [VMEM] * 3,
        [],
        {},
        KERNEL_BYTES,
        [],
    )


def weight_specs(streams):
    return [ANY if streams else VMEM]


def weight_buffers(weight, quarters):
    shape = (weight.shape[0], weight.shape[1] // QUARTERS)
    return [pltpu.VMEM((count, *shape), weight.dtype) for count in quarters] + [
        pltpu.SemaphoreType.DMA((count,)) for count in quarters
    ]


def run_forward_far(section, place, pieces, gain, up, down, stash, streams):
    rows, (local, width) = pieces[0].shape[0], up.shape
    part = struct(rows, len(FAR) * width // QUARTERS)
    first = 4 + len(pieces)
    result = call(
        functools.partial(forward_far, section, len(pieces), bool(stash), streams),
        [place, *pieces, gain, up, down, *stash],
        [SMEM] + [VMEM] * (len(pieces) + 1) + weight_specs(streams) * 2 + [ANY] * len(stash),
        [
            part,
            struct(rows, local),
            struct(rows, width),
            struct(rows, LANES, dtype=jnp.float32),
            struct(rows, local, dtype=jnp.float32),
            struct(rows, width // QUARTERS, dtype=jnp.float32),
        ],
        [VMEM] * 2 + [ANY] * 4,
        [
            pltpu.VMEM((rows, LANES), jnp.float32),
            pltpu.VMEM((rows, local), jnp.float32),
            pltpu.VMEM((rows, width // QUARTERS), jnp.float32),
            pltpu.SemaphoreType.DMA((QUARTERS + 3,)),
            *(weight_buffers(up, [QUARTERS, len(FAR)]) if streams else []),
        ],
        {first + i: 2 + i for i in range(len(stash))},
        STREAM_BYTES if streams else KERNEL_BYTES,
        [(rows, width, local), (rows, local, 3 * width // 4)],
    )
    return (result[0], result[1], result[2:])


def run_forward_near(section, place, hidden, down, streams):
    rows, (local, width) = hidden.shape[0], down.shape
    part = struct(rows, width // QUARTERS)
    return call(
        functools.partial(forward_near, section, streams),
        [place, hidden, down],
        [SMEM, VMEM, *weight_specs(streams)],
        [part] * 2,
        [VMEM] * 2,
        weight_buffers(down, [len(NEAR)]) if streams else [],
        {},
        KERNEL_BYTES,
        [(rows, local, width // 4)],
    )


def run_early_grad(section, place, entered, down):
    rows, (local, width) = entered.shape[0], down.shape
    return call(
        functools.partial(early_grad, section),
        [place, entered, down],
        [SMEM, VMEM, VMEM],
        [struct(rows, width), struct(rows, local, dtype=jnp.float32)],
        [ANY] * 2,
        [pltpu.VMEM((rows, local), jnp.float32), pltpu.SemaphoreType.DMA((2,))],
        {},
        KERNEL_BYTES,
        [(rows, width, local)],
    )


def run_last_far(section, place, pieces, hidden_grad, gain, up, stash):
    rows, (local, width) = pieces[0].shape[0], up.shape
    part = struct(rows, len(FAR) * (width // QUARTERS + LANES))
    result = call(
        functools.partial(last_far, section),
        [place, *pieces, hidden_grad, gain, up, *stash],
        [SMEM] + [VMEM] * (QUARTERS + 3) + [ANY] * 4,
        [
            part,
            struct(rows, local),
            struct(rows, LANES),
            struct(rows, width),
            struct(rows, LANES, dtype=jnp.float32),
            struct(rows, local, dtype=jnp.float32),
            struct(rows, width // QUARTERS, dtype=jnp.float32),
            struct(rows, local),
            struct(QUARTERS, 1, width // QUARTERS, dtype=jnp.float32),
        ],
        [VMEM] * 3 + [ANY] * 6,
        [
            pltpu.VMEM((rows, LANES), jnp.float32),
            pltpu.VMEM((rows, local), jnp.float32),
            pltpu.VMEM((rows, width // QUARTERS), jnp.float32),
            pltpu.VMEM((len(FAR), 1, width // QUARTERS), jnp.float32),
            pltpu.SemaphoreType.DMA((QUARTERS + 7,)),
        ],
        {QUARTERS + 4 + i: 3 + i for i in range(4)},
        KERNEL_BYTES,
        [(rows, width, local), (rows, local, 3 * width // 4)],
    )
    return (result[0], result[1:3], result[3:7], result[7:])


def run_backward_far(section, place, pieces, kept, up, down, grads):
    rows, (local, width) = pieces[0].shape[0], up.shape
    part = struct(rows, len(FAR) * (width // QUARTERS + LANES))
    result = call(
        functools.partial(backward_far, section),
        [place, *pieces, *kept, up, down, *grads],
        [SMEM] + [VMEM] * (QUARTERS + 5) + [ANY] * 3,
        [
            part,
            struct(rows, local),
            struct(rows, LANES),
            struct(rows, width),
            struct(rows, local),
            struct(QUARTERS, 1, width // QUARTERS, dtype=jnp.float32),
        ],
        [VMEM] * 3 + [ANY] * 3,
        [
            pltpu.VMEM((len(FAR), 1, width // QUARTERS), jnp.float32),
            pltpu.SemaphoreType.DMA((QUARTERS + 4,)),
        ],
        {QUARTERS + 6 + i: 3 + i for i in range(3)},
        KERNEL_BYTES,
        [(rows, width, local), (rows, local, 3 * width // 4)],
    )
    return (result[0], result[1:3], result[3:])


def run_backward_near(section, place, passed, kept, up, gain_part):
    rows, (local, width) = kept[0].shape[0], up.shape
    part = struct(rows, width // QUARTERS + LANES)
    result = call(
        functools.partial(backward_near, section),
        [place, *passed, kept[0], kept[1], up, gain_part],
        [SMEM] + [VMEM] * 5 + [ANY],
        [part, part, struct(*gain_part.shape, dtype=jnp.float32)],
        [VMEM, VMEM, ANY],
        [
            pltpu.VMEM((len(NEAR), 1, width // QUARTERS), jnp.float32),
            pltpu.SemaphoreType.DMA((len(NEAR),)),
        ],
        {6: 2},
        KERNEL_BYTES,
        [(rows, local, width // 4)],
    )
    return (result[:2], result[2])


def run_final(section, place, pieces, grads, kept, gain, up, down):
    rows, (local, width) = pieces[0].shape[0], up.shape
    buffers = [
        pltpu.VMEM((SLOTS, BLOCK, width), jnp.float32),
        pltpu.SemaphoreType.DMA((SLOTS,)),
    ]
    grad_down, preact_grad, gain_part, scaled = call(
        functools.partial(final_down, section),
        [place, *pieces, *grads, *kept, gain, up, down],
        [SMEM] + [VMEM] * (QUARTERS + 9),
        [
            struct(local, width, dtype=jnp.float32),
            struct(rows, local),
            struct(*grads[2].shape, dtype=jnp.float32),
            struct(rows, width),
        ],
        [ANY] + [VMEM] * 3,
        [
            pltpu.VMEM((rows, width), jnp.bfloat16),
            pltpu.VMEM((rows, local), jnp.bfloat16),
            pltpu.VMEM((local, rows), jnp.float32),
            *buffers,
        ],
        {},
        KERNEL_BYTES,
        [(rows, width, local)] * 2 + [(local, rows, width)],
    )
    blocks = hidden_blocks(local)
    half = (len(blocks) + 1) // 2
    grad_up = ()
    for taken in (blocks[:half], blocks[half:]):
        grad_up = call(
            functools.partial(final_up, taken),
            [preact_grad, scaled, *grad_up],
            [VMEM, VMEM] + [ANY] * len(grad_up),
            [struct(local, width, dtype=jnp.float32)],
            [ANY],
            buffers,
            {2: 0} if grad_up else {},
            KERNEL_BYTES,
            [(local // 2, rows, width)],
        )
    return (grad_up[0], grad_down, gain_part)


def within(sections, flip):
    count = lax.axis_size("dp")
    return [(s * count + r, s * count + (r ^ flip)) for s in sections for r in range(count)]


def between(moves, flip):
    count = lax.axis_size("dp")
    return [(s * count + r, t * count + (r ^ flip)) for s, t in moves for r in range(count)]


def send_quarter(part, sections, k):
    return lax.ppermute(part, AXES, within(sections, k * (lax.axis_size("dp") // QUARTERS)))


def sum_quarters(arrived, cross, own, sections):
    inner = lax.axis_size("dp") // QUARTERS
    width = own.shape[1]
    cross = cross.astype(jnp.float32) + arrived[:, width:].astype(jnp.float32)
    cross = send_quarter(cross.astype(jnp.bfloat16), sections, 2)
    total = own.astype(jnp.float32) + arrived[:, :width].astype(jnp.float32)
    total = total + cross.astype(jnp.float32)
    flip = 1
    while flip < inner:
        rounded = total.astype(jnp.bfloat16)
        other = lax.ppermute(rounded, AXES, within(sections, flip))
        total = rounded.astype(jnp.float32) + other.astype(jnp.float32)
        flip *= 2
    return total


def hand_on(own, moves):
    inner = lax.axis_size("dp") // QUARTERS
    pieces = {
        k: lax.ppermute(own, AXES, between(moves, k * inner)) for k in range(QUARTERS - 1, -1, -1)
    }
    return [pieces[k] for k in range(QUARTERS)]


def gather_chunks(chunk, sections):
    inner = lax.axis_size("dp") // QUARTERS
    held = chunk
    flip = 1
    while flip < inner:
        other = lax.ppermute(held, AXES, within(sections, flip))
        held = jnp.concatenate([held, other], axis=0)
        flip *= 2
    pieces = {k: send_quarter(held, sections, k) for k in range(QUARTERS - 1, 0, -1)}
    return [held] + [pieces[k] for k in range(1, QUARTERS)]


def sum_over_dp(value):
    flip = 1
    while flip < lax.axis_size("dp"):
        value = value + lax.ppermute(
            value, "dp", [(r, r ^ flip) for r in range(lax.axis_size("dp"))]
        )
        flip *= 2
    return value


def body(section_input, out_cotangent, up_weight, down_weight, norm_gain):
    section_count = lax.axis_size("section")
    section_pos = lax.axis_index("section")
    count = lax.axis_size("dp")
    position = lax.axis_index("dp")
    width = up_weight.shape[1]
    quarter_width = width // QUARTERS
    last = section_count - 1

    def alike(section):
        return [s for s in range(section_count) if s % 2 == section % 2]

    def moves(section, step):
        return [(s, s + step) for s in alike(section) if 0 <= s + step < section_count]

    inner = count // QUARTERS
    place = jnp.stack([section_pos, position // inner, position % inner]).astype(jnp.int32)
    chunk = jnp.where(section_pos == last, out_cotangent, section_input)
    chunk, place = lax.optimization_barrier((chunk[None], place))
    held = gather_chunks(chunk, [0, last])
    streamed_up, streamed_down = (
        pltpu.with_memory_space_constraint(weight[0].T, pltpu.HBM)
        for weight in (up_weight, down_weight)
    )
    up, down = (
        pltpu.with_memory_space_constraint(weight[0].T, pltpu.VMEM)
        for weight in (up_weight, down_weight)
    )
    place = run_touch(place, held[0], up, down)
    entered, own_entered, own_gain = run_lay_rows(place, held, norm_gain)

    pieces, stash, own = [entered], (), own_entered
    for section in range(last):
        here = alike(section)
        streams = section == 0
        weights = (streamed_up, streamed_down) if streams else (up, down)
        far, hidden, stash = run_forward_far(
            section, place, pieces, norm_gain, *weights, stash, streams
        )
        arrived = send_quarter(far, here, 1)
        near = run_forward_near(section, place, hidden, weights[1], streams)
        result = own.astype(jnp.float32) + sum_quarters(arrived, *near, here)
        result = result.astype(jnp.bfloat16)
        pieces = hand_on(result, moves(section, 1))
        own = pieces[0]
        if section == 0:
            for _ in range(TOUCHES):
                place = run_touch(place, result, up, down)
            grad_rows, early = run_early_grad(last, place, entered, down)

    for section in range(last, 0, -1):
        here = alike(section)
        if section == last:
            far, passed, stash, grads = run_last_far(
                last, place, pieces, early, norm_gain, up, stash
            )
            *stash, own_normed = stash
            own_scale = stash[1][:, :1]
            grads = [grad_rows, *grads]
            own = own_entered
        else:
            far, passed, grads = run_backward_far(section, place, pieces, stash, up, down, grads)
            own = pieces[0]
        arrived = send_quarter(far, here, 1)
        near, gain_part = run_backward_near(section, place, passed, stash, up, grads[2])
        grads = [grads[0], grads[1], gain_part]
        total = sum_quarters(arrived, *near, here)
        along = total[:, quarter_width : quarter_width + 1] * (1.0 / width)
        normed_grad = total[:, :quarter_width] * own_gain
        result = own.astype(jnp.float32) + own_scale * (normed_grad - own_normed * along)
        pieces = hand_on(result.astype(jnp.bfloat16), moves(section, -1))

    grad_up, grad_down, gain_part = run_final(
        0, place, pieces, grads, stash, norm_gain, up, down
    )
    grad_gain = sum_over_dp(gain_part.reshape(1, width))
    return (grad_up.T[None], grad_down.T[None], grad_gain)


def solution(mesh):
    placed = (
        P(None, "dp", None),
        P(None, "dp", None),
        P("section", None, "dp"),
        P("section", None, "dp"),
        P("section", None),
    )
    return jax.shard_map(
        body,
        mesh=mesh,
        in_specs=placed,
        out_specs=(P("section", None, "dp"), P("section", None, "dp"), P("section", None)),
        check_vma=False,
    )
```

```python
import functools
import math

import jax
import jax.numpy as jnp
from jax import lax
from jax.experimental import pallas as pl
from jax.experimental.pallas import tpu as pltpu
from jax.sharding import PartitionSpec as P

D = 6656
HIDDEN_SIZE = 8960


EPSILON = 1e-05
GELU_SCALE = 0.7978845608028654
GELU_CUBIC = 0.044715

INV_WIDTH = 1.0 / math.sqrt(D)
INV_HIDDEN = 1.0 / math.sqrt(HIDDEN_SIZE)

AXES = ("section", "dp")
QUARTERS = 4
LANES = 128
BLOCK = 128
SLOTS = 3
TOUCHES = 1
KERNEL_BYTES = 18 * 1024 * 1024
STREAM_BYTES = 32 * 1024 * 1024

ANY = pl.BlockSpec(memory_space=pl.ANY)
VMEM = pl.BlockSpec(memory_space=pltpu.VMEM)
SMEM = pl.BlockSpec(memory_space=pltpu.SMEM)


def gelu_value(preact):
    inner = GELU_SCALE * (preact + GELU_CUBIC * preact * preact * preact)
    return 0.5 * preact * (1.0 + jnp.tanh(inner))


def gelu_slope(preact):
    inner = GELU_SCALE * (preact + GELU_CUBIC * preact * preact * preact)
    tangent = jnp.tanh(inner)
    return 0.5 * (1.0 + tangent) + 0.5 * preact * (1.0 - tangent * tangent) * GELU_SCALE * (
        1.0 + 3.0 * GELU_CUBIC * preact * preact
    )


def outer_rows(left, right):
    return lax.dot_general(
        left, right, (((0,), (0,)), ((), ())), preferred_element_type=jnp.float32
    )


def across_hidden(left, right):
    return lax.dot_general(
        left, right, (((1,), (1,)), ((), ())), preferred_element_type=jnp.float32
    )


def plain_product(left, right):
    return jnp.dot(left, right, preferred_element_type=jnp.float32)


FAR, NEAR = (3,), (2, 1, 0)


def quarter(place_ref, k, width):
    start = (place_ref[1] ^ k) * width
    return pl.ds(pl.multiple_of(start, LANES), width)


def read_quarter(place_ref, piece_refs, k, width):
    if len(piece_refs) == 1:
        return piece_refs[0][:, quarter(place_ref, k, width)]
    return piece_refs[k][...]


def write_out(copies):
    for copy in copies:
        copy.start()
    for copy in copies:
        copy.wait()


def quarter_copies(place_ref, piece_refs, target, sems, width):
    if len(piece_refs) == 1:
        return [pltpu.make_async_copy(piece_refs[0], target, sems.at[0])]
    return [
        pltpu.make_async_copy(ref, target.at[:, quarter(place_ref, k, width)], sems.at[k])
        for k, ref in enumerate(piece_refs)
    ]


def stream(place_ref, source, buffer_ref, sems, quarters):
    width = buffer_ref.shape[2]
    copies = {
        k: pltpu.make_async_copy(
            source.at[:, quarter(place_ref, k, width)], buffer_ref.at[at], sems.at[at]
        )
        for at, k in enumerate(quarters)
    }
    for copy in copies.values():
        copy.start()

    def read(k):
        copies[k].wait()
        return buffer_ref[list(quarters).index(k)]

    return read


def lying(place_ref, weight_ref):
    width = weight_ref.shape[1] // QUARTERS
    return lambda k: weight_ref[:, quarter(place_ref, k, width)]


def contract_width(weight, rows):
    total = None
    for k in range(QUARTERS):
        part = across_hidden(weight(k), rows(k))
        total = part if total is None else total + part
    return total.T


def enter_section(place_ref, piece_refs, gain_ref, up, width):
    squares = 0.0
    for k in range(QUARTERS):
        values = read_quarter(place_ref, piece_refs, k, width).astype(jnp.float32)
        squares = squares + jnp.sum(values * values, axis=-1, keepdims=True)
    norm_scale = lax.rsqrt(squares * (1.0 / (QUARTERS * width)) + EPSILON)

    def read(k):
        normed = read_quarter(place_ref, piece_refs, k, width).astype(jnp.float32) * norm_scale
        return (normed * gain_ref[:, quarter(place_ref, k, width)]).astype(jnp.bfloat16)

    return (norm_scale, contract_width(up, read) * INV_WIDTH)


def hidden_part(part_refs, quarters, hidden, down):
    for at, k in enumerate(quarters):
        part_refs[at][...] = (plain_product(hidden, down(k)) * INV_HIDDEN).astype(jnp.bfloat16)


def scaled_part(part_refs, quarters, preact_grad, along, rows_of, up, gain_ref):
    width = gain_ref.shape[2]
    for at, k in enumerate(quarters):
        part = plain_product(preact_grad, up(k)) * INV_WIDTH
        gain_ref[at] = jnp.sum(part * rows_of(k), axis=0, keepdims=True)
        part_refs[at][:, :width] = part.astype(jnp.bfloat16)
        part_refs[at][:, width:] = along


def along_rows(preact_grad, preact):
    total = jnp.sum(preact_grad.astype(jnp.float32) * preact, axis=-1, keepdims=True)
    return jnp.broadcast_to(total.astype(jnp.bfloat16), (total.shape[0], LANES))


def gain_copies(place_ref, gain_ref, target, quarters, sems):
    return [
        pltpu.make_async_copy(gain_ref.at[at], target.at[place_ref[1] ^ k], sems.at[at])
        for at, k in enumerate(quarters)
    ]


def forward_far(section, pieces, with_stash, streams, place_ref, *refs):
    piece_refs, refs = refs[:pieces], refs[pieces:]
    gain_ref, up_ref, down_ref = refs[:3]
    refs = refs[3 + (4 if with_stash else 0) :]
    part_refs, hidden_ref, refs = refs[:1], refs[1], refs[2:]
    rows_out, scale_out, preact_out, own_out, scale_ref, preact_ref, own_ref, sems = refs[:8]
    width = own_ref.shape[1]

    @pl.when(place_ref[0] == section)
    def _():
        if streams:
            up_buffer, down_buffer, up_sems, down_sems = refs[8:]
            up = stream(place_ref, up_ref, up_buffer, up_sems, range(QUARTERS))
            down = stream(place_ref, down_ref, down_buffer, down_sems, FAR)
        else:
            up, down = lying(place_ref, up_ref), lying(place_ref, down_ref)
        copies = quarter_copies(place_ref, piece_refs, rows_out, sems, width)
        for copy in copies:
            copy.start()
        norm_scale, preact = enter_section(
            place_ref, piece_refs, gain_ref, up, width
        )
        scale_ref[...] = jnp.broadcast_to(norm_scale, scale_ref.shape)
        preact_ref[...] = preact
        own_rows = read_quarter(place_ref, piece_refs, 0, width)
        own_ref[...] = own_rows.astype(jnp.float32) * norm_scale
        more = [
            pltpu.make_async_copy(scale_ref, scale_out, sems.at[QUARTERS]),
            pltpu.make_async_copy(preact_ref, preact_out, sems.at[QUARTERS + 1]),
            pltpu.make_async_copy(own_ref, own_out, sems.at[QUARTERS + 2]),
        ]
        for copy in more:
            copy.start()
        hidden = gelu_value(preact).astype(jnp.bfloat16)
        hidden_ref[...] = hidden
        hidden_part(part_refs, FAR, hidden, down)
        for copy in copies + more:
            copy.wait()


def forward_near(section, streams, place_ref, hidden_ref, down_ref, *refs):
    @pl.when(place_ref[0] == section)
    def _():
        if streams:
            down = stream(place_ref, down_ref, *refs[len(NEAR) :], NEAR)
        else:
            down = lying(place_ref, down_ref)
        hidden_part(refs[: len(NEAR)], NEAR, hidden_ref[...], down)


def early_grad(
    section, place_ref, rows_ref, down_ref, grad_out, hidden_grad_out, total_ref, sems
):
    width = rows_ref.shape[1] // QUARTERS

    @pl.when(place_ref[0] == section)
    def _():
        first = pltpu.make_async_copy(rows_ref, grad_out, sems.at[0])
        first.start()
        total_ref[...] = INV_HIDDEN * contract_width(
            lying(place_ref, down_ref),
            lambda k: read_quarter(place_ref, [rows_ref], k, width),
        )
        second = pltpu.make_async_copy(total_ref, hidden_grad_out, sems.at[1])
        second.start()
        first.wait()
        second.wait()


def last_far(section, place_ref, *refs):
    piece_refs, refs = refs[:QUARTERS], refs[QUARTERS:]
    hidden_grad_ref, gain_row_ref, up_ref = refs[:3]
    refs = refs[7:]
    part_refs, preact_grad_ref, along_ref, refs = refs[:1], refs[1], refs[2], refs[3:]
    rows_out, scale_out, preact_out, own_out, preact_grad_out, gain_out = refs[:6]
    scale_ref, preact_ref, own_ref, gain_ref, sems = refs[6:]
    width = gain_ref.shape[2]
    up = lying(place_ref, up_ref)

    @pl.when(place_ref[0] == section)
    def _():
        copies = quarter_copies(place_ref, piece_refs, rows_out, sems, width)
        for copy in copies:
            copy.start()
        norm_scale, preact = enter_section(place_ref, piece_refs, gain_row_ref, up, width)
        preact_grad = (hidden_grad_ref[...] * gelu_slope(preact)).astype(jnp.bfloat16)
        along = along_rows(preact_grad, preact)
        scale_ref[...] = jnp.broadcast_to(norm_scale, scale_ref.shape)
        preact_ref[...] = preact
        preact_grad_ref[...] = preact_grad
        along_ref[...] = along
        own_ref[...] = piece_refs[0][...].astype(jnp.float32) * norm_scale
        more = [
            pltpu.make_async_copy(scale_ref, scale_out, sems.at[QUARTERS]),
            pltpu.make_async_copy(preact_ref, preact_out, sems.at[QUARTERS + 1]),
            pltpu.make_async_copy(own_ref, own_out, sems.at[QUARTERS + 2]),
            pltpu.make_async_copy(preact_grad_ref, preact_grad_out, sems.at[QUARTERS + 3]),
        ]
        for copy in more:
            copy.start()

        def rows_of(k):
            return piece_refs[k][...].astype(jnp.float32) * norm_scale

        scaled_part(part_refs, FAR, preact_grad, along, rows_of, up, gain_ref)
        write_out(gain_copies(place_ref, gain_ref, gain_out, FAR, sems.at[pl.ds(QUARTERS + 4, len(FAR))]))
        for copy in copies + more:
            copy.wait()


def backward_far(section, place_ref, *refs):
    piece_refs, refs = refs[:QUARTERS], refs[QUARTERS:]
    rows_ref, scale_ref, preact_ref, up_ref, down_ref = refs[:5]
    refs = refs[8:]
    part_refs, preact_grad_ref, along_ref, refs = refs[:1], refs[1], refs[2], refs[3:]
    grad_out, preact_grad_out, gain_out, gain_ref, sems = refs
    width = gain_ref.shape[2]

    @pl.when(place_ref[0] == section)
    def _():
        copies = quarter_copies(place_ref, piece_refs, grad_out, sems, width)
        for copy in copies:
            copy.start()
        hidden_grad = INV_HIDDEN * contract_width(
            lying(place_ref, down_ref), lambda k: piece_refs[k][...]
        )
        preact = preact_ref[...]
        preact_grad = (hidden_grad * gelu_slope(preact)).astype(jnp.bfloat16)
        along = along_rows(preact_grad, preact)
        preact_grad_ref[...] = preact_grad
        along_ref[...] = along
        more = pltpu.make_async_copy(preact_grad_ref, preact_grad_out, sems.at[QUARTERS])
        more.start()
        norm_scale = scale_ref[:, :1]

        def rows_of(k):
            return rows_ref[:, quarter(place_ref, k, width)].astype(jnp.float32) * norm_scale

        up = lying(place_ref, up_ref)
        scaled_part(part_refs, FAR, preact_grad, along, rows_of, up, gain_ref)
        write_out(gain_copies(place_ref, gain_ref, gain_out, FAR, sems.at[pl.ds(QUARTERS + 1, len(FAR))]))
        for copy in copies + [more]:
            copy.wait()


def backward_near(
    section, place_ref, preact_grad_ref, along_ref, rows_ref, scale_ref, up_ref, gain_in, *refs
):
    del gain_in
    part_refs, (gain_out, gain_ref, sems) = refs[: len(NEAR)], refs[len(NEAR) :]
    width = gain_ref.shape[2]

    @pl.when(place_ref[0] == section)
    def _():
        norm_scale = scale_ref[:, :1]

        def rows_of(k):
            return rows_ref[:, quarter(place_ref, k, width)].astype(jnp.float32) * norm_scale

        scaled_part(
            part_refs, NEAR, preact_grad_ref[...], along_ref[...],
            rows_of, lying(place_ref, up_ref), gain_ref,
        )
        write_out(gain_copies(place_ref, gain_ref, gain_out, NEAR, sems))


def hidden_blocks(local):
    return [(start, min(BLOCK, local - start)) for start in range(0, local, BLOCK)]


def outer_blocks(left_ref, right_ref, factor, blocks, target, buffer_ref, sems, beside):
    copies = []
    for i, (start, size) in enumerate(blocks):
        slot = i % SLOTS
        if i >= SLOTS:
            copies[i - SLOTS].wait()
        value = outer_rows(left_ref[:, start : start + size], right_ref[...])
        buffer_ref[slot, :size] = value * factor
        copy = pltpu.make_async_copy(
            buffer_ref.at[slot, pl.ds(0, size)], target.at[pl.ds(start, size)], sems.at[slot]
        )
        copy.start()
        copies.append(copy)
        if i < len(beside):
            beside[i]()
    for run in beside[len(blocks) :]:
        run()
    for copy in copies[-SLOTS:]:
        copy.wait()


def final_down(section, place_ref, *refs):
    piece_refs, refs = refs[:QUARTERS], refs[QUARTERS:]
    grad_in, preact_grad_in, gain_in, rows_ref, scale_ref, preact_ref, gain_row_ref = refs[:7]
    up_ref, down_ref = refs[7:9]
    target, preact_grad_ref, gain_ref, scaled_ref = refs[9:13]
    grad_ref, hidden_ref, hidden_grad_ref, buffer_ref, sems = refs[13:]
    width = gain_ref.shape[2]
    up, down = lying(place_ref, up_ref), lying(place_ref, down_ref)
    active = place_ref[0] == section

    @pl.when(active)
    def _():
        for k in range(QUARTERS):
            grad_ref[:, quarter(place_ref, k, width)] = piece_refs[k][...]

    @pl.when(jnp.logical_not(active))
    def _():
        grad_ref[...] = grad_in[...]
        preact_grad_ref[...] = preact_grad_in[...]
        gain_ref[...] = gain_in[...]

    norm_scale = scale_ref[:, :1]
    hidden_ref[...] = gelu_value(preact_ref[...]).astype(jnp.bfloat16)

    def add_grad(k):
        @pl.when(active)
        def _():
            part = across_hidden(down(k), piece_refs[k][...])
            hidden_grad_ref[...] = part if k == 0 else hidden_grad_ref[...] + part

    def finish_grad():
        @pl.when(active)
        def _():
            hidden_grad = hidden_grad_ref[...].T * INV_HIDDEN
            preact_grad_ref[...] = (hidden_grad * gelu_slope(preact_ref[...])).astype(jnp.bfloat16)

    def add_gain(k):
        @pl.when(active)
        def _():
            part = plain_product(preact_grad_ref[...], up(k)) * INV_WIDTH
            rows = rows_ref[:, quarter(place_ref, k, width)]
            normed = rows.astype(jnp.float32) * norm_scale
            gain_ref[place_ref[1] ^ k] = jnp.sum(part * normed, axis=0, keepdims=True)

    def scale_rows():
        normed = rows_ref[...].astype(jnp.float32) * norm_scale
        scaled_ref[...] = (normed * gain_row_ref[...]).astype(jnp.bfloat16)

    beside = [functools.partial(add_grad, k) for k in range(QUARTERS)]
    beside += [finish_grad] + [functools.partial(add_gain, k) for k in range(QUARTERS)]
    beside += [scale_rows]
    blocks = hidden_blocks(target.shape[0])
    outer_blocks(hidden_ref, grad_ref, INV_HIDDEN, blocks, target, buffer_ref, sems, beside)


def final_up(blocks, preact_grad_ref, scaled_ref, *refs):
    target, buffer_ref, sems = refs[-3:]
    outer_blocks(preact_grad_ref, scaled_ref, INV_WIDTH, blocks, target, buffer_ref, sems, [])


def struct(*shape, dtype=jnp.bfloat16):
    return jax.ShapeDtypeStruct(shape, dtype)


def call(kernel, inputs, specs, outputs, out_specs, scratch, aliases, limit, products):
    flops = sum(2 * a * b * c for a, b, c in products)
    return pl.pallas_call(
        kernel,
        out_shape=outputs,
        in_specs=specs,
        out_specs=out_specs,
        scratch_shapes=scratch,
        input_output_aliases=aliases,
        cost_estimate=pl.CostEstimate(
            flops=flops,
            bytes_accessed=sum(2 * b * c for _, b, c in products),
            transcendentals=0,
        ),
        compiler_params=pltpu.CompilerParams(vmem_limit_bytes=limit),
    )(*inputs)


def touch(place_ref, after_ref, up_ref, down_ref, place_out):
    del after_ref, up_ref, down_ref
    for i in range(place_ref.shape[0]):
        place_out[i] = place_ref[i]


def run_touch(place, after, up, down):
    return pl.pallas_call(
        touch,
        out_shape=jax.ShapeDtypeStruct(place.shape, place.dtype),
        in_specs=[SMEM, ANY, VMEM, VMEM],
        out_specs=SMEM,
        compiler_params=pltpu.CompilerParams(vmem_limit_bytes=KERNEL_BYTES),
    )(place, after, up, down)


def lay_rows(place_ref, *refs):
    piece_refs, gain_ref = refs[:QUARTERS], refs[QUARTERS]
    rows_ref, own_ref, own_gain_ref = refs[QUARTERS + 1 :]
    inner, micro, tokens, width = piece_refs[0].shape
    for outer in range(QUARTERS):
        for k, ref in enumerate(piece_refs):

            @pl.when((place_ref[1] ^ k) == outer)
            def _(outer=outer, ref=ref):
                for i in range(inner):
                    for j in range(micro):
                        start = ((outer * inner + i) * micro + j) * tokens
                        rows_ref[start : start + tokens, :] = ref[place_ref[2] ^ i, j]

    own = quarter(place_ref, 0, width // QUARTERS)
    own_ref[...] = rows_ref[:, own]
    own_gain_ref[...] = jnp.broadcast_to(gain_ref[:, own], own_gain_ref.shape)


def run_lay_rows(place, pieces, gain):
    rows, width = QUARTERS * pieces[0].size // gain.size, gain.shape[1]
    return call(
        lay_rows,
        [place, *pieces, gain],
        [SMEM] + [VMEM] * (QUARTERS + 1),
        [
            struct(rows, width),
            struct(rows, width // QUARTERS),
            struct(rows, width // QUARTERS, dtype=jnp.float32),
        ],
        [VMEM] * 3,
        [],
        {},
        KERNEL_BYTES,
        [],
    )


def weight_specs(streams):
    return [ANY if streams else VMEM]


def weight_buffers(weight, quarters):
    shape = (weight.shape[0], weight.shape[1] // QUARTERS)
    return [pltpu.VMEM((count, *shape), weight.dtype) for count in quarters] + [
        pltpu.SemaphoreType.DMA((count,)) for count in quarters
    ]


def run_forward_far(section, place, pieces, gain, up, down, stash, streams):
    rows, (local, width) = pieces[0].shape[0], up.shape
    part = struct(rows, width // QUARTERS)
    first = 4 + len(pieces)
    result = call(
        functools.partial(forward_far, section, len(pieces), bool(stash), streams),
        [place, *pieces, gain, up, down, *stash],
        [SMEM] + [VMEM] * (len(pieces) + 1) + weight_specs(streams) * 2 + [ANY] * len(stash),
        [
            *[part] * len(FAR),
            struct(rows, local),
            struct(rows, width),
            struct(rows, LANES, dtype=jnp.float32),
            struct(rows, local, dtype=jnp.float32),
            struct(rows, width // QUARTERS, dtype=jnp.float32),
        ],
        [VMEM] * 2 + [ANY] * 4,
        [
            pltpu.VMEM((rows, LANES), jnp.float32),
            pltpu.VMEM((rows, local), jnp.float32),
            pltpu.VMEM((rows, width // QUARTERS), jnp.float32),
            pltpu.SemaphoreType.DMA((QUARTERS + 3,)),
            *(weight_buffers(up, [QUARTERS, len(FAR)]) if streams else []),
        ],
        {first + i: 2 + i for i in range(len(stash))},
        STREAM_BYTES if streams else KERNEL_BYTES,
        [(rows, width, local), (rows, local, 3 * width // 4)],
    )
    return (result[:1], result[1], result[2:])


def run_forward_near(section, place, hidden, down, streams):
    rows, (local, width) = hidden.shape[0], down.shape
    part = struct(rows, width // QUARTERS)
    return call(
        functools.partial(forward_near, section, streams),
        [place, hidden, down],
        [SMEM, VMEM, *weight_specs(streams)],
        [part] * len(NEAR),
        [VMEM] * len(NEAR),
        weight_buffers(down, [len(NEAR)]) if streams else [],
        {},
        KERNEL_BYTES,
        [(rows, local, width // 4)],
    )


def run_early_grad(section, place, entered, down):
    rows, (local, width) = entered.shape[0], down.shape
    return call(
        functools.partial(early_grad, section),
        [place, entered, down],
        [SMEM, VMEM, VMEM],
        [struct(rows, width), struct(rows, local, dtype=jnp.float32)],
        [ANY] * 2,
        [pltpu.VMEM((rows, local), jnp.float32), pltpu.SemaphoreType.DMA((2,))],
        {},
        KERNEL_BYTES,
        [(rows, width, local)],
    )


def run_last_far(section, place, pieces, hidden_grad, gain, up, stash):
    rows, (local, width) = pieces[0].shape[0], up.shape
    part = struct(rows, width // QUARTERS + LANES)
    result = call(
        functools.partial(last_far, section),
        [place, *pieces, hidden_grad, gain, up, *stash],
        [SMEM] + [VMEM] * (QUARTERS + 3) + [ANY] * 4,
        [
            *[part] * len(FAR),
            struct(rows, local),
            struct(rows, LANES),
            struct(rows, width),
            struct(rows, LANES, dtype=jnp.float32),
            struct(rows, local, dtype=jnp.float32),
            struct(rows, width // QUARTERS, dtype=jnp.float32),
            struct(rows, local),
            struct(QUARTERS, 1, width // QUARTERS, dtype=jnp.float32),
        ],
        [VMEM] * 3 + [ANY] * 6,
        [
            pltpu.VMEM((rows, LANES), jnp.float32),
            pltpu.VMEM((rows, local), jnp.float32),
            pltpu.VMEM((rows, width // QUARTERS), jnp.float32),
            pltpu.VMEM((len(FAR), 1, width // QUARTERS), jnp.float32),
            pltpu.SemaphoreType.DMA((QUARTERS + 7,)),
        ],
        {QUARTERS + 4 + i: 3 + i for i in range(4)},
        KERNEL_BYTES,
        [(rows, width, local), (rows, local, 3 * width // 4)],
    )
    return (result[:1], result[1:3], result[3:7], result[7:])


def run_backward_far(section, place, pieces, kept, up, down, grads):
    rows, (local, width) = pieces[0].shape[0], up.shape
    part = struct(rows, width // QUARTERS + LANES)
    result = call(
        functools.partial(backward_far, section),
        [place, *pieces, *kept, up, down, *grads],
        [SMEM] + [VMEM] * (QUARTERS + 5) + [ANY] * 3,
        [
            *[part] * len(FAR),
            struct(rows, local),
            struct(rows, LANES),
            struct(rows, width),
            struct(rows, local),
            struct(QUARTERS, 1, width // QUARTERS, dtype=jnp.float32),
        ],
        [VMEM] * 3 + [ANY] * 3,
        [
            pltpu.VMEM((len(FAR), 1, width // QUARTERS), jnp.float32),
            pltpu.SemaphoreType.DMA((QUARTERS + 4,)),
        ],
        {QUARTERS + 6 + i: 3 + i for i in range(3)},
        KERNEL_BYTES,
        [(rows, width, local), (rows, local, 3 * width // 4)],
    )
    return (result[:1], result[1:3], result[3:])


def run_backward_near(section, place, passed, kept, up, gain_part):
    rows, (local, width) = kept[0].shape[0], up.shape
    part = struct(rows, width // QUARTERS + LANES)
    result = call(
        functools.partial(backward_near, section),
        [place, *passed, kept[0], kept[1], up, gain_part],
        [SMEM] + [VMEM] * 5 + [ANY],
        [part] * len(NEAR) + [struct(*gain_part.shape, dtype=jnp.float32)],
        [VMEM] * len(NEAR) + [ANY],
        [
            pltpu.VMEM((len(NEAR), 1, width // QUARTERS), jnp.float32),
            pltpu.SemaphoreType.DMA((len(NEAR),)),
        ],
        {6: len(NEAR)},
        KERNEL_BYTES,
        [(rows, local, width // 4)],
    )
    return (result[:-1], result[-1])


def run_final(section, place, pieces, grads, kept, gain, up, down):
    rows, (local, width) = pieces[0].shape[0], up.shape
    buffers = [
        pltpu.VMEM((SLOTS, BLOCK, width), jnp.float32),
        pltpu.SemaphoreType.DMA((SLOTS,)),
    ]
    grad_down, preact_grad, gain_part, scaled = call(
        functools.partial(final_down, section),
        [place, *pieces, *grads, *kept, gain, up, down],
        [SMEM] + [VMEM] * (QUARTERS + 9),
        [
            struct(local, width, dtype=jnp.float32),
            struct(rows, local),
            struct(*grads[2].shape, dtype=jnp.float32),
            struct(rows, width),
        ],
        [ANY] + [VMEM] * 3,
        [
            pltpu.VMEM((rows, width), jnp.bfloat16),
            pltpu.VMEM((rows, local), jnp.bfloat16),
            pltpu.VMEM((local, rows), jnp.float32),
            *buffers,
        ],
        {},
        KERNEL_BYTES,
        [(rows, width, local)] * 2 + [(local, rows, width)],
    )
    blocks = hidden_blocks(local)
    third = (len(blocks) + 2) // 3
    grad_up = ()
    for taken in (blocks[:third], blocks[third : 2 * third], blocks[2 * third :]):
        grad_up = call(
            functools.partial(final_up, taken),
            [preact_grad, scaled, *grad_up],
            [VMEM, VMEM] + [ANY] * len(grad_up),
            [struct(local, width, dtype=jnp.float32)],
            [ANY],
            buffers,
            {2: 0} if grad_up else {},
            KERNEL_BYTES,
            [(local // 3, rows, width)],
        )
    return (grad_up[0], grad_down, gain_part)


def within(sections, flip):
    count = lax.axis_size("dp")
    return [(s * count + r, s * count + (r ^ flip)) for s in sections for r in range(count)]


def between(moves, flip):
    count = lax.axis_size("dp")
    return [(s * count + r, t * count + (r ^ flip)) for s, t in moves for r in range(count)]


def send_quarter(part, sections, k):
    return lax.ppermute(part, AXES, within(sections, k * (lax.axis_size("dp") // QUARTERS)))


def sum_quarters(own, arrived, sections):
    inner = lax.axis_size("dp") // QUARTERS
    total = own.astype(jnp.float32)
    for value in arrived:
        total = total + value.astype(jnp.float32)
    flip = 1
    while flip < inner:
        rounded = total.astype(jnp.bfloat16)
        other = lax.ppermute(rounded, AXES, within(sections, flip))
        total = rounded.astype(jnp.float32) + other.astype(jnp.float32)
        flip *= 2
    return total


def hand_on(own, moves):
    inner = lax.axis_size("dp") // QUARTERS
    pieces = {
        k: lax.ppermute(own, AXES, between(moves, k * inner)) for k in range(QUARTERS - 1, -1, -1)
    }
    return [pieces[k] for k in range(QUARTERS)]


def gather_chunks(chunk, sections):
    inner = lax.axis_size("dp") // QUARTERS
    held = chunk
    flip = 1
    while flip < inner:
        other = lax.ppermute(held, AXES, within(sections, flip))
        held = jnp.concatenate([held, other], axis=0)
        flip *= 2
    pieces = {k: send_quarter(held, sections, k) for k in range(QUARTERS - 1, 0, -1)}
    return [held] + [pieces[k] for k in range(1, QUARTERS)]


def sum_over_dp(value):
    flip = 1
    while flip < lax.axis_size("dp"):
        value = value + lax.ppermute(
            value, "dp", [(r, r ^ flip) for r in range(lax.axis_size("dp"))]
        )
        flip *= 2
    return value


def body(section_input, out_cotangent, up_weight, down_weight, norm_gain):
    section_count = lax.axis_size("section")
    section_pos = lax.axis_index("section")
    count = lax.axis_size("dp")
    position = lax.axis_index("dp")
    width = up_weight.shape[1]
    quarter_width = width // QUARTERS
    last = section_count - 1

    def alike(section):
        return [s for s in range(section_count) if s % 2 == section % 2]

    def moves(section, step):
        return [(s, s + step) for s in alike(section) if 0 <= s + step < section_count]

    inner = count // QUARTERS
    place = jnp.stack([section_pos, position // inner, position % inner]).astype(jnp.int32)
    chunk = jnp.where(section_pos == last, out_cotangent, section_input)
    chunk, place = lax.optimization_barrier((chunk[None], place))
    held = gather_chunks(chunk, [0, last])
    streamed_up, streamed_down = (
        pltpu.with_memory_space_constraint(weight[0].T, pltpu.HBM)
        for weight in (up_weight, down_weight)
    )
    up, down = (
        pltpu.with_memory_space_constraint(weight[0].T, pltpu.VMEM)
        for weight in (up_weight, down_weight)
    )
    place = run_touch(place, held[0], up, down)
    entered, own_entered, own_gain = run_lay_rows(place, held, norm_gain)

    pieces, stash, own = [entered], (), own_entered
    for section in range(last):
        here = alike(section)
        streams = section == 0
        weights = (streamed_up, streamed_down) if streams else (up, down)
        far, hidden, stash = run_forward_far(
            section, place, pieces, norm_gain, *weights, stash, streams
        )
        arrived = [send_quarter(part, here, k) for part, k in zip(far, FAR)]
        near = run_forward_near(section, place, hidden, weights[1], streams)
        arrived += [send_quarter(part, here, k) for part, k in zip(near[:-1], NEAR)]
        result = own.astype(jnp.float32) + sum_quarters(near[-1], arrived, here)
        result = result.astype(jnp.bfloat16)
        pieces = hand_on(result, moves(section, 1))
        own = pieces[0]
        if section == 0:
            for _ in range(TOUCHES):
                place = run_touch(place, result, up, down)
            grad_rows, early = run_early_grad(last, place, entered, down)

    for section in range(last, 0, -1):
        here = alike(section)
        if section == last:
            far, passed, stash, grads = run_last_far(
                last, place, pieces, early, norm_gain, up, stash
            )
            *stash, own_normed = stash
            own_scale = stash[1][:, :1]
            grads = [grad_rows, *grads]
            own = own_entered
        else:
            far, passed, grads = run_backward_far(section, place, pieces, stash, up, down, grads)
            own = pieces[0]
        arrived = [send_quarter(part, here, k) for part, k in zip(far, FAR)]
        near, gain_part = run_backward_near(section, place, passed, stash, up, grads[2])
        grads = [grads[0], grads[1], gain_part]
        arrived += [send_quarter(part, here, k) for part, k in zip(near[:-1], NEAR)]
        total = sum_quarters(near[-1], arrived, here)
        along = total[:, quarter_width : quarter_width + 1] * (1.0 / width)
        normed_grad = total[:, :quarter_width] * own_gain
        result = own.astype(jnp.float32) + own_scale * (normed_grad - own_normed * along)
        pieces = hand_on(result.astype(jnp.bfloat16), moves(section, -1))

    grad_up, grad_down, gain_part = run_final(
        0, place, pieces, grads, stash, norm_gain, up, down
    )
    grad_gain = sum_over_dp(gain_part.reshape(1, width))
    return (grad_up.T[None], grad_down.T[None], grad_gain)


def solution(mesh):
    placed = (
        P(None, "dp", None),
        P(None, "dp", None),
        P("section", None, "dp"),
        P("section", None, "dp"),
        P("section", None),
    )
    return jax.shard_map(
        body,
        mesh=mesh,
        in_specs=placed,
        out_specs=(P("section", None, "dp"), P("section", None, "dp"), P("section", None)),
        check_vma=False,
    )
```

```python
import functools
import math

import jax
import jax.numpy as jnp
from jax import lax
from jax.experimental import pallas as pl
from jax.experimental.pallas import tpu as pltpu
from jax.sharding import PartitionSpec as P

D = 6656
HIDDEN_SIZE = 8960


EPSILON = 1e-05
GELU_SCALE = 0.7978845608028654
GELU_CUBIC = 0.044715

INV_WIDTH = 1.0 / math.sqrt(D)
INV_HIDDEN = 1.0 / math.sqrt(HIDDEN_SIZE)

AXES = ("section", "dp")
QUARTERS = 4
LANES = 128
BLOCK = 128
SLOTS = 3
TOUCHES = 1
KERNEL_BYTES = 18 * 1024 * 1024
STREAM_BYTES = 32 * 1024 * 1024

ANY = pl.BlockSpec(memory_space=pl.ANY)
VMEM = pl.BlockSpec(memory_space=pltpu.VMEM)
SMEM = pl.BlockSpec(memory_space=pltpu.SMEM)


def gelu_value(preact):
    inner = GELU_SCALE * (preact + GELU_CUBIC * preact * preact * preact)
    return 0.5 * preact * (1.0 + jnp.tanh(inner))


def gelu_slope(preact):
    inner = GELU_SCALE * (preact + GELU_CUBIC * preact * preact * preact)
    tangent = jnp.tanh(inner)
    return 0.5 * (1.0 + tangent) + 0.5 * preact * (1.0 - tangent * tangent) * GELU_SCALE * (
        1.0 + 3.0 * GELU_CUBIC * preact * preact
    )


def outer_rows(left, right):
    return lax.dot_general(
        left, right, (((0,), (0,)), ((), ())), preferred_element_type=jnp.float32
    )


def across_hidden(left, right):
    return lax.dot_general(
        left, right, (((1,), (1,)), ((), ())), preferred_element_type=jnp.float32
    )


def plain_product(left, right):
    return jnp.dot(left, right, preferred_element_type=jnp.float32)


FAR, NEAR = (3, 2, 1), (0,)


def quarter(place_ref, k, width):
    start = (place_ref[1] ^ k) * width
    return pl.ds(pl.multiple_of(start, LANES), width)


def read_quarter(place_ref, piece_refs, k, width):
    if len(piece_refs) == 1:
        return piece_refs[0][:, quarter(place_ref, k, width)]
    return piece_refs[k][...]


def write_out(copies):
    for copy in copies:
        copy.start()
    for copy in copies:
        copy.wait()


def quarter_copies(place_ref, piece_refs, target, sems, width):
    if len(piece_refs) == 1:
        return [pltpu.make_async_copy(piece_refs[0], target, sems.at[0])]
    return [
        pltpu.make_async_copy(ref, target.at[:, quarter(place_ref, k, width)], sems.at[k])
        for k, ref in enumerate(piece_refs)
    ]


def stream(place_ref, source, buffer_ref, sems, quarters):
    width = buffer_ref.shape[2]
    copies = {
        k: pltpu.make_async_copy(
            source.at[:, quarter(place_ref, k, width)], buffer_ref.at[at], sems.at[at]
        )
        for at, k in enumerate(quarters)
    }
    for copy in copies.values():
        copy.start()

    def read(k):
        copies[k].wait()
        return buffer_ref[list(quarters).index(k)]

    return read


def lying(place_ref, weight_ref):
    width = weight_ref.shape[1] // QUARTERS
    return lambda k: weight_ref[:, quarter(place_ref, k, width)]


def contract_width(weight, rows):
    total = None
    for k in range(QUARTERS):
        part = across_hidden(weight(k), rows(k))
        total = part if total is None else total + part
    return total.T


def enter_section(place_ref, piece_refs, gain_ref, up, width):
    squares = 0.0
    for k in range(QUARTERS):
        values = read_quarter(place_ref, piece_refs, k, width).astype(jnp.float32)
        squares = squares + jnp.sum(values * values, axis=-1, keepdims=True)
    norm_scale = lax.rsqrt(squares * (1.0 / (QUARTERS * width)) + EPSILON)

    def read(k):
        normed = read_quarter(place_ref, piece_refs, k, width).astype(jnp.float32) * norm_scale
        return (normed * gain_ref[:, quarter(place_ref, k, width)]).astype(jnp.bfloat16)

    return (norm_scale, contract_width(up, read) * INV_WIDTH)


def hidden_part(part_refs, quarters, hidden, down):
    for at, k in enumerate(quarters):
        part_refs[at][...] = (plain_product(hidden, down(k)) * INV_HIDDEN).astype(jnp.bfloat16)


def scaled_part(part_refs, quarters, preact_grad, along, rows_of, up, gain_ref):
    width = gain_ref.shape[2]
    for at, k in enumerate(quarters):
        part = plain_product(preact_grad, up(k)) * INV_WIDTH
        gain_ref[at] = jnp.sum(part * rows_of(k), axis=0, keepdims=True)
        part_refs[at][:, :width] = part.astype(jnp.bfloat16)
        part_refs[at][:, width:] = along


def along_rows(preact_grad, preact):
    total = jnp.sum(preact_grad.astype(jnp.float32) * preact, axis=-1, keepdims=True)
    return jnp.broadcast_to(total.astype(jnp.bfloat16), (total.shape[0], LANES))


def gain_copies(place_ref, gain_ref, target, quarters, sems):
    return [
        pltpu.make_async_copy(gain_ref.at[at], target.at[place_ref[1] ^ k], sems.at[at])
        for at, k in enumerate(quarters)
    ]


def forward_far(section, pieces, with_stash, streams, place_ref, *refs):
    piece_refs, refs = refs[:pieces], refs[pieces:]
    gain_ref, up_ref, down_ref = refs[:3]
    refs = refs[3 + (4 if with_stash else 0) :]
    part_refs, hidden_ref, refs = refs[:3], refs[3], refs[4:]
    rows_out, scale_out, preact_out, own_out, scale_ref, preact_ref, own_ref, sems = refs[:8]
    width = own_ref.shape[1]

    @pl.when(place_ref[0] == section)
    def _():
        if streams:
            up_buffer, down_buffer, up_sems, down_sems = refs[8:]
            up = stream(place_ref, up_ref, up_buffer, up_sems, range(QUARTERS))
            down = stream(place_ref, down_ref, down_buffer, down_sems, FAR)
        else:
            up, down = lying(place_ref, up_ref), lying(place_ref, down_ref)
        copies = quarter_copies(place_ref, piece_refs, rows_out, sems, width)
        for copy in copies:
            copy.start()
        norm_scale, preact = enter_section(
            place_ref, piece_refs, gain_ref, up, width
        )
        scale_ref[...] = jnp.broadcast_to(norm_scale, scale_ref.shape)
        preact_ref[...] = preact
        own_rows = read_quarter(place_ref, piece_refs, 0, width)
        own_ref[...] = own_rows.astype(jnp.float32) * norm_scale
        more = [
            pltpu.make_async_copy(scale_ref, scale_out, sems.at[QUARTERS]),
            pltpu.make_async_copy(preact_ref, preact_out, sems.at[QUARTERS + 1]),
            pltpu.make_async_copy(own_ref, own_out, sems.at[QUARTERS + 2]),
        ]
        for copy in more:
            copy.start()
        hidden = gelu_value(preact).astype(jnp.bfloat16)
        hidden_ref[...] = hidden
        hidden_part(part_refs, FAR, hidden, down)
        for copy in copies + more:
            copy.wait()


def forward_near(section, streams, place_ref, hidden_ref, down_ref, part_ref, *refs):
    @pl.when(place_ref[0] == section)
    def _():
        if streams:
            down = stream(place_ref, down_ref, *refs, NEAR)
        else:
            down = lying(place_ref, down_ref)
        hidden_part([part_ref], NEAR, hidden_ref[...], down)


def early_grad(
    section, place_ref, rows_ref, down_ref, grad_out, hidden_grad_out, total_ref, sems
):
    width = rows_ref.shape[1] // QUARTERS

    @pl.when(place_ref[0] == section)
    def _():
        first = pltpu.make_async_copy(rows_ref, grad_out, sems.at[0])
        first.start()
        total_ref[...] = INV_HIDDEN * contract_width(
            lying(place_ref, down_ref),
            lambda k: read_quarter(place_ref, [rows_ref], k, width),
        )
        second = pltpu.make_async_copy(total_ref, hidden_grad_out, sems.at[1])
        second.start()
        first.wait()
        second.wait()


def last_far(section, place_ref, *refs):
    piece_refs, refs = refs[:QUARTERS], refs[QUARTERS:]
    hidden_grad_ref, gain_row_ref, up_ref = refs[:3]
    refs = refs[7:]
    part_refs, preact_grad_ref, along_ref, refs = refs[:3], refs[3], refs[4], refs[5:]
    rows_out, scale_out, preact_out, own_out, preact_grad_out, gain_out = refs[:6]
    scale_ref, preact_ref, own_ref, gain_ref, sems = refs[6:]
    width = gain_ref.shape[2]
    up = lying(place_ref, up_ref)

    @pl.when(place_ref[0] == section)
    def _():
        copies = quarter_copies(place_ref, piece_refs, rows_out, sems, width)
        for copy in copies:
            copy.start()
        norm_scale, preact = enter_section(place_ref, piece_refs, gain_row_ref, up, width)
        preact_grad = (hidden_grad_ref[...] * gelu_slope(preact)).astype(jnp.bfloat16)
        along = along_rows(preact_grad, preact)
        scale_ref[...] = jnp.broadcast_to(norm_scale, scale_ref.shape)
        preact_ref[...] = preact
        preact_grad_ref[...] = preact_grad
        along_ref[...] = along
        own_ref[...] = piece_refs[0][...].astype(jnp.float32) * norm_scale
        more = [
            pltpu.make_async_copy(scale_ref, scale_out, sems.at[QUARTERS]),
            pltpu.make_async_copy(preact_ref, preact_out, sems.at[QUARTERS + 1]),
            pltpu.make_async_copy(own_ref, own_out, sems.at[QUARTERS + 2]),
            pltpu.make_async_copy(preact_grad_ref, preact_grad_out, sems.at[QUARTERS + 3]),
        ]
        for copy in more:
            copy.start()

        def rows_of(k):
            return piece_refs[k][...].astype(jnp.float32) * norm_scale

        scaled_part(part_refs, FAR, preact_grad, along, rows_of, up, gain_ref)
        write_out(gain_copies(place_ref, gain_ref, gain_out, FAR, sems.at[pl.ds(QUARTERS + 4, len(FAR))]))
        for copy in copies + more:
            copy.wait()


def backward_far(section, place_ref, *refs):
    piece_refs, refs = refs[:QUARTERS], refs[QUARTERS:]
    rows_ref, scale_ref, preact_ref, up_ref, down_ref = refs[:5]
    refs = refs[8:]
    part_refs, preact_grad_ref, along_ref, refs = refs[:3], refs[3], refs[4], refs[5:]
    grad_out, preact_grad_out, gain_out, gain_ref, sems = refs
    width = gain_ref.shape[2]

    @pl.when(place_ref[0] == section)
    def _():
        copies = quarter_copies(place_ref, piece_refs, grad_out, sems, width)
        for copy in copies:
            copy.start()
        hidden_grad = INV_HIDDEN * contract_width(
            lying(place_ref, down_ref), lambda k: piece_refs[k][...]
        )
        preact = preact_ref[...]
        preact_grad = (hidden_grad * gelu_slope(preact)).astype(jnp.bfloat16)
        along = along_rows(preact_grad, preact)
        preact_grad_ref[...] = preact_grad
        along_ref[...] = along
        more = pltpu.make_async_copy(preact_grad_ref, preact_grad_out, sems.at[QUARTERS])
        more.start()
        norm_scale = scale_ref[:, :1]

        def rows_of(k):
            return rows_ref[:, quarter(place_ref, k, width)].astype(jnp.float32) * norm_scale

        up = lying(place_ref, up_ref)
        scaled_part(part_refs, FAR, preact_grad, along, rows_of, up, gain_ref)
        write_out(gain_copies(place_ref, gain_ref, gain_out, FAR, sems.at[pl.ds(QUARTERS + 1, len(FAR))]))
        for copy in copies + [more]:
            copy.wait()


def backward_near(
    section, place_ref, preact_grad_ref, along_ref, rows_ref, scale_ref, up_ref, gain_in,
    part_ref, gain_out, gain_ref, sems,
):
    del gain_in
    width = gain_ref.shape[2]

    @pl.when(place_ref[0] == section)
    def _():
        norm_scale = scale_ref[:, :1]

        def rows_of(k):
            return rows_ref[:, quarter(place_ref, k, width)].astype(jnp.float32) * norm_scale

        scaled_part(
            [part_ref], NEAR, preact_grad_ref[...], along_ref[...],
            rows_of, lying(place_ref, up_ref), gain_ref,
        )
        write_out(gain_copies(place_ref, gain_ref, gain_out, NEAR, sems))


def hidden_blocks(local):
    return [(start, min(BLOCK, local - start)) for start in range(0, local, BLOCK)]


def outer_blocks(left_ref, right_ref, factor, blocks, target, buffer_ref, sems, beside):
    copies = []
    for i, (start, size) in enumerate(blocks):
        slot = i % SLOTS
        if i >= SLOTS:
            copies[i - SLOTS].wait()
        value = outer_rows(left_ref[:, start : start + size], right_ref[...])
        buffer_ref[slot, :size] = value * factor
        copy = pltpu.make_async_copy(
            buffer_ref.at[slot, pl.ds(0, size)], target.at[pl.ds(start, size)], sems.at[slot]
        )
        copy.start()
        copies.append(copy)
        if i < len(beside):
            beside[i]()
    for run in beside[len(blocks) :]:
        run()
    for copy in copies[-SLOTS:]:
        copy.wait()


def final_down(section, place_ref, *refs):
    piece_refs, refs = refs[:QUARTERS], refs[QUARTERS:]
    grad_in, preact_grad_in, gain_in, rows_ref, scale_ref, preact_ref, gain_row_ref = refs[:7]
    up_ref, down_ref = refs[7:9]
    target, preact_grad_ref, gain_ref, scaled_ref = refs[9:13]
    grad_ref, hidden_ref, hidden_grad_ref, buffer_ref, sems = refs[13:]
    width = gain_ref.shape[2]
    up, down = lying(place_ref, up_ref), lying(place_ref, down_ref)
    active = place_ref[0] == section

    @pl.when(active)
    def _():
        for k in range(QUARTERS):
            grad_ref[:, quarter(place_ref, k, width)] = piece_refs[k][...]

    @pl.when(jnp.logical_not(active))
    def _():
        grad_ref[...] = grad_in[...]
        preact_grad_ref[...] = preact_grad_in[...]
        gain_ref[...] = gain_in[...]

    norm_scale = scale_ref[:, :1]
    hidden_ref[...] = gelu_value(preact_ref[...]).astype(jnp.bfloat16)

    def add_grad(k):
        @pl.when(active)
        def _():
            part = across_hidden(down(k), piece_refs[k][...])
            hidden_grad_ref[...] = part if k == 0 else hidden_grad_ref[...] + part

    def finish_grad():
        @pl.when(active)
        def _():
            hidden_grad = hidden_grad_ref[...].T * INV_HIDDEN
            preact_grad_ref[...] = (hidden_grad * gelu_slope(preact_ref[...])).astype(jnp.bfloat16)

    def add_gain(k):
        @pl.when(active)
        def _():
            part = plain_product(preact_grad_ref[...], up(k)) * INV_WIDTH
            rows = rows_ref[:, quarter(place_ref, k, width)]
            normed = rows.astype(jnp.float32) * norm_scale
            gain_ref[place_ref[1] ^ k] = jnp.sum(part * normed, axis=0, keepdims=True)

    def scale_rows():
        normed = rows_ref[...].astype(jnp.float32) * norm_scale
        scaled_ref[...] = (normed * gain_row_ref[...]).astype(jnp.bfloat16)

    beside = [functools.partial(add_grad, k) for k in range(QUARTERS)]
    beside += [finish_grad] + [functools.partial(add_gain, k) for k in range(QUARTERS)]
    beside += [scale_rows]
    blocks = hidden_blocks(target.shape[0])
    outer_blocks(hidden_ref, grad_ref, INV_HIDDEN, blocks, target, buffer_ref, sems, beside)


def final_up(blocks, preact_grad_ref, scaled_ref, *refs):
    target, buffer_ref, sems = refs[-3:]
    outer_blocks(preact_grad_ref, scaled_ref, INV_WIDTH, blocks, target, buffer_ref, sems, [])


def struct(*shape, dtype=jnp.bfloat16):
    return jax.ShapeDtypeStruct(shape, dtype)


def call(kernel, inputs, specs, outputs, out_specs, scratch, aliases, limit, products):
    flops = sum(2 * a * b * c for a, b, c in products)
    return pl.pallas_call(
        kernel,
        out_shape=outputs,
        in_specs=specs,
        out_specs=out_specs,
        scratch_shapes=scratch,
        input_output_aliases=aliases,
        cost_estimate=pl.CostEstimate(
            flops=flops,
            bytes_accessed=sum(2 * b * c for _, b, c in products),
            transcendentals=0,
        ),
        compiler_params=pltpu.CompilerParams(vmem_limit_bytes=limit),
    )(*inputs)


def touch(place_ref, after_ref, up_ref, down_ref, place_out):
    del after_ref, up_ref, down_ref
    for i in range(place_ref.shape[0]):
        place_out[i] = place_ref[i]


def run_touch(place, after, up, down):
    return pl.pallas_call(
        touch,
        out_shape=jax.ShapeDtypeStruct(place.shape, place.dtype),
        in_specs=[SMEM, ANY, VMEM, VMEM],
        out_specs=SMEM,
        compiler_params=pltpu.CompilerParams(vmem_limit_bytes=KERNEL_BYTES),
    )(place, after, up, down)


def lay_rows(place_ref, held_ref, gain_ref, rows_ref, own_ref, own_gain_ref):
    count, micro, tokens, width = held_ref.shape
    inner = count // QUARTERS
    for outer in range(QUARTERS):
        for i in range(inner):
            block = (place_ref[2] ^ i) * QUARTERS + (place_ref[1] ^ outer)
            for j in range(micro):
                start = ((outer * inner + i) * micro + j) * tokens
                rows_ref[start : start + tokens, :] = held_ref[block, j]
    own = quarter(place_ref, 0, width // QUARTERS)
    own_ref[...] = rows_ref[:, own]
    own_gain_ref[...] = jnp.broadcast_to(gain_ref[:, own], own_gain_ref.shape)


def run_lay_rows(place, held, gain):
    rows, width = held.size // gain.size, gain.shape[1]
    return call(
        lay_rows,
        [place, held, gain],
        [SMEM, VMEM, VMEM],
        [
            struct(rows, width),
            struct(rows, width // QUARTERS),
            struct(rows, width // QUARTERS, dtype=jnp.float32),
        ],
        [VMEM] * 3,
        [],
        {},
        KERNEL_BYTES,
        [],
    )


def weight_specs(streams):
    return [ANY if streams else VMEM]


def weight_buffers(weight, quarters):
    shape = (weight.shape[0], weight.shape[1] // QUARTERS)
    return [pltpu.VMEM((count, *shape), weight.dtype) for count in quarters] + [
        pltpu.SemaphoreType.DMA((count,)) for count in quarters
    ]


def run_forward_far(section, place, pieces, gain, up, down, stash, streams):
    rows, (local, width) = pieces[0].shape[0], up.shape
    part = struct(rows, width // QUARTERS)
    first = 4 + len(pieces)
    result = call(
        functools.partial(forward_far, section, len(pieces), bool(stash), streams),
        [place, *pieces, gain, up, down, *stash],
        [SMEM] + [VMEM] * (len(pieces) + 1) + weight_specs(streams) * 2 + [ANY] * len(stash),
        [
            *[part] * len(FAR),
            struct(rows, local),
            struct(rows, width),
            struct(rows, LANES, dtype=jnp.float32),
            struct(rows, local, dtype=jnp.float32),
            struct(rows, width // QUARTERS, dtype=jnp.float32),
        ],
        [VMEM] * 4 + [ANY] * 4,
        [
            pltpu.VMEM((rows, LANES), jnp.float32),
            pltpu.VMEM((rows, local), jnp.float32),
            pltpu.VMEM((rows, width // QUARTERS), jnp.float32),
            pltpu.SemaphoreType.DMA((QUARTERS + 3,)),
            *(weight_buffers(up, [QUARTERS, len(FAR)]) if streams else []),
        ],
        {first + i: 4 + i for i in range(len(stash))},
        STREAM_BYTES if streams else KERNEL_BYTES,
        [(rows, width, local), (rows, local, 3 * width // 4)],
    )
    return (result[:3], result[3], result[4:])


def run_forward_near(section, place, hidden, down, streams):
    rows, (local, width) = hidden.shape[0], down.shape
    part = struct(rows, width // QUARTERS)
    return call(
        functools.partial(forward_near, section, streams),
        [place, hidden, down],
        [SMEM, VMEM, *weight_specs(streams)],
        [part],
        [VMEM],
        weight_buffers(down, [len(NEAR)]) if streams else [],
        {},
        KERNEL_BYTES,
        [(rows, local, width // 4)],
    )


def run_early_grad(section, place, entered, down):
    rows, (local, width) = entered.shape[0], down.shape
    return call(
        functools.partial(early_grad, section),
        [place, entered, down],
        [SMEM, VMEM, VMEM],
        [struct(rows, width), struct(rows, local, dtype=jnp.float32)],
        [ANY] * 2,
        [pltpu.VMEM((rows, local), jnp.float32), pltpu.SemaphoreType.DMA((2,))],
        {},
        KERNEL_BYTES,
        [(rows, width, local)],
    )


def run_last_far(section, place, pieces, hidden_grad, gain, up, stash):
    rows, (local, width) = pieces[0].shape[0], up.shape
    part = struct(rows, width // QUARTERS + LANES)
    result = call(
        functools.partial(last_far, section),
        [place, *pieces, hidden_grad, gain, up, *stash],
        [SMEM] + [VMEM] * (QUARTERS + 3) + [ANY] * 4,
        [
            *[part] * len(FAR),
            struct(rows, local),
            struct(rows, LANES),
            struct(rows, width),
            struct(rows, LANES, dtype=jnp.float32),
            struct(rows, local, dtype=jnp.float32),
            struct(rows, width // QUARTERS, dtype=jnp.float32),
            struct(rows, local),
            struct(QUARTERS, 1, width // QUARTERS, dtype=jnp.float32),
        ],
        [VMEM] * 5 + [ANY] * 6,
        [
            pltpu.VMEM((rows, LANES), jnp.float32),
            pltpu.VMEM((rows, local), jnp.float32),
            pltpu.VMEM((rows, width // QUARTERS), jnp.float32),
            pltpu.VMEM((len(FAR), 1, width // QUARTERS), jnp.float32),
            pltpu.SemaphoreType.DMA((QUARTERS + 7,)),
        ],
        {QUARTERS + 4 + i: 5 + i for i in range(4)},
        KERNEL_BYTES,
        [(rows, width, local), (rows, local, 3 * width // 4)],
    )
    return (result[:3], result[3:5], result[5:9], result[9:])


def run_backward_far(section, place, pieces, kept, up, down, grads):
    rows, (local, width) = pieces[0].shape[0], up.shape
    part = struct(rows, width // QUARTERS + LANES)
    result = call(
        functools.partial(backward_far, section),
        [place, *pieces, *kept, up, down, *grads],
        [SMEM] + [VMEM] * (QUARTERS + 5) + [ANY] * 3,
        [
            *[part] * len(FAR),
            struct(rows, local),
            struct(rows, LANES),
            struct(rows, width),
            struct(rows, local),
            struct(QUARTERS, 1, width // QUARTERS, dtype=jnp.float32),
        ],
        [VMEM] * 5 + [ANY] * 3,
        [
            pltpu.VMEM((len(FAR), 1, width // QUARTERS), jnp.float32),
            pltpu.SemaphoreType.DMA((QUARTERS + 4,)),
        ],
        {QUARTERS + 6 + i: 5 + i for i in range(3)},
        KERNEL_BYTES,
        [(rows, width, local), (rows, local, 3 * width // 4)],
    )
    return (result[:3], result[3:5], result[5:])


def run_backward_near(section, place, passed, kept, up, gain_part):
    rows, (local, width) = kept[0].shape[0], up.shape
    part = struct(rows, width // QUARTERS + LANES)
    result = call(
        functools.partial(backward_near, section),
        [place, *passed, kept[0], kept[1], up, gain_part],
        [SMEM] + [VMEM] * 5 + [ANY],
        [part, struct(*gain_part.shape, dtype=jnp.float32)],
        [VMEM, ANY],
        [
            pltpu.VMEM((len(NEAR), 1, width // QUARTERS), jnp.float32),
            pltpu.SemaphoreType.DMA((len(NEAR),)),
        ],
        {6: 1},
        KERNEL_BYTES,
        [(rows, local, width // 4)],
    )
    return result


def run_final(section, place, pieces, grads, kept, gain, up, down):
    rows, (local, width) = pieces[0].shape[0], up.shape
    buffers = [
        pltpu.VMEM((SLOTS, BLOCK, width), jnp.float32),
        pltpu.SemaphoreType.DMA((SLOTS,)),
    ]
    grad_down, preact_grad, gain_part, scaled = call(
        functools.partial(final_down, section),
        [place, *pieces, *grads, *kept, gain, up, down],
        [SMEM] + [VMEM] * (QUARTERS + 9),
        [
            struct(local, width, dtype=jnp.float32),
            struct(rows, local),
            struct(*grads[2].shape, dtype=jnp.float32),
            struct(rows, width),
        ],
        [ANY] + [VMEM] * 3,
        [
            pltpu.VMEM((rows, width), jnp.bfloat16),
            pltpu.VMEM((rows, local), jnp.bfloat16),
            pltpu.VMEM((local, rows), jnp.float32),
            *buffers,
        ],
        {},
        KERNEL_BYTES,
        [(rows, width, local)] * 2 + [(local, rows, width)],
    )
    blocks = hidden_blocks(local)
    taken = 0
    grad_up, total = (), gain_part.reshape(1, width)
    flips = [1 << i for i in range(lax.axis_size("dp").bit_length() - 1)]
    for i, flip in enumerate(flips):
        other = lax.ppermute(
            total, "dp", [(r, r ^ flip) for r in range(lax.axis_size("dp"))]
        )
        until = -(-len(blocks) * (i + 1) // len(flips))
        if until > taken:
            grad_up = call(
                functools.partial(final_up, blocks[taken:until]),
                [preact_grad, scaled, *grad_up],
                [VMEM, VMEM] + [ANY] * len(grad_up),
                [struct(local, width, dtype=jnp.float32)],
                [ANY],
                buffers,
                {2: 0} if grad_up else {},
                KERNEL_BYTES,
                [(local * (until - taken) // len(blocks), rows, width)],
            )
            taken = until
            if until < len(blocks):
                other, *grad_up = lax.optimization_barrier((other, *grad_up))
        total = total + other
    return (grad_up[0], grad_down, total)


def within(sections, flip):
    count = lax.axis_size("dp")
    return [(s * count + r, s * count + (r ^ flip)) for s in sections for r in range(count)]


def between(moves, flip):
    count = lax.axis_size("dp")
    return [(s * count + r, t * count + (r ^ flip)) for s, t in moves for r in range(count)]


def send_quarter(part, sections, k):
    return lax.ppermute(part, AXES, within(sections, k * (lax.axis_size("dp") // QUARTERS)))


def sum_quarters(own, arrived, sections):
    inner = lax.axis_size("dp") // QUARTERS
    total = own.astype(jnp.float32)
    for value in arrived:
        total = total + value.astype(jnp.float32)
    flip = 1
    while flip < inner:
        rounded = total.astype(jnp.bfloat16)
        other = lax.ppermute(rounded, AXES, within(sections, flip))
        total = rounded.astype(jnp.float32) + other.astype(jnp.float32)
        flip *= 2
    return total


def hand_on(own, moves):
    inner = lax.axis_size("dp") // QUARTERS
    pieces = {
        k: lax.ppermute(own, AXES, between(moves, k * inner)) for k in range(QUARTERS - 1, -1, -1)
    }
    return [pieces[k] for k in range(QUARTERS)]


def gather_chunks(chunk, sections):
    inner = lax.axis_size("dp") // QUARTERS
    pieces = {k: send_quarter(chunk, sections, k) for k in range(QUARTERS - 1, 0, -1)}
    held = along = jnp.concatenate([chunk] + [pieces[k] for k in range(1, QUARTERS)], axis=0)
    flip = 1
    while flip < inner:
        other = lax.ppermute(held, AXES, within(sections, flip))
        held = jnp.concatenate([held, other], axis=0)
        flip *= 2
    return (held, along)


def body(section_input, out_cotangent, up_weight, down_weight, norm_gain):
    section_count = lax.axis_size("section")
    section_pos = lax.axis_index("section")
    count = lax.axis_size("dp")
    position = lax.axis_index("dp")
    width = up_weight.shape[1]
    quarter_width = width // QUARTERS
    last = section_count - 1

    def alike(section):
        return [s for s in range(section_count) if s % 2 == section % 2]

    def moves(section, step):
        return [(s, s + step) for s in alike(section) if 0 <= s + step < section_count]

    inner = count // QUARTERS
    place = jnp.stack([section_pos, position // inner, position % inner]).astype(jnp.int32)
    chunk = jnp.where(section_pos == last, out_cotangent, section_input)
    chunk, place = lax.optimization_barrier((chunk[None], place))
    held, along = gather_chunks(chunk, [0, last])
    streamed_up, streamed_down = (
        pltpu.with_memory_space_constraint(weight[0].T, pltpu.HBM)
        for weight in (up_weight, down_weight)
    )
    up, down = (
        pltpu.with_memory_space_constraint(weight[0].T, pltpu.VMEM)
        for weight in (up_weight, down_weight)
    )
    place = run_touch(place, along, up, down)
    entered, own_entered, own_gain = run_lay_rows(place, held, norm_gain)

    pieces, stash, own = [entered], (), own_entered
    for section in range(last):
        here = alike(section)
        streams = section == 0
        weights = (streamed_up, streamed_down) if streams else (up, down)
        far, hidden, stash = run_forward_far(
            section, place, pieces, norm_gain, *weights, stash, streams
        )
        arrived = [send_quarter(part, here, k) for part, k in zip(far, FAR)]
        (near,) = run_forward_near(section, place, hidden, weights[1], streams)
        result = own.astype(jnp.float32) + sum_quarters(near, arrived, here)
        result = result.astype(jnp.bfloat16)
        pieces = hand_on(result, moves(section, 1))
        own = pieces[0]
        if section == 0:
            for _ in range(TOUCHES):
                place = run_touch(place, result, up, down)
            grad_rows, early = run_early_grad(last, place, entered, down)

    for section in range(last, 0, -1):
        here = alike(section)
        if section == last:
            far, passed, stash, grads = run_last_far(
                last, place, pieces, early, norm_gain, up, stash
            )
            *stash, own_normed = stash
            own_scale = stash[1][:, :1]
            grads = [grad_rows, *grads]
            own = own_entered
        else:
            far, passed, grads = run_backward_far(section, place, pieces, stash, up, down, grads)
            own = pieces[0]
        arrived = [send_quarter(part, here, k) for part, k in zip(far, FAR)]
        near, gain_part = run_backward_near(section, place, passed, stash, up, grads[2])
        grads = [grads[0], grads[1], gain_part]
        total = sum_quarters(near, arrived, here)
        along = total[:, quarter_width : quarter_width + 1] * (1.0 / width)
        normed_grad = total[:, :quarter_width] * own_gain
        result = own.astype(jnp.float32) + own_scale * (normed_grad - own_normed * along)
        pieces = hand_on(result.astype(jnp.bfloat16), moves(section, -1))

    grad_up, grad_down, grad_gain = run_final(
        0, place, pieces, grads, stash, norm_gain, up, down
    )
    return (grad_up.T[None], grad_down.T[None], grad_gain)


def solution(mesh):
    placed = (
        P(None, "dp", None),
        P(None, "dp", None),
        P("section", None, "dp"),
        P("section", None, "dp"),
        P("section", None),
    )
    return jax.shard_map(
        body,
        mesh=mesh,
        in_specs=placed,
        out_specs=(P("section", None, "dp"), P("section", None, "dp"), P("section", None)),
        check_vma=False,
    )
```

```python
import functools
import math

import jax
import jax.numpy as jnp
from jax import lax
from jax.experimental import pallas as pl
from jax.experimental.pallas import tpu as pltpu
from jax.sharding import PartitionSpec as P

D = 6656
HIDDEN_SIZE = 8960


EPSILON = 1e-05
GELU_SCALE = 0.7978845608028654
GELU_CUBIC = 0.044715

INV_WIDTH = 1.0 / math.sqrt(D)
INV_HIDDEN = 1.0 / math.sqrt(HIDDEN_SIZE)

AXES = ("section", "dp")
QUARTERS = 4
LANES = 128
BLOCK = 128
SLOTS = 3
TOUCHES = 1
KERNEL_BYTES = 18 * 1024 * 1024
STREAM_BYTES = 32 * 1024 * 1024

ANY = pl.BlockSpec(memory_space=pl.ANY)
VMEM = pl.BlockSpec(memory_space=pltpu.VMEM)
SMEM = pl.BlockSpec(memory_space=pltpu.SMEM)


def gelu_value(preact):
    inner = GELU_SCALE * (preact + GELU_CUBIC * preact * preact * preact)
    return 0.5 * preact * (1.0 + jnp.tanh(inner))


def gelu_slope(preact):
    inner = GELU_SCALE * (preact + GELU_CUBIC * preact * preact * preact)
    tangent = jnp.tanh(inner)
    return 0.5 * (1.0 + tangent) + 0.5 * preact * (1.0 - tangent * tangent) * GELU_SCALE * (
        1.0 + 3.0 * GELU_CUBIC * preact * preact
    )


def outer_rows(left, right):
    return lax.dot_general(
        left, right, (((0,), (0,)), ((), ())), preferred_element_type=jnp.float32
    )


def across_hidden(left, right):
    return lax.dot_general(
        left, right, (((1,), (1,)), ((), ())), preferred_element_type=jnp.float32
    )


def plain_product(left, right):
    return jnp.dot(left, right, preferred_element_type=jnp.float32)


FAR, NEAR = (3, 2, 1), (0,)


def quarter(place_ref, k, width):
    start = (place_ref[1] ^ k) * width
    return pl.ds(pl.multiple_of(start, LANES), width)


def read_quarter(place_ref, piece_refs, k, width):
    if len(piece_refs) == 1:
        return piece_refs[0][:, quarter(place_ref, k, width)]
    return piece_refs[k][...]


def write_out(copies):
    for copy in copies:
        copy.start()
    for copy in copies:
        copy.wait()


def quarter_copies(place_ref, piece_refs, target, sems, width):
    if len(piece_refs) == 1:
        return [pltpu.make_async_copy(piece_refs[0], target, sems.at[0])]
    return [
        pltpu.make_async_copy(ref, target.at[:, quarter(place_ref, k, width)], sems.at[k])
        for k, ref in enumerate(piece_refs)
    ]


def stream(place_ref, source, buffer_ref, sems, quarters):
    width = buffer_ref.shape[2]
    copies = {
        k: pltpu.make_async_copy(
            source.at[:, quarter(place_ref, k, width)], buffer_ref.at[at], sems.at[at]
        )
        for at, k in enumerate(quarters)
    }
    for copy in copies.values():
        copy.start()

    def read(k):
        copies[k].wait()
        return buffer_ref[list(quarters).index(k)]

    return read


def lying(place_ref, weight_ref):
    width = weight_ref.shape[1] // QUARTERS
    return lambda k: weight_ref[:, quarter(place_ref, k, width)]


def contract_width(weight, rows):
    total = None
    for k in range(QUARTERS):
        part = across_hidden(weight(k), rows(k))
        total = part if total is None else total + part
    return total.T


def enter_section(place_ref, piece_refs, gain_ref, up, width):
    squares = 0.0
    for k in range(QUARTERS):
        values = read_quarter(place_ref, piece_refs, k, width).astype(jnp.float32)
        squares = squares + jnp.sum(values * values, axis=-1, keepdims=True)
    norm_scale = lax.rsqrt(squares * (1.0 / (QUARTERS * width)) + EPSILON)

    def read(k):
        normed = read_quarter(place_ref, piece_refs, k, width).astype(jnp.float32) * norm_scale
        return (normed * gain_ref[:, quarter(place_ref, k, width)]).astype(jnp.bfloat16)

    return (norm_scale, contract_width(up, read) * INV_WIDTH)


def hidden_part(part_refs, quarters, hidden, down):
    for at, k in enumerate(quarters):
        part_refs[at][...] = (plain_product(hidden, down(k)) * INV_HIDDEN).astype(jnp.bfloat16)


def scaled_part(part_refs, quarters, preact_grad, along, rows_of, up, gain_ref):
    width = gain_ref.shape[2]
    for at, k in enumerate(quarters):
        part = plain_product(preact_grad, up(k)) * INV_WIDTH
        gain_ref[at] = jnp.sum(part * rows_of(k), axis=0, keepdims=True)
        part_refs[at][:, :width] = part.astype(jnp.bfloat16)
        part_refs[at][:, width:] = along


def along_rows(preact_grad, preact):
    total = jnp.sum(preact_grad.astype(jnp.float32) * preact, axis=-1, keepdims=True)
    return jnp.broadcast_to(total.astype(jnp.bfloat16), (total.shape[0], LANES))


def gain_copies(place_ref, gain_ref, target, quarters, sems):
    return [
        pltpu.make_async_copy(gain_ref.at[at], target.at[place_ref[1] ^ k], sems.at[at])
        for at, k in enumerate(quarters)
    ]


def forward_far(section, pieces, with_stash, streams, place_ref, *refs):
    piece_refs, refs = refs[:pieces], refs[pieces:]
    gain_ref, up_ref, down_ref = refs[:3]
    refs = refs[3 + (4 if with_stash else 0) :]
    part_refs, hidden_ref, refs = refs[:3], refs[3], refs[4:]
    rows_out, scale_out, preact_out, own_out, scale_ref, preact_ref, own_ref, sems = refs[:8]
    width = own_ref.shape[1]

    @pl.when(place_ref[0] == section)
    def _():
        if streams:
            up_buffer, down_buffer, up_sems, down_sems = refs[8:]
            up = stream(place_ref, up_ref, up_buffer, up_sems, range(QUARTERS))
            down = stream(place_ref, down_ref, down_buffer, down_sems, FAR)
        else:
            up, down = lying(place_ref, up_ref), lying(place_ref, down_ref)
        copies = quarter_copies(place_ref, piece_refs, rows_out, sems, width)
        for copy in copies:
            copy.start()
        norm_scale, preact = enter_section(
            place_ref, piece_refs, gain_ref, up, width
        )
        scale_ref[...] = jnp.broadcast_to(norm_scale, scale_ref.shape)
        preact_ref[...] = preact
        own_rows = read_quarter(place_ref, piece_refs, 0, width)
        own_ref[...] = own_rows.astype(jnp.float32) * norm_scale
        more = [
            pltpu.make_async_copy(scale_ref, scale_out, sems.at[QUARTERS]),
            pltpu.make_async_copy(preact_ref, preact_out, sems.at[QUARTERS + 1]),
            pltpu.make_async_copy(own_ref, own_out, sems.at[QUARTERS + 2]),
        ]
        for copy in more:
            copy.start()
        hidden = gelu_value(preact).astype(jnp.bfloat16)
        hidden_ref[...] = hidden
        hidden_part(part_refs, FAR, hidden, down)
        for copy in copies + more:
            copy.wait()


def forward_near(section, streams, place_ref, hidden_ref, down_ref, part_ref, *refs):
    @pl.when(place_ref[0] == section)
    def _():
        if streams:
            down = stream(place_ref, down_ref, *refs, NEAR)
        else:
            down = lying(place_ref, down_ref)
        hidden_part([part_ref], NEAR, hidden_ref[...], down)


def early_grad(
    section, place_ref, rows_ref, down_ref, grad_out, hidden_grad_out, total_ref, sems
):
    width = rows_ref.shape[1] // QUARTERS

    @pl.when(place_ref[0] == section)
    def _():
        first = pltpu.make_async_copy(rows_ref, grad_out, sems.at[0])
        first.start()
        total_ref[...] = INV_HIDDEN * contract_width(
            lying(place_ref, down_ref),
            lambda k: read_quarter(place_ref, [rows_ref], k, width),
        )
        second = pltpu.make_async_copy(total_ref, hidden_grad_out, sems.at[1])
        second.start()
        first.wait()
        second.wait()


def last_far(section, place_ref, *refs):
    piece_refs, refs = refs[:QUARTERS], refs[QUARTERS:]
    hidden_grad_ref, gain_row_ref, up_ref = refs[:3]
    refs = refs[7:]
    part_refs, preact_grad_ref, along_ref, refs = refs[:3], refs[3], refs[4], refs[5:]
    rows_out, scale_out, preact_out, own_out, preact_grad_out, gain_out = refs[:6]
    scale_ref, preact_ref, own_ref, gain_ref, sems = refs[6:]
    width = gain_ref.shape[2]
    up = lying(place_ref, up_ref)

    @pl.when(place_ref[0] == section)
    def _():
        copies = quarter_copies(place_ref, piece_refs, rows_out, sems, width)
        for copy in copies:
            copy.start()
        norm_scale, preact = enter_section(place_ref, piece_refs, gain_row_ref, up, width)
        preact_grad = (hidden_grad_ref[...] * gelu_slope(preact)).astype(jnp.bfloat16)
        along = along_rows(preact_grad, preact)
        scale_ref[...] = jnp.broadcast_to(norm_scale, scale_ref.shape)
        preact_ref[...] = preact
        preact_grad_ref[...] = preact_grad
        along_ref[...] = along
        own_ref[...] = piece_refs[0][...].astype(jnp.float32) * norm_scale
        more = [
            pltpu.make_async_copy(scale_ref, scale_out, sems.at[QUARTERS]),
            pltpu.make_async_copy(preact_ref, preact_out, sems.at[QUARTERS + 1]),
            pltpu.make_async_copy(own_ref, own_out, sems.at[QUARTERS + 2]),
            pltpu.make_async_copy(preact_grad_ref, preact_grad_out, sems.at[QUARTERS + 3]),
        ]
        for copy in more:
            copy.start()

        def rows_of(k):
            return piece_refs[k][...].astype(jnp.float32) * norm_scale

        scaled_part(part_refs, FAR, preact_grad, along, rows_of, up, gain_ref)
        write_out(gain_copies(place_ref, gain_ref, gain_out, FAR, sems.at[pl.ds(QUARTERS + 4, len(FAR))]))
        for copy in copies + more:
            copy.wait()


def backward_far(section, place_ref, *refs):
    piece_refs, refs = refs[:QUARTERS], refs[QUARTERS:]
    rows_ref, scale_ref, preact_ref, up_ref, down_ref = refs[:5]
    refs = refs[8:]
    part_refs, preact_grad_ref, along_ref, refs = refs[:3], refs[3], refs[4], refs[5:]
    grad_out, preact_grad_out, gain_out, gain_ref, sems = refs
    width = gain_ref.shape[2]

    @pl.when(place_ref[0] == section)
    def _():
        copies = quarter_copies(place_ref, piece_refs, grad_out, sems, width)
        for copy in copies:
            copy.start()
        hidden_grad = INV_HIDDEN * contract_width(
            lying(place_ref, down_ref), lambda k: piece_refs[k][...]
        )
        preact = preact_ref[...]
        preact_grad = (hidden_grad * gelu_slope(preact)).astype(jnp.bfloat16)
        along = along_rows(preact_grad, preact)
        preact_grad_ref[...] = preact_grad
        along_ref[...] = along
        more = pltpu.make_async_copy(preact_grad_ref, preact_grad_out, sems.at[QUARTERS])
        more.start()
        norm_scale = scale_ref[:, :1]

        def rows_of(k):
            return rows_ref[:, quarter(place_ref, k, width)].astype(jnp.float32) * norm_scale

        up = lying(place_ref, up_ref)
        scaled_part(part_refs, FAR, preact_grad, along, rows_of, up, gain_ref)
        write_out(gain_copies(place_ref, gain_ref, gain_out, FAR, sems.at[pl.ds(QUARTERS + 1, len(FAR))]))
        for copy in copies + [more]:
            copy.wait()


def backward_near(
    section, place_ref, preact_grad_ref, along_ref, rows_ref, scale_ref, up_ref, gain_in,
    part_ref, gain_out, gain_ref, sems,
):
    del gain_in
    width = gain_ref.shape[2]

    @pl.when(place_ref[0] == section)
    def _():
        norm_scale = scale_ref[:, :1]

        def rows_of(k):
            return rows_ref[:, quarter(place_ref, k, width)].astype(jnp.float32) * norm_scale

        scaled_part(
            [part_ref], NEAR, preact_grad_ref[...], along_ref[...],
            rows_of, lying(place_ref, up_ref), gain_ref,
        )
        write_out(gain_copies(place_ref, gain_ref, gain_out, NEAR, sems))


def hidden_blocks(local):
    return [(start, min(BLOCK, local - start)) for start in range(0, local, BLOCK)]


def outer_blocks(left_ref, right_ref, factor, blocks, target, buffer_ref, sems, beside):
    copies = []
    for i, (start, size) in enumerate(blocks):
        slot = i % SLOTS
        if i >= SLOTS:
            copies[i - SLOTS].wait()
        value = outer_rows(left_ref[:, start : start + size], right_ref[...])
        buffer_ref[slot, :size] = value * factor
        copy = pltpu.make_async_copy(
            buffer_ref.at[slot, pl.ds(0, size)], target.at[pl.ds(start, size)], sems.at[slot]
        )
        copy.start()
        copies.append(copy)
        if i < len(beside):
            beside[i]()
    for run in beside[len(blocks) :]:
        run()
    for copy in copies[-SLOTS:]:
        copy.wait()


def final_down(section, place_ref, *refs):
    piece_refs, refs = refs[:QUARTERS], refs[QUARTERS:]
    grad_in, preact_grad_in, gain_in, rows_ref, scale_ref, preact_ref, gain_row_ref = refs[:7]
    up_ref, down_ref = refs[7:9]
    target, preact_grad_ref, gain_ref, scaled_ref = refs[9:13]
    grad_ref, hidden_ref, hidden_grad_ref, buffer_ref, sems = refs[13:]
    width = gain_ref.shape[2]
    up, down = lying(place_ref, up_ref), lying(place_ref, down_ref)
    active = place_ref[0] == section

    @pl.when(active)
    def _():
        for k in range(QUARTERS):
            grad_ref[:, quarter(place_ref, k, width)] = piece_refs[k][...]

    @pl.when(jnp.logical_not(active))
    def _():
        grad_ref[...] = grad_in[...]
        preact_grad_ref[...] = preact_grad_in[...]
        gain_ref[...] = gain_in[...]

    norm_scale = scale_ref[:, :1]
    hidden_ref[...] = gelu_value(preact_ref[...]).astype(jnp.bfloat16)

    def add_grad(k):
        @pl.when(active)
        def _():
            part = across_hidden(down(k), piece_refs[k][...])
            hidden_grad_ref[...] = part if k == 0 else hidden_grad_ref[...] + part

    def finish_grad():
        @pl.when(active)
        def _():
            hidden_grad = hidden_grad_ref[...].T * INV_HIDDEN
            preact_grad_ref[...] = (hidden_grad * gelu_slope(preact_ref[...])).astype(jnp.bfloat16)

    def add_gain(k):
        @pl.when(active)
        def _():
            part = plain_product(preact_grad_ref[...], up(k)) * INV_WIDTH
            rows = rows_ref[:, quarter(place_ref, k, width)]
            normed = rows.astype(jnp.float32) * norm_scale
            gain_ref[place_ref[1] ^ k] = jnp.sum(part * normed, axis=0, keepdims=True)

    def scale_rows():
        normed = rows_ref[...].astype(jnp.float32) * norm_scale
        scaled_ref[...] = (normed * gain_row_ref[...]).astype(jnp.bfloat16)

    beside = [functools.partial(add_grad, k) for k in range(QUARTERS)]
    beside += [finish_grad] + [functools.partial(add_gain, k) for k in range(QUARTERS)]
    beside += [scale_rows]
    blocks = hidden_blocks(target.shape[0])
    outer_blocks(hidden_ref, grad_ref, INV_HIDDEN, blocks, target, buffer_ref, sems, beside)


def final_up(blocks, preact_grad_ref, scaled_ref, *refs):
    target, buffer_ref, sems = refs[-3:]
    outer_blocks(preact_grad_ref, scaled_ref, INV_WIDTH, blocks, target, buffer_ref, sems, [])


def struct(*shape, dtype=jnp.bfloat16):
    return jax.ShapeDtypeStruct(shape, dtype)


def call(kernel, inputs, specs, outputs, out_specs, scratch, aliases, limit, products):
    flops = sum(2 * a * b * c for a, b, c in products)
    return pl.pallas_call(
        kernel,
        out_shape=outputs,
        in_specs=specs,
        out_specs=out_specs,
        scratch_shapes=scratch,
        input_output_aliases=aliases,
        cost_estimate=pl.CostEstimate(
            flops=flops,
            bytes_accessed=sum(2 * b * c for _, b, c in products),
            transcendentals=0,
        ),
        compiler_params=pltpu.CompilerParams(vmem_limit_bytes=limit),
    )(*inputs)


def touch(place_ref, *refs):
    place_out = refs[-1]
    for i in range(place_ref.shape[0]):
        place_out[i] = place_ref[i]


def run_touch(place, after, *weights):
    return pl.pallas_call(
        touch,
        out_shape=jax.ShapeDtypeStruct(place.shape, place.dtype),
        in_specs=[SMEM, ANY] + [VMEM] * len(weights),
        out_specs=SMEM,
        compiler_params=pltpu.CompilerParams(vmem_limit_bytes=KERNEL_BYTES),
    )(place, after, *weights)


def lay_rows(place_ref, held_ref, gain_ref, rows_ref, own_ref, own_gain_ref):
    count, micro, tokens, width = held_ref.shape
    inner = count // QUARTERS
    for outer in range(QUARTERS):
        for i in range(inner):
            block = (place_ref[2] ^ i) * QUARTERS + (place_ref[1] ^ outer)
            for j in range(micro):
                start = ((outer * inner + i) * micro + j) * tokens
                rows_ref[start : start + tokens, :] = held_ref[block, j]
    own = quarter(place_ref, 0, width // QUARTERS)
    own_ref[...] = rows_ref[:, own]
    own_gain_ref[...] = jnp.broadcast_to(gain_ref[:, own], own_gain_ref.shape)


def run_lay_rows(place, held, gain):
    rows, width = held.size // gain.size, gain.shape[1]
    return call(
        lay_rows,
        [place, held, gain],
        [SMEM, VMEM, VMEM],
        [
            struct(rows, width),
            struct(rows, width // QUARTERS),
            struct(rows, width // QUARTERS, dtype=jnp.float32),
        ],
        [VMEM] * 3,
        [],
        {},
        KERNEL_BYTES,
        [],
    )


def weight_specs(streams):
    return [ANY if streams else VMEM]


def weight_buffers(weight, quarters):
    shape = (weight.shape[0], weight.shape[1] // QUARTERS)
    return [pltpu.VMEM((count, *shape), weight.dtype) for count in quarters] + [
        pltpu.SemaphoreType.DMA((count,)) for count in quarters
    ]


def run_forward_far(section, place, pieces, gain, up, down, stash, streams):
    rows, (local, width) = pieces[0].shape[0], up.shape
    part = struct(rows, width // QUARTERS)
    first = 4 + len(pieces)
    result = call(
        functools.partial(forward_far, section, len(pieces), bool(stash), streams),
        [place, *pieces, gain, up, down, *stash],
        [SMEM] + [VMEM] * (len(pieces) + 1) + weight_specs(streams) * 2 + [ANY] * len(stash),
        [
            *[part] * len(FAR),
            struct(rows, local),
            struct(rows, width),
            struct(rows, LANES, dtype=jnp.float32),
            struct(rows, local, dtype=jnp.float32),
            struct(rows, width // QUARTERS, dtype=jnp.float32),
        ],
        [VMEM] * 4 + [ANY] * 4,
        [
            pltpu.VMEM((rows, LANES), jnp.float32),
            pltpu.VMEM((rows, local), jnp.float32),
            pltpu.VMEM((rows, width // QUARTERS), jnp.float32),
            pltpu.SemaphoreType.DMA((QUARTERS + 3,)),
            *(weight_buffers(up, [QUARTERS, len(FAR)]) if streams else []),
        ],
        {first + i: 4 + i for i in range(len(stash))},
        STREAM_BYTES if streams else KERNEL_BYTES,
        [(rows, width, local), (rows, local, 3 * width // 4)],
    )
    return (result[:3], result[3], result[4:])


def run_forward_near(section, place, hidden, down, streams):
    rows, (local, width) = hidden.shape[0], down.shape
    part = struct(rows, width // QUARTERS)
    return call(
        functools.partial(forward_near, section, streams),
        [place, hidden, down],
        [SMEM, VMEM, *weight_specs(streams)],
        [part],
        [VMEM],
        weight_buffers(down, [len(NEAR)]) if streams else [],
        {},
        KERNEL_BYTES,
        [(rows, local, width // 4)],
    )


def run_early_grad(section, place, entered, down):
    rows, (local, width) = entered.shape[0], down.shape
    return call(
        functools.partial(early_grad, section),
        [place, entered, down],
        [SMEM, VMEM, VMEM],
        [struct(rows, width), struct(rows, local, dtype=jnp.float32)],
        [ANY] * 2,
        [pltpu.VMEM((rows, local), jnp.float32), pltpu.SemaphoreType.DMA((2,))],
        {},
        KERNEL_BYTES,
        [(rows, width, local)],
    )


def run_last_far(section, place, pieces, hidden_grad, gain, up, stash):
    rows, (local, width) = pieces[0].shape[0], up.shape
    part = struct(rows, width // QUARTERS + LANES)
    result = call(
        functools.partial(last_far, section),
        [place, *pieces, hidden_grad, gain, up, *stash],
        [SMEM] + [VMEM] * (QUARTERS + 3) + [ANY] * 4,
        [
            *[part] * len(FAR),
            struct(rows, local),
            struct(rows, LANES),
            struct(rows, width),
            struct(rows, LANES, dtype=jnp.float32),
            struct(rows, local, dtype=jnp.float32),
            struct(rows, width // QUARTERS, dtype=jnp.float32),
            struct(rows, local),
            struct(QUARTERS, 1, width // QUARTERS, dtype=jnp.float32),
        ],
        [VMEM] * 5 + [ANY] * 6,
        [
            pltpu.VMEM((rows, LANES), jnp.float32),
            pltpu.VMEM((rows, local), jnp.float32),
            pltpu.VMEM((rows, width // QUARTERS), jnp.float32),
            pltpu.VMEM((len(FAR), 1, width // QUARTERS), jnp.float32),
            pltpu.SemaphoreType.DMA((QUARTERS + 7,)),
        ],
        {QUARTERS + 4 + i: 5 + i for i in range(4)},
        KERNEL_BYTES,
        [(rows, width, local), (rows, local, 3 * width // 4)],
    )
    return (result[:3], result[3:5], result[5:9], result[9:])


def run_backward_far(section, place, pieces, kept, up, down, grads):
    rows, (local, width) = pieces[0].shape[0], up.shape
    part = struct(rows, width // QUARTERS + LANES)
    result = call(
        functools.partial(backward_far, section),
        [place, *pieces, *kept, up, down, *grads],
        [SMEM] + [VMEM] * (QUARTERS + 5) + [ANY] * 3,
        [
            *[part] * len(FAR),
            struct(rows, local),
            struct(rows, LANES),
            struct(rows, width),
            struct(rows, local),
            struct(QUARTERS, 1, width // QUARTERS, dtype=jnp.float32),
        ],
        [VMEM] * 5 + [ANY] * 3,
        [
            pltpu.VMEM((len(FAR), 1, width // QUARTERS), jnp.float32),
            pltpu.SemaphoreType.DMA((QUARTERS + 4,)),
        ],
        {QUARTERS + 6 + i: 5 + i for i in range(3)},
        KERNEL_BYTES,
        [(rows, width, local), (rows, local, 3 * width // 4)],
    )
    return (result[:3], result[3:5], result[5:])


def run_backward_near(section, place, passed, kept, up, gain_part):
    rows, (local, width) = kept[0].shape[0], up.shape
    part = struct(rows, width // QUARTERS + LANES)
    result = call(
        functools.partial(backward_near, section),
        [place, *passed, kept[0], kept[1], up, gain_part],
        [SMEM] + [VMEM] * 5 + [ANY],
        [part, struct(*gain_part.shape, dtype=jnp.float32)],
        [VMEM, ANY],
        [
            pltpu.VMEM((len(NEAR), 1, width // QUARTERS), jnp.float32),
            pltpu.SemaphoreType.DMA((len(NEAR),)),
        ],
        {6: 1},
        KERNEL_BYTES,
        [(rows, local, width // 4)],
    )
    return result


def run_final(section, place, pieces, grads, kept, gain, up, down):
    rows, (local, width) = pieces[0].shape[0], up.shape
    buffers = [
        pltpu.VMEM((SLOTS, BLOCK, width), jnp.float32),
        pltpu.SemaphoreType.DMA((SLOTS,)),
    ]
    grad_down, preact_grad, gain_part, scaled = call(
        functools.partial(final_down, section),
        [place, *pieces, *grads, *kept, gain, up, down],
        [SMEM] + [VMEM] * (QUARTERS + 9),
        [
            struct(local, width, dtype=jnp.float32),
            struct(rows, local),
            struct(*grads[2].shape, dtype=jnp.float32),
            struct(rows, width),
        ],
        [ANY] + [VMEM] * 3,
        [
            pltpu.VMEM((rows, width), jnp.bfloat16),
            pltpu.VMEM((rows, local), jnp.bfloat16),
            pltpu.VMEM((local, rows), jnp.float32),
            *buffers,
        ],
        {},
        KERNEL_BYTES,
        [(rows, width, local)] * 2 + [(local, rows, width)],
    )
    blocks = hidden_blocks(local)
    taken = 0
    grad_up, total = (), gain_part.reshape(1, width)
    flips = [1 << i for i in range(lax.axis_size("dp").bit_length() - 1)]
    for i, flip in enumerate(flips):
        other = lax.ppermute(
            total, "dp", [(r, r ^ flip) for r in range(lax.axis_size("dp"))]
        )
        until = -(-len(blocks) * (i + 1) // len(flips))
        if until > taken:
            grad_up = call(
                functools.partial(final_up, blocks[taken:until]),
                [preact_grad, scaled, *grad_up],
                [VMEM, VMEM] + [ANY] * len(grad_up),
                [struct(local, width, dtype=jnp.float32)],
                [ANY],
                buffers,
                {2: 0} if grad_up else {},
                KERNEL_BYTES,
                [(local * (until - taken) // len(blocks), rows, width)],
            )
            taken = until
            if until < len(blocks):
                other, *grad_up = lax.optimization_barrier((other, *grad_up))
        total = total + other
    return (grad_up[0], grad_down, total)


def within(sections, flip):
    count = lax.axis_size("dp")
    return [(s * count + r, s * count + (r ^ flip)) for s in sections for r in range(count)]


def between(moves, flip):
    count = lax.axis_size("dp")
    return [(s * count + r, t * count + (r ^ flip)) for s, t in moves for r in range(count)]


def send_quarter(part, sections, k):
    return lax.ppermute(part, AXES, within(sections, k * (lax.axis_size("dp") // QUARTERS)))


def sum_quarters(own, arrived, sections):
    inner = lax.axis_size("dp") // QUARTERS
    total = own.astype(jnp.float32)
    for value in arrived:
        total = total + value.astype(jnp.float32)
    flip = 1
    while flip < inner:
        rounded = total.astype(jnp.bfloat16)
        other = lax.ppermute(rounded, AXES, within(sections, flip))
        total = rounded.astype(jnp.float32) + other.astype(jnp.float32)
        flip *= 2
    return (total, rounded)


def hand_on(own, moves):
    inner = lax.axis_size("dp") // QUARTERS
    pieces = {
        k: lax.ppermute(own, AXES, between(moves, k * inner)) for k in range(QUARTERS - 1, -1, -1)
    }
    return [pieces[k] for k in range(QUARTERS)]


def gather_chunks(chunk, sections):
    inner = lax.axis_size("dp") // QUARTERS
    pieces = {k: send_quarter(chunk, sections, k) for k in range(QUARTERS - 1, 0, -1)}
    held = along = jnp.concatenate([chunk] + [pieces[k] for k in range(1, QUARTERS)], axis=0)
    flip = 1
    while flip < inner:
        other = lax.ppermute(held, AXES, within(sections, flip))
        held = jnp.concatenate([held, other], axis=0)
        flip *= 2
    return (held, along)


def body(section_input, out_cotangent, up_weight, down_weight, norm_gain):
    section_count = lax.axis_size("section")
    section_pos = lax.axis_index("section")
    count = lax.axis_size("dp")
    position = lax.axis_index("dp")
    width = up_weight.shape[1]
    quarter_width = width // QUARTERS
    last = section_count - 1

    def alike(section):
        return [s for s in range(section_count) if s % 2 == section % 2]

    def moves(section, step):
        return [(s, s + step) for s in alike(section) if 0 <= s + step < section_count]

    inner = count // QUARTERS
    place = jnp.stack([section_pos, position // inner, position % inner]).astype(jnp.int32)
    chunk = jnp.where(section_pos == last, out_cotangent, section_input)
    chunk, place = lax.optimization_barrier((chunk[None], place))
    held, along = gather_chunks(chunk, [0, last])
    streamed_up, streamed_down = (
        pltpu.with_memory_space_constraint(weight[0].T, pltpu.HBM)
        for weight in (up_weight, down_weight)
    )
    up, down = (
        pltpu.with_memory_space_constraint(weight[0].T, pltpu.VMEM)
        for weight in (up_weight, down_weight)
    )
    place = run_touch(place, along, down)
    entered, own_entered, own_gain = run_lay_rows(place, held, norm_gain)

    pieces, stash, own = [entered], (), own_entered
    for section in range(last):
        here = alike(section)
        streams = section == 0
        weights = (streamed_up, streamed_down) if streams else (up, down)
        far, hidden, stash = run_forward_far(
            section, place, pieces, norm_gain, *weights, stash, streams
        )
        arrived = [send_quarter(part, here, k) for part, k in zip(far, FAR)]
        (near,) = run_forward_near(section, place, hidden, weights[1], streams)
        total, sent = sum_quarters(near, arrived, here)
        result = own.astype(jnp.float32) + total
        if section == 0:
            place = run_touch(place, sent, up)
        result = result.astype(jnp.bfloat16)
        pieces = hand_on(result, moves(section, 1))
        own = pieces[0]
        if section == 0:
            for _ in range(TOUCHES):
                place = run_touch(place, result, up, down)
            grad_rows, early = run_early_grad(last, place, entered, down)

    for section in range(last, 0, -1):
        here = alike(section)
        if section == last:
            far, passed, stash, grads = run_last_far(
                last, place, pieces, early, norm_gain, up, stash
            )
            *stash, own_normed = stash
            own_scale = stash[1][:, :1]
            grads = [grad_rows, *grads]
            own = own_entered
        else:
            far, passed, grads = run_backward_far(section, place, pieces, stash, up, down, grads)
            own = pieces[0]
        arrived = [send_quarter(part, here, k) for part, k in zip(far, FAR)]
        near, gain_part = run_backward_near(section, place, passed, stash, up, grads[2])
        grads = [grads[0], grads[1], gain_part]
        total, _ = sum_quarters(near, arrived, here)
        along = total[:, quarter_width : quarter_width + 1] * (1.0 / width)
        normed_grad = total[:, :quarter_width] * own_gain
        result = own.astype(jnp.float32) + own_scale * (normed_grad - own_normed * along)
        result = result.astype(jnp.bfloat16)
        pieces = hand_on(result, moves(section, -1))
        if section == last:
            place = run_touch(place, result, up, down)

    grad_up, grad_down, grad_gain = run_final(
        0, place, pieces, grads, stash, norm_gain, up, down
    )
    return (grad_up.T[None], grad_down.T[None], grad_gain)


def solution(mesh):
    placed = (
        P(None, "dp", None),
        P(None, "dp", None),
        P("section", None, "dp"),
        P("section", None, "dp"),
        P("section", None),
    )
    return jax.shard_map(
        body,
        mesh=mesh,
        in_specs=placed,
        out_specs=(P("section", None, "dp"), P("section", None, "dp"), P("section", None)),
        check_vma=False,
    )
```

```python
import functools
import math

import jax
import jax.numpy as jnp
from jax import lax
from jax.experimental import pallas as pl
from jax.experimental.pallas import tpu as pltpu
from jax.sharding import PartitionSpec as P

D = 6656
HIDDEN_SIZE = 8960


EPSILON = 1e-05
GELU_SCALE = 0.7978845608028654
GELU_CUBIC = 0.044715

INV_WIDTH = 1.0 / math.sqrt(D)
INV_HIDDEN = 1.0 / math.sqrt(HIDDEN_SIZE)

AXES = ("section", "dp")
QUARTERS = 4
LANES = 128
BLOCK = 128
SLOTS = 3
TOUCHES = 1
KERNEL_BYTES = 18 * 1024 * 1024
STREAM_BYTES = 32 * 1024 * 1024

ANY = pl.BlockSpec(memory_space=pl.ANY)
VMEM = pl.BlockSpec(memory_space=pltpu.VMEM)
SMEM = pl.BlockSpec(memory_space=pltpu.SMEM)


def gelu_value(preact):
    inner = GELU_SCALE * (preact + GELU_CUBIC * preact * preact * preact)
    return 0.5 * preact * (1.0 + jnp.tanh(inner))


def gelu_slope(preact):
    inner = GELU_SCALE * (preact + GELU_CUBIC * preact * preact * preact)
    tangent = jnp.tanh(inner)
    return 0.5 * (1.0 + tangent) + 0.5 * preact * (1.0 - tangent * tangent) * GELU_SCALE * (
        1.0 + 3.0 * GELU_CUBIC * preact * preact
    )


def outer_rows(left, right):
    return lax.dot_general(
        left, right, (((0,), (0,)), ((), ())), preferred_element_type=jnp.float32
    )


def across_hidden(left, right):
    return lax.dot_general(
        left, right, (((1,), (1,)), ((), ())), preferred_element_type=jnp.float32
    )


def plain_product(left, right):
    return jnp.dot(left, right, preferred_element_type=jnp.float32)


FAR, NEAR = (3, 2, 1), (0,)


def quarter(place_ref, k, width):
    start = (place_ref[1] ^ k) * width
    return pl.ds(pl.multiple_of(start, LANES), width)


def read_quarter(place_ref, piece_refs, k, width):
    if len(piece_refs) == 1:
        return piece_refs[0][:, quarter(place_ref, k, width)]
    return piece_refs[k][...]


def write_out(copies):
    for copy in copies:
        copy.start()
    for copy in copies:
        copy.wait()


def quarter_copies(place_ref, piece_refs, target, sems, width):
    if len(piece_refs) == 1:
        return [pltpu.make_async_copy(piece_refs[0], target, sems.at[0])]
    return [
        pltpu.make_async_copy(ref, target.at[:, quarter(place_ref, k, width)], sems.at[k])
        for k, ref in enumerate(piece_refs)
    ]


def stream(place_ref, source, buffer_ref, sems, quarters):
    width = buffer_ref.shape[2]
    copies = {
        k: pltpu.make_async_copy(
            source.at[:, quarter(place_ref, k, width)], buffer_ref.at[at], sems.at[at]
        )
        for at, k in enumerate(quarters)
    }
    for copy in copies.values():
        copy.start()

    def read(k):
        copies[k].wait()
        return buffer_ref[list(quarters).index(k)]

    return read


def lying(place_ref, weight_ref):
    width = weight_ref.shape[1] // QUARTERS
    return lambda k: weight_ref[:, quarter(place_ref, k, width)]


def contract_width(weight, rows):
    total = None
    for k in range(QUARTERS):
        part = across_hidden(weight(k), rows(k))
        total = part if total is None else total + part
    return total.T


def enter_section(place_ref, piece_refs, gain_ref, up, width):
    squares = 0.0
    for k in range(QUARTERS):
        values = read_quarter(place_ref, piece_refs, k, width).astype(jnp.float32)
        squares = squares + jnp.sum(values * values, axis=-1, keepdims=True)
    norm_scale = lax.rsqrt(squares * (1.0 / (QUARTERS * width)) + EPSILON)

    def read(k):
        normed = read_quarter(place_ref, piece_refs, k, width).astype(jnp.float32) * norm_scale
        return (normed * gain_ref[:, quarter(place_ref, k, width)]).astype(jnp.bfloat16)

    return (norm_scale, contract_width(up, read) * INV_WIDTH)


def hidden_part(part_refs, quarters, hidden, down):
    for at, k in enumerate(quarters):
        part_refs[at][...] = (plain_product(hidden, down(k)) * INV_HIDDEN).astype(jnp.bfloat16)


def scaled_part(part_refs, quarters, preact_grad, along, rows_of, up, gain_ref):
    width = gain_ref.shape[2]
    for at, k in enumerate(quarters):
        part = plain_product(preact_grad, up(k)) * INV_WIDTH
        gain_ref[at] = jnp.sum(part * rows_of(k), axis=0, keepdims=True)
        part_refs[at][:, :width] = part.astype(jnp.bfloat16)
        part_refs[at][:, width:] = along


def along_rows(preact_grad, preact):
    total = jnp.sum(preact_grad.astype(jnp.float32) * preact, axis=-1, keepdims=True)
    return jnp.broadcast_to(total.astype(jnp.bfloat16), (total.shape[0], LANES))


def gain_copies(place_ref, gain_ref, target, quarters, sems):
    return [
        pltpu.make_async_copy(gain_ref.at[at], target.at[place_ref[1] ^ k], sems.at[at])
        for at, k in enumerate(quarters)
    ]


def forward_far(section, pieces, with_stash, streams, place_ref, *refs):
    piece_refs, refs = refs[:pieces], refs[pieces:]
    gain_ref, up_ref, down_ref = refs[:3]
    refs = refs[3 + (4 if with_stash else 0) :]
    part_refs, hidden_ref, refs = refs[:3], refs[3], refs[4:]
    rows_out, scale_out, preact_out, own_out, scale_ref, preact_ref, own_ref, sems = refs[:8]
    width = own_ref.shape[1]

    @pl.when(place_ref[0] == section)
    def _():
        if streams:
            up_buffer, down_buffer, up_sems, down_sems = refs[8:]
            up = stream(place_ref, up_ref, up_buffer, up_sems, range(QUARTERS))
            down = stream(place_ref, down_ref, down_buffer, down_sems, FAR)
        else:
            up, down = lying(place_ref, up_ref), lying(place_ref, down_ref)
        copies = quarter_copies(place_ref, piece_refs, rows_out, sems, width)
        for copy in copies:
            copy.start()
        norm_scale, preact = enter_section(
            place_ref, piece_refs, gain_ref, up, width
        )
        scale_ref[...] = jnp.broadcast_to(norm_scale, scale_ref.shape)
        preact_ref[...] = preact
        own_rows = read_quarter(place_ref, piece_refs, 0, width)
        own_ref[...] = own_rows.astype(jnp.float32) * norm_scale
        more = [
            pltpu.make_async_copy(scale_ref, scale_out, sems.at[QUARTERS]),
            pltpu.make_async_copy(preact_ref, preact_out, sems.at[QUARTERS + 1]),
            pltpu.make_async_copy(own_ref, own_out, sems.at[QUARTERS + 2]),
        ]
        for copy in more:
            copy.start()
        hidden = gelu_value(preact).astype(jnp.bfloat16)
        hidden_ref[...] = hidden
        hidden_part(part_refs, FAR, hidden, down)
        for copy in copies + more:
            copy.wait()


def forward_near(section, streams, place_ref, hidden_ref, down_ref, part_ref, *refs):
    @pl.when(place_ref[0] == section)
    def _():
        if streams:
            down = stream(place_ref, down_ref, *refs, NEAR)
        else:
            down = lying(place_ref, down_ref)
        hidden_part([part_ref], NEAR, hidden_ref[...], down)


def early_grad(
    section, place_ref, rows_ref, down_ref, grad_out, hidden_grad_out, total_ref, sems
):
    width = rows_ref.shape[1] // QUARTERS

    @pl.when(place_ref[0] == section)
    def _():
        first = pltpu.make_async_copy(rows_ref, grad_out, sems.at[0])
        first.start()
        total_ref[...] = INV_HIDDEN * contract_width(
            lying(place_ref, down_ref),
            lambda k: read_quarter(place_ref, [rows_ref], k, width),
        )
        second = pltpu.make_async_copy(total_ref, hidden_grad_out, sems.at[1])
        second.start()
        first.wait()
        second.wait()


def last_far(section, place_ref, *refs):
    piece_refs, refs = refs[:QUARTERS], refs[QUARTERS:]
    hidden_grad_ref, gain_row_ref, up_ref = refs[:3]
    refs = refs[7:]
    part_refs, preact_grad_ref, along_ref, refs = refs[:3], refs[3], refs[4], refs[5:]
    rows_out, scale_out, preact_out, own_out, preact_grad_out, gain_out = refs[:6]
    scale_ref, preact_ref, own_ref, gain_ref, sems = refs[6:]
    width = gain_ref.shape[2]
    up = lying(place_ref, up_ref)

    @pl.when(place_ref[0] == section)
    def _():
        copies = quarter_copies(place_ref, piece_refs, rows_out, sems, width)
        for copy in copies:
            copy.start()
        norm_scale, preact = enter_section(place_ref, piece_refs, gain_row_ref, up, width)
        preact_grad = (hidden_grad_ref[...] * gelu_slope(preact)).astype(jnp.bfloat16)
        along = along_rows(preact_grad, preact)
        scale_ref[...] = jnp.broadcast_to(norm_scale, scale_ref.shape)
        preact_ref[...] = preact
        preact_grad_ref[...] = preact_grad
        along_ref[...] = along
        own_ref[...] = piece_refs[0][...].astype(jnp.float32) * norm_scale
        more = [
            pltpu.make_async_copy(scale_ref, scale_out, sems.at[QUARTERS]),
            pltpu.make_async_copy(preact_ref, preact_out, sems.at[QUARTERS + 1]),
            pltpu.make_async_copy(own_ref, own_out, sems.at[QUARTERS + 2]),
            pltpu.make_async_copy(preact_grad_ref, preact_grad_out, sems.at[QUARTERS + 3]),
        ]
        for copy in more:
            copy.start()

        def rows_of(k):
            return piece_refs[k][...].astype(jnp.float32) * norm_scale

        scaled_part(part_refs, FAR, preact_grad, along, rows_of, up, gain_ref)
        write_out(gain_copies(place_ref, gain_ref, gain_out, FAR, sems.at[pl.ds(QUARTERS + 4, len(FAR))]))
        for copy in copies + more:
            copy.wait()


def backward_far(section, place_ref, *refs):
    piece_refs, refs = refs[:QUARTERS], refs[QUARTERS:]
    rows_ref, scale_ref, preact_ref, up_ref, down_ref = refs[:5]
    refs = refs[8:]
    part_refs, preact_grad_ref, along_ref, refs = refs[:3], refs[3], refs[4], refs[5:]
    grad_out, preact_grad_out, gain_out, gain_ref, sems = refs
    width = gain_ref.shape[2]

    @pl.when(place_ref[0] == section)
    def _():
        copies = quarter_copies(place_ref, piece_refs, grad_out, sems, width)
        for copy in copies:
            copy.start()
        hidden_grad = INV_HIDDEN * contract_width(
            lying(place_ref, down_ref), lambda k: piece_refs[k][...]
        )
        preact = preact_ref[...]
        preact_grad = (hidden_grad * gelu_slope(preact)).astype(jnp.bfloat16)
        along = along_rows(preact_grad, preact)
        preact_grad_ref[...] = preact_grad
        along_ref[...] = along
        more = pltpu.make_async_copy(preact_grad_ref, preact_grad_out, sems.at[QUARTERS])
        more.start()
        norm_scale = scale_ref[:, :1]

        def rows_of(k):
            return rows_ref[:, quarter(place_ref, k, width)].astype(jnp.float32) * norm_scale

        up = lying(place_ref, up_ref)
        scaled_part(part_refs, FAR, preact_grad, along, rows_of, up, gain_ref)
        write_out(gain_copies(place_ref, gain_ref, gain_out, FAR, sems.at[pl.ds(QUARTERS + 1, len(FAR))]))
        for copy in copies + [more]:
            copy.wait()


def backward_near(
    section, place_ref, preact_grad_ref, along_ref, rows_ref, scale_ref, up_ref, gain_in,
    part_ref, gain_out, gain_ref, sems,
):
    del gain_in
    width = gain_ref.shape[2]

    @pl.when(place_ref[0] == section)
    def _():
        norm_scale = scale_ref[:, :1]

        def rows_of(k):
            return rows_ref[:, quarter(place_ref, k, width)].astype(jnp.float32) * norm_scale

        scaled_part(
            [part_ref], NEAR, preact_grad_ref[...], along_ref[...],
            rows_of, lying(place_ref, up_ref), gain_ref,
        )
        write_out(gain_copies(place_ref, gain_ref, gain_out, NEAR, sems))


def hidden_blocks(local):
    return [(start, min(BLOCK, local - start)) for start in range(0, local, BLOCK)]


def outer_blocks(left_ref, right_ref, factor, blocks, target, buffer_ref, sems, beside):
    copies = []
    for i, (start, size) in enumerate(blocks):
        slot = i % SLOTS
        if i >= SLOTS:
            copies[i - SLOTS].wait()
        value = outer_rows(left_ref[:, start : start + size], right_ref[...])
        buffer_ref[slot, :size] = value * factor
        copy = pltpu.make_async_copy(
            buffer_ref.at[slot, pl.ds(0, size)], target.at[pl.ds(start, size)], sems.at[slot]
        )
        copy.start()
        copies.append(copy)
        if i < len(beside):
            beside[i]()
    for run in beside[len(blocks) :]:
        run()
    for copy in copies[-SLOTS:]:
        copy.wait()


def final_down(section, place_ref, *refs):
    piece_refs, refs = refs[:QUARTERS], refs[QUARTERS:]
    grad_in, preact_grad_in, gain_in, rows_ref, scale_ref, preact_ref, gain_row_ref = refs[:7]
    up_ref, down_ref = refs[7:9]
    target, preact_grad_ref, gain_ref, scaled_ref = refs[9:13]
    grad_ref, hidden_ref, hidden_grad_ref, buffer_ref, sems = refs[13:]
    width = gain_ref.shape[2]
    up, down = lying(place_ref, up_ref), lying(place_ref, down_ref)
    active = place_ref[0] == section

    @pl.when(active)
    def _():
        for k in range(QUARTERS):
            grad_ref[:, quarter(place_ref, k, width)] = piece_refs[k][...]

    @pl.when(jnp.logical_not(active))
    def _():
        grad_ref[...] = grad_in[...]
        preact_grad_ref[...] = preact_grad_in[...]
        gain_ref[...] = gain_in[...]

    norm_scale = scale_ref[:, :1]
    hidden_ref[...] = gelu_value(preact_ref[...]).astype(jnp.bfloat16)

    def add_grad(k):
        @pl.when(active)
        def _():
            part = across_hidden(down(k), piece_refs[k][...])
            hidden_grad_ref[...] = part if k == 0 else hidden_grad_ref[...] + part

    def finish_grad():
        @pl.when(active)
        def _():
            hidden_grad = hidden_grad_ref[...].T * INV_HIDDEN
            preact_grad_ref[...] = (hidden_grad * gelu_slope(preact_ref[...])).astype(jnp.bfloat16)

    def add_gain(k):
        @pl.when(active)
        def _():
            part = plain_product(preact_grad_ref[...], up(k)) * INV_WIDTH
            rows = rows_ref[:, quarter(place_ref, k, width)]
            normed = rows.astype(jnp.float32) * norm_scale
            gain_ref[place_ref[1] ^ k] = jnp.sum(part * normed, axis=0, keepdims=True)

    def scale_rows():
        normed = rows_ref[...].astype(jnp.float32) * norm_scale
        scaled_ref[...] = (normed * gain_row_ref[...]).astype(jnp.bfloat16)

    beside = [functools.partial(add_grad, k) for k in range(QUARTERS)]
    beside += [finish_grad] + [functools.partial(add_gain, k) for k in range(QUARTERS)]
    beside += [scale_rows]
    blocks = hidden_blocks(target.shape[0])
    outer_blocks(hidden_ref, grad_ref, INV_HIDDEN, blocks, target, buffer_ref, sems, beside)


def final_up(blocks, preact_grad_ref, scaled_ref, *refs):
    target, buffer_ref, sems = refs[-3:]
    outer_blocks(preact_grad_ref, scaled_ref, INV_WIDTH, blocks, target, buffer_ref, sems, [])


def struct(*shape, dtype=jnp.bfloat16):
    return jax.ShapeDtypeStruct(shape, dtype)


def call(kernel, inputs, specs, outputs, out_specs, scratch, aliases, limit, products):
    flops = sum(2 * a * b * c for a, b, c in products)
    return pl.pallas_call(
        kernel,
        out_shape=outputs,
        in_specs=specs,
        out_specs=out_specs,
        scratch_shapes=scratch,
        input_output_aliases=aliases,
        cost_estimate=pl.CostEstimate(
            flops=flops,
            bytes_accessed=sum(2 * b * c for _, b, c in products),
            transcendentals=0,
        ),
        compiler_params=pltpu.CompilerParams(vmem_limit_bytes=limit),
    )(*inputs)


def touch(place_ref, after_ref, up_ref, down_ref, place_out):
    del after_ref, up_ref, down_ref
    for i in range(place_ref.shape[0]):
        place_out[i] = place_ref[i]


def run_touch(place, after, up, down):
    return pl.pallas_call(
        touch,
        out_shape=jax.ShapeDtypeStruct(place.shape, place.dtype),
        in_specs=[SMEM, ANY, VMEM, VMEM],
        out_specs=SMEM,
        compiler_params=pltpu.CompilerParams(vmem_limit_bytes=KERNEL_BYTES),
    )(place, after, up, down)


def lay_rows(place_ref, held_ref, gain_ref, rows_ref, own_ref, own_gain_ref):
    count, micro, tokens, width = held_ref.shape
    inner = count // QUARTERS
    for outer in range(QUARTERS):
        for i in range(inner):
            block = (place_ref[2] ^ i) * QUARTERS + (place_ref[1] ^ outer)
            for j in range(micro):
                start = ((outer * inner + i) * micro + j) * tokens
                rows_ref[start : start + tokens, :] = held_ref[block, j]
    own = quarter(place_ref, 0, width // QUARTERS)
    own_ref[...] = rows_ref[:, own]
    own_gain_ref[...] = jnp.broadcast_to(gain_ref[:, own], own_gain_ref.shape)


def run_lay_rows(place, held, gain):
    rows, width = held.size // gain.size, gain.shape[1]
    return call(
        lay_rows,
        [place, held, gain],
        [SMEM, VMEM, VMEM],
        [
            struct(rows, width),
            struct(rows, width // QUARTERS),
            struct(rows, width // QUARTERS, dtype=jnp.float32),
        ],
        [VMEM] * 3,
        [],
        {},
        KERNEL_BYTES,
        [],
    )


def weight_specs(streams):
    return [ANY if streams else VMEM]


def weight_buffers(weight, quarters):
    shape = (weight.shape[0], weight.shape[1] // QUARTERS)
    return [pltpu.VMEM((count, *shape), weight.dtype) for count in quarters] + [
        pltpu.SemaphoreType.DMA((count,)) for count in quarters
    ]


def run_forward_far(section, place, pieces, gain, up, down, stash, streams):
    rows, (local, width) = pieces[0].shape[0], up.shape
    part = struct(rows, width // QUARTERS)
    first = 4 + len(pieces)
    result = call(
        functools.partial(forward_far, section, len(pieces), bool(stash), streams),
        [place, *pieces, gain, up, down, *stash],
        [SMEM] + [VMEM] * (len(pieces) + 1) + weight_specs(streams) * 2 + [ANY] * len(stash),
        [
            *[part] * len(FAR),
            struct(rows, local),
            struct(rows, width),
            struct(rows, LANES, dtype=jnp.float32),
            struct(rows, local, dtype=jnp.float32),
            struct(rows, width // QUARTERS, dtype=jnp.float32),
        ],
        [VMEM] * 4 + [ANY] * 4,
        [
            pltpu.VMEM((rows, LANES), jnp.float32),
            pltpu.VMEM((rows, local), jnp.float32),
            pltpu.VMEM((rows, width // QUARTERS), jnp.float32),
            pltpu.SemaphoreType.DMA((QUARTERS + 3,)),
            *(weight_buffers(up, [QUARTERS, len(FAR)]) if streams else []),
        ],
        {first + i: 4 + i for i in range(len(stash))},
        STREAM_BYTES if streams else KERNEL_BYTES,
        [(rows, width, local), (rows, local, 3 * width // 4)],
    )
    return (result[:3], result[3], result[4:])


def run_forward_near(section, place, hidden, down, streams):
    rows, (local, width) = hidden.shape[0], down.shape
    part = struct(rows, width // QUARTERS)
    return call(
        functools.partial(forward_near, section, streams),
        [place, hidden, down],
        [SMEM, VMEM, *weight_specs(streams)],
        [part],
        [VMEM],
        weight_buffers(down, [len(NEAR)]) if streams else [],
        {},
        KERNEL_BYTES,
        [(rows, local, width // 4)],
    )


def run_early_grad(section, place, entered, down):
    rows, (local, width) = entered.shape[0], down.shape
    return call(
        functools.partial(early_grad, section),
        [place, entered, down],
        [SMEM, VMEM, VMEM],
        [struct(rows, width), struct(rows, local, dtype=jnp.float32)],
        [ANY] * 2,
        [pltpu.VMEM((rows, local), jnp.float32), pltpu.SemaphoreType.DMA((2,))],
        {},
        KERNEL_BYTES,
        [(rows, width, local)],
    )


def run_last_far(section, place, pieces, hidden_grad, gain, up, stash):
    rows, (local, width) = pieces[0].shape[0], up.shape
    part = struct(rows, width // QUARTERS + LANES)
    result = call(
        functools.partial(last_far, section),
        [place, *pieces, hidden_grad, gain, up, *stash],
        [SMEM] + [VMEM] * (QUARTERS + 3) + [ANY] * 4,
        [
            *[part] * len(FAR),
            struct(rows, local),
            struct(rows, LANES),
            struct(rows, width),
            struct(rows, LANES, dtype=jnp.float32),
            struct(rows, local, dtype=jnp.float32),
            struct(rows, width // QUARTERS, dtype=jnp.float32),
            struct(rows, local),
            struct(QUARTERS, 1, width // QUARTERS, dtype=jnp.float32),
        ],
        [VMEM] * 5 + [ANY] * 6,
        [
            pltpu.VMEM((rows, LANES), jnp.float32),
            pltpu.VMEM((rows, local), jnp.float32),
            pltpu.VMEM((rows, width // QUARTERS), jnp.float32),
            pltpu.VMEM((len(FAR), 1, width // QUARTERS), jnp.float32),
            pltpu.SemaphoreType.DMA((QUARTERS + 7,)),
        ],
        {QUARTERS + 4 + i: 5 + i for i in range(4)},
        KERNEL_BYTES,
        [(rows, width, local), (rows, local, 3 * width // 4)],
    )
    return (result[:3], result[3:5], result[5:9], result[9:])


def run_backward_far(section, place, pieces, kept, up, down, grads):
    rows, (local, width) = pieces[0].shape[0], up.shape
    part = struct(rows, width // QUARTERS + LANES)
    result = call(
        functools.partial(backward_far, section),
        [place, *pieces, *kept, up, down, *grads],
        [SMEM] + [VMEM] * (QUARTERS + 5) + [ANY] * 3,
        [
            *[part] * len(FAR),
            struct(rows, local),
            struct(rows, LANES),
            struct(rows, width),
            struct(rows, local),
            struct(QUARTERS, 1, width // QUARTERS, dtype=jnp.float32),
        ],
        [VMEM] * 5 + [ANY] * 3,
        [
            pltpu.VMEM((len(FAR), 1, width // QUARTERS), jnp.float32),
            pltpu.SemaphoreType.DMA((QUARTERS + 4,)),
        ],
        {QUARTERS + 6 + i: 5 + i for i in range(3)},
        KERNEL_BYTES,
        [(rows, width, local), (rows, local, 3 * width // 4)],
    )
    return (result[:3], result[3:5], result[5:])


def run_backward_near(section, place, passed, kept, up, gain_part):
    rows, (local, width) = kept[0].shape[0], up.shape
    part = struct(rows, width // QUARTERS + LANES)
    result = call(
        functools.partial(backward_near, section),
        [place, *passed, kept[0], kept[1], up, gain_part],
        [SMEM] + [VMEM] * 5 + [ANY],
        [part, struct(*gain_part.shape, dtype=jnp.float32)],
        [VMEM, ANY],
        [
            pltpu.VMEM((len(NEAR), 1, width // QUARTERS), jnp.float32),
            pltpu.SemaphoreType.DMA((len(NEAR),)),
        ],
        {6: 1},
        KERNEL_BYTES,
        [(rows, local, width // 4)],
    )
    return result


def run_final(section, place, pieces, grads, kept, gain, up, down):
    rows, (local, width) = pieces[0].shape[0], up.shape
    buffers = [
        pltpu.VMEM((SLOTS, BLOCK, width), jnp.float32),
        pltpu.SemaphoreType.DMA((SLOTS,)),
    ]
    grad_down, preact_grad, gain_part, scaled = call(
        functools.partial(final_down, section),
        [place, *pieces, *grads, *kept, gain, up, down],
        [SMEM] + [VMEM] * (QUARTERS + 9),
        [
            struct(local, width, dtype=jnp.float32),
            struct(rows, local),
            struct(*grads[2].shape, dtype=jnp.float32),
            struct(rows, width),
        ],
        [ANY] + [VMEM] * 3,
        [
            pltpu.VMEM((rows, width), jnp.bfloat16),
            pltpu.VMEM((rows, local), jnp.bfloat16),
            pltpu.VMEM((local, rows), jnp.float32),
            *buffers,
        ],
        {},
        KERNEL_BYTES,
        [(rows, width, local)] * 2 + [(local, rows, width)],
    )
    blocks = hidden_blocks(local)
    taken = 0
    grad_up, total = (), gain_part.reshape(1, width)
    flips = [1 << i for i in range(lax.axis_size("dp").bit_length() - 1)]
    for i, flip in enumerate(flips):
        other = lax.ppermute(
            total, "dp", [(r, r ^ flip) for r in range(lax.axis_size("dp"))]
        )
        until = -(-len(blocks) * (i + 1) // len(flips))
        if until > taken:
            grad_up = call(
                functools.partial(final_up, blocks[taken:until]),
                [preact_grad, scaled, *grad_up],
                [VMEM, VMEM] + [ANY] * len(grad_up),
                [struct(local, width, dtype=jnp.float32)],
                [ANY],
                buffers,
                {2: 0} if grad_up else {},
                KERNEL_BYTES,
                [(local * (until - taken) // len(blocks), rows, width)],
            )
            taken = until
            if until < len(blocks):
                other, *grad_up = lax.optimization_barrier((other, *grad_up))
        total = total + other
    return (grad_up[0], grad_down, total)


def within(sections, flip):
    count = lax.axis_size("dp")
    return [(s * count + r, s * count + (r ^ flip)) for s in sections for r in range(count)]


def between(moves, flip):
    count = lax.axis_size("dp")
    return [(s * count + r, t * count + (r ^ flip)) for s, t in moves for r in range(count)]


def send_quarter(part, sections, k):
    return lax.ppermute(part, AXES, within(sections, k * (lax.axis_size("dp") // QUARTERS)))


def sum_quarters(own, arrived, sections):
    inner = lax.axis_size("dp") // QUARTERS
    total = own.astype(jnp.float32)
    for value in arrived:
        total = total + value.astype(jnp.float32)
    flip = 1
    while flip < inner:
        rounded = total.astype(jnp.bfloat16)
        other = lax.ppermute(rounded, AXES, within(sections, flip))
        total = rounded.astype(jnp.float32) + other.astype(jnp.float32)
        flip *= 2
    return total


def hand_on(own, moves):
    inner = lax.axis_size("dp") // QUARTERS
    pieces = {
        k: lax.ppermute(own, AXES, between(moves, k * inner)) for k in (3, 2, 0, 1)
    }
    return [pieces[k] for k in range(QUARTERS)]


def gather_chunks(chunk, sections):
    inner = lax.axis_size("dp") // QUARTERS
    pieces = {k: send_quarter(chunk, sections, k) for k in range(QUARTERS - 1, 0, -1)}
    held = along = jnp.concatenate([chunk] + [pieces[k] for k in range(1, QUARTERS)], axis=0)
    flip = 1
    while flip < inner:
        other = lax.ppermute(held, AXES, within(sections, flip))
        held = jnp.concatenate([held, other], axis=0)
        flip *= 2
    return (held, along)


def body(section_input, out_cotangent, up_weight, down_weight, norm_gain):
    section_count = lax.axis_size("section")
    section_pos = lax.axis_index("section")
    count = lax.axis_size("dp")
    position = lax.axis_index("dp")
    width = up_weight.shape[1]
    quarter_width = width // QUARTERS
    last = section_count - 1

    def alike(section):
        return [s for s in range(section_count) if s % 2 == section % 2]

    def moves(section, step):
        return [(s, s + step) for s in alike(section) if 0 <= s + step < section_count]

    inner = count // QUARTERS
    place = jnp.stack([section_pos, position // inner, position % inner]).astype(jnp.int32)
    chunk = jnp.where(section_pos == last, out_cotangent, section_input)
    chunk, place = lax.optimization_barrier((chunk[None], place))
    held, along = gather_chunks(chunk, [0, last])
    streamed_up, streamed_down = (
        pltpu.with_memory_space_constraint(weight[0].T, pltpu.HBM)
        for weight in (up_weight, down_weight)
    )
    up, down = (
        pltpu.with_memory_space_constraint(weight[0].T, pltpu.VMEM)
        for weight in (up_weight, down_weight)
    )
    place = run_touch(place, along, up, down)
    entered, own_entered, own_gain = run_lay_rows(place, held, norm_gain)

    pieces, stash, own = [entered], (), own_entered
    for section in range(last):
        here = alike(section)
        streams = section == 0
        weights = (streamed_up, streamed_down) if streams else (up, down)
        far, hidden, stash = run_forward_far(
            section, place, pieces, norm_gain, *weights, stash, streams
        )
        arrived = [send_quarter(part, here, k) for part, k in zip(far, FAR)]
        (near,) = run_forward_near(section, place, hidden, weights[1], streams)
        result = own.astype(jnp.float32) + sum_quarters(near, arrived, here)
        result = result.astype(jnp.bfloat16)
        pieces = hand_on(result, moves(section, 1))
        own = pieces[0]
        if section == 0:
            for _ in range(TOUCHES):
                place = run_touch(place, result, up, down)
            grad_rows, early = run_early_grad(last, place, entered, down)

    for section in range(last, 0, -1):
        here = alike(section)
        if section == last:
            far, passed, stash, grads = run_last_far(
                last, place, pieces, early, norm_gain, up, stash
            )
            *stash, own_normed = stash
            own_scale = stash[1][:, :1]
            grads = [grad_rows, *grads]
            own = own_entered
        else:
            far, passed, grads = run_backward_far(section, place, pieces, stash, up, down, grads)
            own = pieces[0]
        arrived = [send_quarter(part, here, k) for part, k in zip(far, FAR)]
        near, gain_part = run_backward_near(section, place, passed, stash, up, grads[2])
        grads = [grads[0], grads[1], gain_part]
        total = sum_quarters(near, arrived, here)
        along = total[:, quarter_width : quarter_width + 1] * (1.0 / width)
        normed_grad = total[:, :quarter_width] * own_gain
        result = own.astype(jnp.float32) + own_scale * (normed_grad - own_normed * along)
        pieces = hand_on(result.astype(jnp.bfloat16), moves(section, -1))

    grad_up, grad_down, grad_gain = run_final(
        0, place, pieces, grads, stash, norm_gain, up, down
    )
    return (grad_up.T[None], grad_down.T[None], grad_gain)


def solution(mesh):
    placed = (
        P(None, "dp", None),
        P(None, "dp", None),
        P("section", None, "dp"),
        P("section", None, "dp"),
        P("section", None),
    )
    return jax.shard_map(
        body,
        mesh=mesh,
        in_specs=placed,
        out_specs=(P("section", None, "dp"), P("section", None, "dp"), P("section", None)),
        check_vma=False,
    )
```
